256 devices in a mesh: rep: 64 (over z, x, core), tp: 4 (over y).
Axes of the slice: x: 4, y: 4, z: 8, core: 2. Of those that a mesh axis runs over, the one named last changes fastest.
Arguments:
- normed_input_rows: bfloat16 [65536, 8192], P('rep', 'tp'), may hold values from -6 to 6
- key_projection_weight: bfloat16 [8192, 512], P('tp'), may hold values from -0.0625 to 0.0625
- value_projection_weight: bfloat16 [8192, 512], P('tp'), may hold values from -0.0625 to 0.0625
- adapter_down_factors: bfloat16 [256, 8192, 64], P('rep', 'tp'), may hold values from -0.0625 to 0.0625
- adapter_up_factors: bfloat16 [256, 64, 2, 512], P('rep', None, None, 'tp'), may hold values from -0.75 to 0.75
- request_owner_replica: int32 [4096, 1], P('rep'), may hold values from 0 to 63; in each aligned block of 64 rows (0 to 63, 64 to 127, ...) at most 2 rows name the same one
- request_adapter_slot: int32 [4096], P('rep'), may hold values from 0 to 3
- prefill_adapter_slot: int32 [64], P('rep'), may hold values from 0 to 3
- prefill_first_row: int32 [64], P('rep'), may hold values from 0 to 4095
- context_length: int32 [4096], P('rep'), may hold values from 2 to 64, as said below
- request_page_table: int32 [4096, 4], P('rep'), may hold values from 0 to 255, as said below
- queries: bfloat16 [4096, 4096], P('rep', 'tp'), may hold values from -48 to 48
- rotated_cache_keys: bfloat16 [16384, 16, 512], P('rep', None, 'tp'), may hold values from -16 to 16
- paged_cache_values: bfloat16 [16384, 16, 512], P('rep', None, 'tp'), may hold values from -6 to 6
Outputs:
- decode_kv: bfloat16 [4096, 2, 512], P('rep', None, 'tp')
- prefill_kv: bfloat16 [61440, 2, 512], P('rep', None, 'tp')
- attended: bfloat16 [4096, 4096], P('rep', 'tp')
The draws below stay inside these ranges and needn't reach their ends.
Inputs may be any that keep to these rules, and one draw needn't show every extreme that they name: `request_owner_replica`: among the 64 decode requests of one replica at most 2 have adapters held by one owner, and some owner holds exactly 2 of them. `context_length`: every replica has a decode request with exactly 64 cached positions. `request_page_table`: pages may be shared between requests.
All inputs are finite; a program needn't handle non-finite values.
Results may differ from the reference program's by a relative error of at most 0.0075.
Values may be sent and summed in bfloat16 or wider, within the bound.
A program may use at most 128 MiB of HBM per device.

```python
import math
import jax
import jax.numpy as jnp
import numpy as np
from jax import lax

MODEL_WIDTH = 8192
HEAD_WIDTH = 128
KEY_VALUE_HEADS = 4
GROUP = 8
ADAPTER_RANK = 64
PAGE = 16
MAXP = 4
DEC_DEV = 64
PRE_DEV = 960
ADAPT_DEV = 4
PAGES_DEV = 256
MOST = 64
ROW_DEV = 1024
ROWS = 65536
DECODES = 4096
PREFILLS = 61440
POOL = 16384
ADAPTER_COUNT = 256
CAP = 2
N_REP = 64


def shared_tables(key):
    tables = jax.random.randint(jax.random.fold_in(key, 101), (DECODES, MAXP), 0, PAGES_DEV)
    base_keys = jnp.clip(jax.random.normal(jax.random.fold_in(key, 102), (POOL, PAGE, KEY_VALUE_HEADS * HEAD_WIDTH), jnp.float32), -6.0, 6.0)
    return (tables, base_keys)


def draw_request_page_table(key, part):
    tables, base_keys = shared_tables(key)
    return tables.astype(jnp.int32)


def draw_rotated_cache_keys(key, part):
    tables, base_keys = shared_tables(key)
    result = base_keys
    return result.astype(jnp.bfloat16)


def draw_queries(key, part):
    key = jax.random.fold_in(key, 3)
    key_one = jax.random.fold_in(key, 0)
    drawn_draw = jnp.clip(jax.random.normal(key_one, (DECODES, KEY_VALUE_HEADS * GROUP * HEAD_WIDTH), jnp.float32), -6.0, 6.0)
    result = drawn_draw
    return result.astype(jnp.bfloat16)


def draw_context_length(key, part):
    key = jax.random.fold_in(key, 4)
    key_one, key_two = jax.random.split(key)
    groups = DECODES // DEC_DEV
    lengths = jax.random.randint(key_one, (groups, DEC_DEV), 2, MOST + 1)
    longest = jax.random.randint(key_two, (groups, 1), 0, DEC_DEV)
    lengths = jnp.where(jnp.arange(DEC_DEV)[None, :] == longest, MOST, lengths)
    return lengths.reshape(DECODES).astype(jnp.int32)


def place_ends(values, stream_key, smallest, top_value):
    dims = values.shape
    spot = [jax.random.randint(jax.random.fold_in(stream_key, axis), (), 0, dims[axis]) for axis in range(len(dims))]
    values = values.at[tuple(spot)].set(smallest)
    longest = dims.index(max(dims))
    spot[longest] = (spot[longest] + 1) % dims[longest]
    return values.at[tuple(spot)].set(top_value)


def level_of(stream_key, dims, cuts, smallest, high):
    loudness = 1.0
    for axis_at, blocks in cuts:
        heights = jax.random.uniform(jax.random.fold_in(jax.random.fold_in(stream_key, 6), axis_at), (blocks,), jnp.float32, smallest / len(cuts), high / len(cuts))
        loudness = loudness * jnp.repeat(jnp.exp(heights), dims[axis_at] // blocks).reshape((-1,) + (1,) * (len(dims) - 1 - axis_at))
    return loudness


def routed_block(key, own, number, rows, number_of, top, limit, lean):
    order = jax.random.permutation(key, number_of)
    heavy_load, ordinary = portions_of(number_of, rows * top, limit, lean, True), portions_of(number_of, rows * top, limit, lean, False)
    places = jnp.arange(number_of)

    def named(sizes, offset_by):
        used = int((sizes > 0).sum())
        fixed = max(1, used // 4)
        passed = fixed + (places - fixed + offset_by * (used - fixed)) % max(1, number_of - fixed)
        return jnp.zeros((number_of,), jnp.int32).at[order[jnp.where(places < fixed, places, passed)]].set(jnp.asarray(sizes, jnp.int32))

    sizes = jnp.where(number % 4 == 0, named(heavy_load, number // 4), named(ordinary, number - number // 4 - 1))
    mixed = jax.random.permutation(jax.random.fold_in(own, 3), number_of)
    source_of, receiver = mixed[0:number_of // 2 * 2:2], mixed[1:number_of // 2 * 2:2]
    room = jnp.minimum(sizes[source_of] - 1, limit - sizes[receiver]) // 2
    room = jnp.where((source_of == order[0]) | (receiver == order[0]) | (sizes[receiver] == 0), 0, jnp.maximum(room, 0))
    passed = jax.random.randint(jax.random.fold_in(own, 4), (number_of // 2,), 0, 1 << 20) % (room + 1)
    sizes = sizes.at[source_of].add(-passed).at[receiver].add(passed)
    labels = jnp.searchsorted(jnp.cumsum(sizes), jnp.arange(rows * top), side="right").astype(jnp.int32)
    table = labels.reshape(top, rows).T
    table = table[jax.random.permutation(jax.random.fold_in(own, 1), rows)]
    offset_by = jax.random.randint(jax.random.fold_in(own, 2), (rows, 1), 0, top)
    return jnp.take_along_axis(table, (jnp.arange(top)[None, :] + offset_by) % top, axis=1)


def portions_of(count, total, limit, slope, full):
    portions = [(1 << 20) // math.isqrt(rank ** slope) + 1 for rank in range(1, count + 1)]
    largest = limit if full else min(limit, max(-(-total // count), total * portions[0] // sum(portions)))
    least = 1 if total - largest >= count - 1 else 0
    holding, spare = [largest] + [least] * (count - 1), total - largest - least * (count - 1)
    while spare > 0:
        free = [i for i in range(1, count) if holding[i] < largest] or [i for i in range(1, count) if holding[i] < limit]
        pool, remaining = sum([portions[i] for i in free]), spare
        for i in free:
            extra = min(limit - holding[i], max(1, remaining * portions[i] // pool), spare)
            holding[i] = holding[i] + extra
            spare = spare - extra
    return np.array(holding)


def scatter_about(rng, shape, deviation, reach, cuts=(), kind=jnp.bfloat16):
    array = deviation * jax.random.normal(rng, shape, jnp.float32)
    if cuts:
        array = array * level_of(rng, shape, cuts, -0.22, 0.18)
    return jnp.clip(array, -reach, reach).astype(kind)


def setup_inputs(seed: int = 0) -> dict:
    arg_keys = jax.random.split(jax.random.key(seed), 15)
    normed_input_rows = scatter_about(arg_keys[0], (ROWS, MODEL_WIDTH), 1.0, 6.0, ((0, 64), (1, 4)))
    key_projection_weight = scatter_about(arg_keys[1], (MODEL_WIDTH, KEY_VALUE_HEADS * HEAD_WIDTH), MODEL_WIDTH ** -0.5, 0.0625, ((0, 4),))
    value_projection_weight = scatter_about(arg_keys[2], (MODEL_WIDTH, KEY_VALUE_HEADS * HEAD_WIDTH), MODEL_WIDTH ** -0.5, 0.0625, ((0, 4),))
    adapter_down_factors = scatter_about(arg_keys[3], (ADAPTER_COUNT, MODEL_WIDTH, ADAPTER_RANK), MODEL_WIDTH ** -0.5, 0.0625, ((0, 64), (1, 4)))
    adapter_up_factors = scatter_about(arg_keys[4], (ADAPTER_COUNT, ADAPTER_RANK, 2, KEY_VALUE_HEADS * HEAD_WIDTH), ADAPTER_RANK ** -0.5, 0.75, ((0, 64), (3, 4)))
    request_owner_replica_keys = jax.random.split(jax.random.fold_in(arg_keys[5], 1), DECODES // DEC_DEV)
    request_owner_replica_turns = jax.random.permutation(jax.random.fold_in(arg_keys[5], 3), DECODES // DEC_DEV)
    request_owner_replica = jax.vmap(lambda own, number: routed_block(jax.random.fold_in(arg_keys[5], 2), own, number, DEC_DEV, N_REP, 1, CAP, 2))(request_owner_replica_keys, request_owner_replica_turns).reshape((DECODES, 1))
    request_adapter_slot = place_ends(jax.random.randint(arg_keys[6], (DECODES,), 0, ADAPT_DEV), jax.random.fold_in(arg_keys[6], 1), 0, ADAPT_DEV - 1).astype(jnp.int32)
    prefill_adapter_slot = place_ends(jax.random.randint(arg_keys[7], (N_REP,), 0, ADAPT_DEV), jax.random.fold_in(arg_keys[7], 1), 0, ADAPT_DEV - 1).astype(jnp.int32)
    prefill_first_row = place_ends(jax.random.randint(arg_keys[8], (N_REP,), 0, 4096), jax.random.fold_in(arg_keys[8], 1), 0, 4095).astype(jnp.int32)
    context_length = draw_context_length(jax.random.fold_in(arg_keys[14], 71), 0)
    request_page_table = draw_request_page_table(jax.random.fold_in(arg_keys[14], 71), 0)
    queries = draw_queries(jax.random.fold_in(arg_keys[14], 71), 0)
    rotated_cache_keys = draw_rotated_cache_keys(jax.random.fold_in(arg_keys[14], 71), 0)
    paged_cache_values = scatter_about(arg_keys[13], (POOL, PAGE, KEY_VALUE_HEADS * HEAD_WIDTH), 1.0, 6.0, ((0, 64), (2, 4)))
    return dict(normed_input_rows=normed_input_rows, key_projection_weight=key_projection_weight, value_projection_weight=value_projection_weight, adapter_down_factors=adapter_down_factors, adapter_up_factors=adapter_up_factors, request_owner_replica=request_owner_replica, request_adapter_slot=request_adapter_slot, prefill_adapter_slot=prefill_adapter_slot, prefill_first_row=prefill_first_row, context_length=context_length, request_page_table=request_page_table, queries=queries, rotated_cache_keys=rotated_cache_keys, paged_cache_values=paged_cache_values)


rope_base = 500000.0
highest_precision = lax.Precision.HIGHEST


def rotate_heads(values, positions):
    row_count = values.shape[0]
    head_rows = values.reshape(row_count, -1, HEAD_WIDTH)
    half_size = HEAD_WIDTH // 2
    freq_index = jnp.arange(half_size).astype(jnp.float32)
    frequency = rope_base ** (-2.0 * freq_index / HEAD_WIDTH)
    angles = positions.astype(jnp.float32)[:, None] * frequency[None, :]
    cosine = jnp.cos(angles)[:, None, :]
    sine_part = jnp.sin(angles)[:, None, :]
    first_half = head_rows[..., :half_size]
    second_half = head_rows[..., half_size:]
    turned = jnp.concatenate([first_half * cosine - second_half * sine_part, second_half * cosine + first_half * sine_part], axis=-1)
    return turned.reshape(row_count, -1)


def attend(queries, new_keys, new_values, cached_keys, cached_values, lengths):
    requests, span_len, columns = cached_keys.shape
    kv_heads = columns // HEAD_WIDTH
    query_heads = queries.astype(jnp.float32).reshape(requests, kv_heads, -1, HEAD_WIDTH)
    key_heads = cached_keys.astype(jnp.float32).reshape(requests, span_len, kv_heads, HEAD_WIDTH)
    value_heads = cached_values.astype(jnp.float32).reshape(requests, span_len, kv_heads, HEAD_WIDTH)
    own_key = new_keys.astype(jnp.float32).reshape(requests, kv_heads, HEAD_WIDTH)
    own_value = new_values.astype(jnp.float32).reshape(requests, kv_heads, HEAD_WIDTH)
    scaling = HEAD_WIDTH ** -0.5
    scores = jnp.einsum("nhgd,nthd->nhgt", query_heads, key_heads, precision=highest_precision) * scaling
    own_score = jnp.einsum("nhgd,nhd->nhg", query_heads, own_key, precision=highest_precision) * scaling
    live_mask = jnp.arange(span_len)[None, :] < lengths[:, None]
    scores = jnp.where(live_mask[:, None, None, :], scores, -1e30)
    row_top = jnp.maximum(jnp.max(scores, axis=-1), own_score)
    weights = jnp.exp(scores - row_top[..., None])
    own_weight = jnp.exp(own_score - row_top)
    totals = jnp.sum(weights, axis=-1) + own_weight
    shares = (weights / totals[..., None]).astype(jnp.bfloat16)
    own_share = (own_weight / totals).astype(jnp.bfloat16)
    blended = jnp.einsum("nhgt,nthd->nhgd", shares.astype(jnp.float32), value_heads, precision=highest_precision)
    blended = blended + own_share.astype(jnp.float32)[..., None] * own_value[:, :, None, :]
    return blended.astype(jnp.bfloat16).reshape(requests, -1)


def reference(normed_input_rows, key_projection_weight, value_projection_weight, adapter_down_factors, adapter_up_factors, request_owner_replica, request_adapter_slot, prefill_adapter_slot, prefill_first_row, context_length, request_page_table, queries, rotated_cache_keys, paged_cache_values):
    owner_ids = request_owner_replica[:, 0]

    def one_replica(replica):
        rows_here = lax.dynamic_slice_in_dim(normed_input_rows, replica * ROW_DEV, ROW_DEV, 0)
        first_request = replica * DEC_DEV
        owners_here = lax.dynamic_slice_in_dim(owner_ids, first_request, DEC_DEV, 0)
        slots_here = lax.dynamic_slice_in_dim(request_adapter_slot, first_request, DEC_DEV, 0)
        lengths = lax.dynamic_slice_in_dim(context_length, first_request, DEC_DEV, 0)
        tables = lax.dynamic_slice_in_dim(request_page_table, first_request, DEC_DEV, 0)
        query_rows = lax.dynamic_slice_in_dim(queries, first_request, DEC_DEV, 0)
        selected_slot = (owners_here * ADAPT_DEV + slots_here).astype(jnp.int32)
        prefill_selected = (replica * ADAPT_DEV + prefill_adapter_slot[replica]).astype(jnp.int32)
        decode_input_rows = rows_here[:DEC_DEV]
        prefill_input_rows = rows_here[DEC_DEV:]
        reduced_decode = jnp.einsum("eg,egm->em", decode_input_rows.astype(jnp.float32), adapter_down_factors[selected_slot].astype(jnp.float32), precision=highest_precision)
        reduced_prefill = jnp.dot(prefill_input_rows, adapter_down_factors[prefill_selected], preferred_element_type=jnp.float32)
        decode_correction = jnp.einsum("yz,yzga->yga", reduced_decode, adapter_up_factors[selected_slot].astype(jnp.float32), precision=highest_precision)
        prefill_correction = jnp.einsum("qg,gcv->qcv", reduced_prefill, adapter_up_factors[prefill_selected].astype(jnp.float32), precision=highest_precision)
        delta = jnp.concatenate([decode_correction, prefill_correction], axis=0)
        key_full = jnp.dot(rows_here, key_projection_weight, preferred_element_type=jnp.float32) + delta[:, 0]
        value_full = jnp.dot(rows_here, value_projection_weight, preferred_element_type=jnp.float32) + delta[:, 1]
        positions = jnp.concatenate([lengths, prefill_first_row[replica] + jnp.arange(PRE_DEV, dtype=jnp.int32)])
        key_full = rotate_heads(key_full, positions)
        new_keys = key_full.astype(jnp.bfloat16)
        new_values = value_full.astype(jnp.bfloat16)
        packed = jnp.stack([new_keys, new_values], axis=1)
        global_pages = (replica * PAGES_DEV + tables).astype(jnp.int32)
        cached_keys = rotated_cache_keys[global_pages].reshape(DEC_DEV, MOST, -1)
        cached_values = paged_cache_values[global_pages].reshape(DEC_DEV, MOST, -1)
        mixed_rows = attend(query_rows, new_keys[:DEC_DEV], new_values[:DEC_DEV], cached_keys, cached_values, lengths)
        return packed[:DEC_DEV], packed[DEC_DEV:], mixed_rows

    decode_kv, prefill_kv, attended = lax.map(one_replica, jnp.arange(N_REP, dtype=jnp.int32))
    return (decode_kv.reshape(DECODES, 2, -1), prefill_kv.reshape(PREFILLS, 2, -1), attended.reshape(DECODES, -1))
```

```python
import jax
import jax.numpy as jnp
import numpy as np
from jax import lax
from jax.experimental import pallas as pl
from jax.experimental.pallas import tpu as pltpu
from jax.sharding import PartitionSpec as P

HEAD = 128
HALF = HEAD // 2
ROPE_BASE = 500000.0
PLANE = 8
BLOCKS = 4
CHUNKS = 2
GROUP = 16
PIECE = 64
MESH = pl.DeviceIdType.MESH
F32 = jnp.float32
BF16 = jnp.bfloat16


def mm(a, b):
    return lax.dot_general(a, b, (((1,), (0,)), ((), ())), preferred_element_type=F32)


def mt(a, b):
    return lax.dot_general(a, b, (((1,), (1,)), ((), ())), preferred_element_type=F32)


def iota(shape, axis):
    return lax.broadcasted_iota(jnp.int32, shape, axis)


def one_hot(condition):
    return jnp.where(condition, 1.0, 0.0).astype(BF16)


def trig(step, count):
    frequency = ROPE_BASE ** (-2.0 * np.arange(HALF) / HEAD)
    angles = step * np.arange(count)[:, None] * np.tile(frequency, 2)[None, :]
    return np.concatenate([np.cos(angles), np.sin(angles)], axis=1).astype(np.float32)


def kernel(
    x_hbm,
    wk_hbm,
    wv_hbm,
    d_hbm,
    up_ref,
    owner_ref,
    slot_ref,
    pslot_ref,
    pfirst_ref,
    length_ref,
    table_ref,
    q_hbm,
    kpool_hbm,
    vpool_hbm,
    low_ref,
    high_ref,
    dec_out,
    pre_out,
    att_out,
    x,
    w,
    d,
    q,
    kpool,
    vpool,
    kbuf,
    vbuf,
    s1a,
    s1b,
    r1a,
    r1b,
    s2a,
    s2b,
    r2a,
    r2b,
    s3,
    r3,
    s4,
    r4,
    uall,
    ug,
    ysend,
    yrecv,
    sr,
    sd,
    sc,
    rr,
    rd,
    rc,
    lrp,
    own,
    stage,
    dec,
    base,
    lens,
    m_s,
    l_s,
    o_s,
    load_sem,
    z1s,
    z1r,
    p1s,
    p1r,
    us,
    ur,
    ys,
    yr,
    ns,
    nr,
    p2s,
    p2r,
    z2s,
    z2r,
):
    t = lax.axis_index("tp")
    rep = lax.axis_index("rep")
    tps = lax.axis_size("tp")
    planes = lax.axis_size("rep") // PLANE
    z = lax.div(rep, PLANE)
    p = lax.rem(rep, PLANE)
    rows = x.shape[0] // BLOCKS
    decodes = q.shape[0]
    slots = 2 * lax.axis_size("rep")
    width = x.shape[1] // CHUNKS
    s1, r1, s2, r2 = (s1a, s1b), (r1a, r1b), (s2a, s2b), (r2a, r2b)

    barrier = pltpu.get_barrier_semaphore()

    def at(rep_to, tp_to):
        return dict(device_id=(rep_to, tp_to), device_id_type=MESH)

    def z_of(dd):
        return lax.rem(z + dd, planes)

    def p_of(dd):
        return lax.rem(p + dd, PLANE)

    def t_of(dd):
        return lax.rem(t + dd, tps)

    def each(low, high, body):
        lax.fori_loop(low, high, lambda i, c: (body(i), c)[1], 0)

    each(1, planes, lambda k: pl.semaphore_signal(barrier, inc=1, **at(z_of(k) * PLANE + p, t)))
    each(1, PLANE, lambda k: pl.semaphore_signal(barrier, inc=1, **at(z * PLANE + p_of(k), t)))
    each(1, tps, lambda k: pl.semaphore_signal(barrier, inc=1, **at(rep, t_of(k))))

    def load(source, target, k):
        return pltpu.make_async_copy(source, target, load_sem.at[k])

    def x_load(b):
        part = pl.ds(b * rows, rows)
        return load(x_hbm.at[part], x.at[part], b)

    def w_load(j):
        columns = pl.ds(pl.multiple_of(t_of(j) * HEAD, HEAD), HEAD)
        return (
            load(wk_hbm.at[:, columns], w.at[j, :, pl.ds(0, HEAD)], BLOCKS + 2 * j),
            load(wv_hbm.at[:, columns], w.at[j, :, pl.ds(HEAD, HEAD)], BLOCKS + 2 * j + 1),
        )

    k0 = BLOCKS + 2 * 4
    q_load = load(q_hbm, q, k0)
    d_load = load(d_hbm, d, k0 + 1)
    kpool_load = load(kpool_hbm, kpool, k0 + 2)
    vpool_load = load(vpool_hbm, vpool, k0 + 3)
    x_load(0).start()
    d_load.start()
    for c in w_load(2):
        c.start()
    for b in (1, 2, 3):
        x_load(b).start()
    for j in (3, 1, 0):
        for c in w_load(j):
            c.start()
    for c in (q_load, kpool_load, vpool_load):
        c.start()

    eye = iota((decodes, decodes), 0) == iota((decodes, decodes), 1)

    def column(row):
        return jnp.sum(jnp.where(eye, jnp.broadcast_to(row, eye.shape), 0.0), axis=1, keepdims=True)

    owner_row = owner_ref[...].astype(F32)
    owner_col = column(owner_row)
    same = owner_col == owner_row
    before_col = iota(eye.shape, 1) < iota(eye.shape, 0)
    before_row = iota(eye.shape, 0) < iota(eye.shape, 1)
    target_col = 2.0 * owner_col + jnp.sum(
        jnp.where(same & before_col, 1.0, 0.0), axis=1, keepdims=True
    )
    target_row = 2.0 * owner_row + jnp.sum(
        jnp.where(same & before_row, 1.0, 0.0), axis=0, keepdims=True
    )
    placing = one_hot(target_row == iota((slots, decodes), 0).astype(F32))
    placing_back = one_hot(target_col == iota((decodes, slots), 1).astype(F32))
    codes = jnp.broadcast_to(column(slot_ref[...].astype(F32)) + 1.0, (decodes, HEAD)).astype(BF16)
    lens[...] = jnp.broadcast_to(column(length_ref[...].astype(F32)), (decodes, HEAD))

    x_load(0).wait()
    for c in range(CHUNKS):
        placed = mm(placing, x[0:decodes, c * width : (c + 1) * width]).astype(BF16)
        s1[c][:, :, 0:width] = placed.reshape(planes, 16, width)
    s1a[:, :, width : width + HEAD] = mm(placing, codes).astype(BF16).reshape(planes, 16, HEAD)

    pairs = up_ref[...]
    count = pairs.shape[0] // 2
    pick = iota((count, 2 * count), 1) - 2 * iota((count, 2 * count), 0)
    rank = uall.shape[1]
    uall[:, :, 0:HEAD] = mm(one_hot(pick == 0), pairs).astype(BF16).reshape(-1, rank, HEAD)
    uall[:, :, HEAD:] = mm(one_hot(pick == 1), pairs).astype(BF16).reshape(-1, rank, HEAD)
    selected = pslot_ref[0]
    ug[t] = uall[selected]

    def z1_copy(c, k):
        to = z_of(k)
        return pltpu.make_async_remote_copy(
            s1[c].at[to], r1[c].at[z], z1s.at[c, k], z1r.at[c, k], **at(to * PLANE + p, t)
        )

    def p1_copy(c, k):
        to = p_of(k)
        return pltpu.make_async_remote_copy(
            s2[c].at[to], r2[c].at[p], p1s.at[c, k], p1r.at[c, k], **at(z * PLANE + to, t)
        )

    def p2_copy(k):
        to = p_of(k)
        return pltpu.make_async_remote_copy(
            s3.at[to], r3.at[p], p2s.at[k], p2r.at[k], **at(z * PLANE + to, t)
        )

    def z2_copy(k):
        to = z_of(k)
        return pltpu.make_async_remote_copy(
            s4.at[to], r4.at[z], z2s.at[k], z2r.at[k], **at(to * PLANE + p, t)
        )

    def up_copy(k):
        return pltpu.make_async_remote_copy(
            ug.at[t], ug.at[t], us.at[k], ur.at[k], **at(rep, t_of(k))
        )

    def low_copy(k):
        return pltpu.make_async_remote_copy(
            ysend, yrecv.at[k - 1], ns.at[k], nr.at[k], **at(rep, t_of(k))
        )

    def ahead(b):
        return 1 + 2 * lax.div(b, 2)

    def back(b):
        return 3 - 2 * lax.div(b, 2)

    def relay_copy(b):
        return pltpu.make_async_remote_copy(
            sr.at[b], rr.at[b], ys.at[0, b], yr.at[0, b], **at(rep, t_of(ahead(b)))
        )

    def direct_copy(b):
        return pltpu.make_async_remote_copy(
            sd.at[b], rd.at[b], ys.at[1, b], yr.at[1, b], **at(rep, t_of(back(b)))
        )

    def sum_copy(b):
        return pltpu.make_async_remote_copy(
            sc.at[b], rc.at[b], ys.at[2, b], yr.at[2, b], **at(rep, t_of(ahead(b)))
        )

    pl.semaphore_wait(barrier, planes - 1 + PLANE - 1 + tps - 1)
    each(1, tps, lambda k: up_copy(k).start())
    for c in range(CHUNKS):
        each(1, planes, lambda k: z1_copy(c, k).start())
    for c in range(CHUNKS):
        r1[c][z] = s1[c][z]

    first = pfirst_ref[0]
    high = high_ref[pl.ds(lax.div(first, PIECE), 1), :]
    low = low_ref[pl.ds(lax.rem(first, PIECE), 1), :]

    def turn(a, b):
        ca, sa, cb, sb = a[:, 0:HEAD], a[:, HEAD:], b[:, 0:HEAD], b[:, HEAD:]
        return ca * cb - sa * sb, sa * cb + ca * sb

    c0, s0 = turn(high, low)
    steps = high_ref[0:16, :]
    cb, sb = steps[:, 0:HEAD], steps[:, HEAD:]
    base[:, 0:HEAD] = c0 * cb - s0 * sb
    base[:, HEAD:] = s0 * cb + c0 * sb

    swap_out = iota((slots, slots), 0)
    swap_in = iota((slots, slots), 1)
    swap = one_hot(
        swap_in == ((swap_out >> 1) & 7) * 16 + (swap_out >> 4) * 2 + (swap_out & 1)
    )

    d_load.wait()
    for c in w_load(2):
        c.wait()
    each(1, tps, lambda k: up_copy(k).wait_recv())

    def part_of(b, j):
        here = pl.ds(pl.multiple_of(b * rows, rows), rows)
        return mm(x[here, :], w[j]) + mm(lrp[here, :], ug[t_of(j)])

    def relay_step(b):
        here = pl.ds(pl.multiple_of(b * rows, rows), rows)

        @pl.when(b > 0)
        def _():
            x_load(b).wait()

        low_rank = mt(x[here, :], d[selected])
        row = iota(low_rank.shape, 0) + b * rows
        lrp[here, :] = jnp.where(row >= decodes, low_rank, 0.0).astype(BF16)
        sr[b] = part_of(b, 2).astype(BF16)
        relay_copy(b).start()

    def direct_step(b):
        sd[b] = part_of(b, back(b)).astype(BF16)
        direct_copy(b).start()

    def sum_step(b):
        part = part_of(b, ahead(b))
        relay_copy(b).wait_recv()
        sc[b] = (part + rr[b].astype(F32)).astype(BF16)
        sum_copy(b).start()

    def own_step(b):
        own[pl.ds(pl.multiple_of(b * rows, rows), rows), :] = part_of(b, 0)

    def order(i):
        return lax.div(i, 2) + 2 * lax.rem(i, 2)

    each(0, BLOCKS, lambda i: relay_step(order(i)))
    for j in (3, 1):
        for c in w_load(j):
            c.wait()
    each(0, BLOCKS, lambda i: direct_step(order(i)))
    each(0, BLOCKS, lambda i: sum_step(order(i)))

    def forward(c):
        each(1, planes, lambda k: z1_copy(c, k).wait_recv())
        moved = mm(swap, r1[c][...].reshape(slots, -1)).astype(BF16)
        s2[c][...] = moved.reshape(PLANE, 16, -1)
        each(1, PLANE, lambda k: p1_copy(c, k).start())
        r2[c][p] = s2[c][p]

    forward(0)
    for c in w_load(0):
        c.wait()
    each(0, BLOCKS, own_step)

    for c in (q_load, kpool_load, vpool_load):
        c.wait()
    maxp, page = table_ref.shape[0], kpool.shape[1]
    span = maxp * page

    def gather(i):
        for j in range(maxp):
            number = table_ref[j, i]
            here = pl.ds(pl.multiple_of((i * maxp + j) * page, page), page)
            kbuf[here, :] = kpool[number]
            vbuf[here, :] = vpool[number]

    each(0, decodes, gather)
    heads = q.shape[1] // HEAD
    scale = HEAD**-0.5

    def queries_of(i):
        here = pl.ds(pl.multiple_of(i * GROUP, GROUP), GROUP)
        return jnp.concatenate(
            [q[here, g * HEAD : (g + 1) * HEAD] for g in range(heads)], axis=0
        )

    def cached(i):
        here = pl.ds(pl.multiple_of(i * GROUP * span, GROUP * span), GROUP * span)
        scores = mt(queries_of(i), kbuf[here, :]) * scale
        length = lens[pl.ds(pl.multiple_of(i * GROUP, GROUP), GROUP), 0:1]
        length = jnp.concatenate([length] * heads, axis=0)
        begin = (iota(length.shape, 0) & (GROUP - 1)) * span
        end = begin + length.astype(jnp.int32)
        place = iota(scores.shape, 1)
        scores = jnp.where((place >= begin) & (place < end), scores, -1e30)
        top = jnp.max(scores, axis=1, keepdims=True)
        weights = jnp.exp(scores - top)
        o_s[i] = mm(weights.astype(BF16), vbuf[here, :])
        m_s[i] = jnp.broadcast_to(top, (GROUP * heads, HEAD))
        l_s[i] = jnp.broadcast_to(jnp.sum(weights, axis=1, keepdims=True), (GROUP * heads, HEAD))

    each(0, decodes // GROUP, cached)
    forward(1)

    partial = jnp.zeros((slots, d.shape[0] * rank), F32)
    for c in range(CHUNKS):
        each(1, PLANE, lambda k: p1_copy(c, k).wait_recv())
        factors = d[:, :, c * width : (c + 1) * width].reshape(-1, width)
        partial = partial + mt(r2[c][:, :, 0:width].reshape(slots, width), factors)
    code = r2a[:, :, width : width + HEAD].reshape(slots, HEAD).astype(F32)
    lane_slot = (iota((slots, HEAD), 1) >> 6) + 1
    lane_slot = lane_slot.astype(F32)
    low_half = code == lane_slot
    high_half = code == lane_slot + 2.0
    mine = jnp.where(low_half, partial[:, 0:HEAD], 0.0) + jnp.where(
        high_half, partial[:, HEAD:], 0.0
    )
    ysend[...] = mine.astype(BF16)
    each(1, tps, lambda k: low_copy(k).start())

    sign = jnp.where(iota((1, HEAD), 1) < HALF, -1.0, 1.0)

    def rotated(keys, cosine, sine):
        return keys * cosine + pltpu.roll(keys, HALF, 1) * (sine * sign)

    def finish(b):
        here = pl.ds(pl.multiple_of(b * rows, rows), rows)
        direct_copy(b).wait_recv()
        sum_copy(b).wait_recv()
        total = own[here, :] + rd[b].astype(F32) + rc[b].astype(F32)
        own[here, :] = total
        low_c, low_s = low_ref[0:PIECE, 0:HEAD], low_ref[0:PIECE, HEAD:]
        for i in range(rows // PIECE):
            if b == 0 and i == 0:
                continue
            a = b * (rows // PIECE) + i - 1
            ca, sa = base[a : a + 1, 0:HEAD], base[a : a + 1, HEAD:]
            piece = total[i * PIECE : (i + 1) * PIECE]
            keys = rotated(piece[:, 0:HEAD], ca * low_c - sa * low_s, sa * low_c + ca * low_s)
            stage[pl.ds(2 * i * PIECE, PIECE, stride=2), :] = keys
            stage[pl.ds(2 * i * PIECE + 1, PIECE, stride=2), :] = piece[:, HEAD:]
        skip = 2 * PIECE if b == 0 else 0
        begin = 2 * (b * rows - decodes) + skip
        pre_out[begin : begin + 2 * rows - skip, :] = stage[skip:, :].astype(BF16)

    finish(0)
    finish(2)

    each(1, tps, lambda k: low_copy(k).wait_recv())
    whole = mine
    for k in range(3):
        whole = whole + yrecv[k].astype(F32)
    wide = jnp.concatenate(
        [jnp.where(low_half, whole, 0.0), jnp.where(high_half, whole, 0.0)], axis=1
    )
    coarse = wide.astype(BF16)
    fine = (wide - coarse.astype(F32)).astype(BF16)
    factors = uall[...].reshape(-1, 2 * HEAD)
    delta = mm(coarse, factors) + mm(fine, factors)
    s3[...] = delta.astype(BF16).reshape(PLANE, 16, 2 * HEAD)
    each(1, PLANE, lambda k: p2_copy(k).start())
    r3[p] = s3[p]

    finish(1)

    each(1, PLANE, lambda k: p2_copy(k).wait_recv())
    s4[...] = mm(swap, r3[...].reshape(slots, -1)).astype(BF16).reshape(planes, 16, -1)
    each(1, planes, lambda k: z2_copy(k).start())
    r4[z] = s4[z]

    finish(3)

    chosen = lens[:, 0:1] == iota((decodes, low_ref.shape[0]), 1).astype(F32)
    angles = lax.dot_general(
        jnp.where(chosen, 1.0, 0.0),
        low_ref[...],
        (((1,), (0,)), ((), ())),
        precision=lax.Precision.HIGHEST,
        preferred_element_type=F32,
    )
    each(1, planes, lambda k: z2_copy(k).wait_recv())
    both = own[0:decodes, :] + mm(placing_back, r4[...].reshape(slots, -1))
    keys = rotated(both[:, 0:HEAD], angles[:, 0:HEAD], angles[:, HEAD:]).astype(BF16).astype(F32)
    values = both[:, HEAD:].astype(BF16).astype(F32)
    dec[pl.ds(0, decodes, stride=2), :] = keys
    dec[pl.ds(1, decodes, stride=2), :] = values
    dec_out[...] = dec[...].astype(BF16)
    for i in range(decodes // GROUP):
        key = jnp.concatenate([keys[i * GROUP : (i + 1) * GROUP]] * heads, axis=0)
        value = jnp.concatenate([values[i * GROUP : (i + 1) * GROUP]] * heads, axis=0)
        score = jnp.sum(queries_of(i).astype(F32) * key, axis=1, keepdims=True) * scale
        old = m_s[i]
        top = jnp.maximum(old, score)
        shrink = jnp.exp(old - top)
        share = jnp.exp(score - top)
        result = (o_s[i] * shrink + share * value) / (l_s[i] * shrink + share)
        for g in range(heads):
            att_out[i * GROUP : (i + 1) * GROUP, g * HEAD : (g + 1) * HEAD] = result[
                g * GROUP : (g + 1) * GROUP
            ].astype(BF16)

    for c in range(CHUNKS):
        each(1, planes, lambda k: z1_copy(c, k).wait_send())
        each(1, PLANE, lambda k: p1_copy(c, k).wait_send())
    each(1, planes, lambda k: z2_copy(k).wait_send())
    each(1, PLANE, lambda k: p2_copy(k).wait_send())
    each(1, tps, lambda k: up_copy(k).wait_send())
    each(1, tps, lambda k: low_copy(k).wait_send())

    def sent(b):
        relay_copy(b).wait_send()
        direct_copy(b).wait_send()
        sum_copy(b).wait_send()

    each(0, BLOCKS, sent)


def shards(
    normed_input_rows,
    key_projection_weight,
    value_projection_weight,
    adapter_down_factors,
    adapter_up_factors,
    request_owner_replica,
    request_adapter_slot,
    prefill_adapter_slot,
    prefill_first_row,
    context_length,
    request_page_table,
    queries,
    rotated_cache_keys,
    paged_cache_values,
):
    total, width = normed_input_rows.shape
    decodes = request_adapter_slot.shape[0]
    adapters, _, rank = adapter_down_factors.shape
    pages, page, local = rotated_cache_keys.shape
    slots = 2 * lax.axis_size("rep")
    planes = lax.axis_size("rep") // PLANE
    tps = lax.axis_size("tp")
    rows = total // BLOCKS
    part = width // CHUNKS
    prefills = total - decodes
    groups = decodes // GROUP
    heads = queries.shape[1] // HEAD
    span = decodes * request_page_table.shape[1] * page
    vmem = pl.BlockSpec(memory_space=pltpu.VMEM)
    smem = pl.BlockSpec(memory_space=pltpu.SMEM)
    hbm = pl.BlockSpec(memory_space=pl.ANY)
    dma = pltpu.SemaphoreType.DMA

    def bf(*shape):
        return pltpu.VMEM(shape, BF16)

    def fl(*shape):
        return pltpu.VMEM(shape, F32)

    decode_kv, prefill_kv, attended = pl.pallas_call(
        kernel,
        out_shape=(
            jax.ShapeDtypeStruct((2 * decodes, HEAD), BF16),
            jax.ShapeDtypeStruct((2 * prefills, HEAD), BF16),
            jax.ShapeDtypeStruct(queries.shape, BF16),
        ),
        in_specs=[hbm, hbm, hbm, hbm, vmem, vmem, vmem, smem, smem, vmem, smem, hbm, hbm, hbm, vmem, vmem],
        out_specs=(vmem, vmem, vmem),
        scratch_shapes=[
            bf(total, width),
            bf(tps, width, 2 * HEAD),
            bf(adapters, rank, width),
            bf(*queries.shape),
            bf(pages, page, local),
            bf(pages, page, local),
            bf(span, HEAD),
            bf(span, HEAD),
            bf(planes, 16, part + HEAD),
            bf(planes, 16, part),
            bf(planes, 16, part + HEAD),
            bf(planes, 16, part),
            bf(PLANE, 16, part + HEAD),
            bf(PLANE, 16, part),
            bf(PLANE, 16, part + HEAD),
            bf(PLANE, 16, part),
            bf(PLANE, 16, 2 * HEAD),
            bf(PLANE, 16, 2 * HEAD),
            bf(planes, 16, 2 * HEAD),
            bf(planes, 16, 2 * HEAD),
            bf(adapters, rank, 2 * HEAD),
            bf(tps, rank, 2 * HEAD),
            bf(slots, HEAD),
            bf(tps - 1, slots, HEAD),
        ]
        + [bf(BLOCKS, rows, 2 * HEAD)] * 6
        + [
            bf(total, rank),
            fl(total, 2 * HEAD),
            fl(2 * rows, HEAD),
            fl(2 * decodes, HEAD),
            fl(16, 2 * HEAD),
            fl(decodes, HEAD),
            fl(groups, GROUP * heads, HEAD),
            fl(groups, GROUP * heads, HEAD),
            fl(groups, GROUP * heads, HEAD),
            dma((BLOCKS + 2 * 4 + 4,)),
            dma((CHUNKS, planes)),
            dma((CHUNKS, planes)),
            dma((CHUNKS, PLANE)),
            dma((CHUNKS, PLANE)),
            dma((tps,)),
            dma((tps,)),
            dma((3, BLOCKS)),
            dma((3, BLOCKS)),
            dma((tps,)),
            dma((tps,)),
            dma((PLANE,)),
            dma((PLANE,)),
            dma((planes,)),
            dma((planes,)),
        ],
        compiler_params=pltpu.CompilerParams(
            collective_id=0, has_side_effects=True, vmem_limit_bytes=44 * 1024 * 1024
        ),
    )(
        normed_input_rows,
        key_projection_weight,
        value_projection_weight,
        jnp.swapaxes(adapter_down_factors, 1, 2),
        adapter_up_factors.reshape(-1, HEAD),
        request_owner_replica.reshape(1, -1),
        request_adapter_slot.reshape(1, -1),
        prefill_adapter_slot,
        prefill_first_row,
        context_length.reshape(1, -1),
        request_page_table.T,
        queries,
        rotated_cache_keys,
        paged_cache_values,
        jnp.asarray(trig(1, 128)),
        jnp.asarray(trig(PIECE, 64)),
    )
    return (
        decode_kv.reshape(decodes, 2, HEAD),
        prefill_kv.reshape(prefills, 2, HEAD),
        attended,
    )


def solution(mesh):
    in_specs = (
        P("rep", "tp"),
        P("tp", None),
        P("tp", None),
        P("rep", "tp", None),
        P("rep", None, None, "tp"),
        P("rep", None),
        P("rep"),
        P("rep"),
        P("rep"),
        P("rep"),
        P("rep", None),
        P("rep", "tp"),
        P("rep", None, "tp"),
        P("rep", None, "tp"),
    )
    out_specs = (P("rep", None, "tp"), P("rep", None, "tp"), P("rep", "tp"))
    return jax.shard_map(shards, mesh=mesh, in_specs=in_specs, out_specs=out_specs, check_vma=False)
```

```python
import jax
import jax.numpy as jnp
import numpy as np
from jax import lax
from jax.experimental import pallas as pl
from jax.experimental.pallas import tpu as pltpu
from jax.sharding import PartitionSpec as P

HEAD = 128
HALF = HEAD // 2
ROPE_BASE = 500000.0
PLANE = 8
BLOCKS = 4
CHUNKS = 2
GROUP = 16
PIECE = 64
MESH = pl.DeviceIdType.MESH
F32 = jnp.float32
BF16 = jnp.bfloat16


def mm(a, b):
    return lax.dot_general(a, b, (((1,), (0,)), ((), ())), preferred_element_type=F32)


def mt(a, b):
    return lax.dot_general(a, b, (((1,), (1,)), ((), ())), preferred_element_type=F32)


def iota(shape, axis):
    return lax.broadcasted_iota(jnp.int32, shape, axis)


def one_hot(condition):
    return jnp.where(condition, 1.0, 0.0).astype(BF16)


def trig(step, count):
    frequency = ROPE_BASE ** (-2.0 * np.arange(HALF) / HEAD)
    angles = step * np.arange(count)[:, None] * np.tile(frequency, 2)[None, :]
    return np.concatenate([np.cos(angles), np.sin(angles)], axis=1).astype(np.float32)


def kernel(
    x_hbm,
    wk_hbm,
    wv_hbm,
    d_hbm,
    up_hbm,
    owner_hbm,
    slot_hbm,
    pslot_hbm,
    pfirst_hbm,
    length_hbm,
    table_hbm,
    q_hbm,
    kpool_hbm,
    vpool_hbm,
    low_hbm,
    high_hbm,
    dec_out,
    pre_out,
    att_out,
    up_ref,
    owner_ref,
    slot_ref,
    pslot_ref,
    pfirst_ref,
    length_ref,
    table_ref,
    low_ref,
    high_ref,
    x,
    w,
    d,
    q,
    kpool,
    vpool,
    kbuf,
    vbuf,
    s1a,
    s1b,
    r1a,
    r1b,
    s2a,
    s2b,
    r2a,
    r2b,
    s3,
    r3,
    s4,
    r4,
    uall,
    ug,
    ysend,
    yrecv,
    sr,
    sd,
    sc,
    rr,
    rd,
    rc,
    lrp,
    own,
    stage,
    dec,
    base,
    lens,
    m_s,
    l_s,
    o_s,
    load_sem,
    ex_s,
    ex_r,
    us,
    ur,
    ys,
    yr,
    ns,
    nr,
):
    t = lax.axis_index("tp")
    rep = lax.axis_index("rep")
    tps = lax.axis_size("tp")
    planes = lax.axis_size("rep") // PLANE
    z = lax.div(rep, PLANE)
    p = lax.rem(rep, PLANE)
    rows = x.shape[0] // BLOCKS
    decodes = q.shape[0]
    slots = 2 * lax.axis_size("rep")
    width = x.shape[1] // CHUNKS
    s1 = (s1a, s1b)

    barrier = pltpu.get_barrier_semaphore()

    def at(rep_to, tp_to):
        return dict(device_id=(rep_to, tp_to), device_id_type=MESH)

    def z_of(dd):
        return lax.rem(z + dd, planes)

    def p_of(dd):
        return lax.rem(p + dd, PLANE)

    def t_of(dd):
        return lax.rem(t + dd, tps)

    def each(low, high, body):
        lax.fori_loop(low, high, lambda i, c: (body(i), c)[1], 0)

    def far_first(count):
        return sorted(range(1, count), key=lambda k: -min(k, count - k))

    for k in far_first(planes):
        pl.semaphore_signal(barrier, inc=1, **at(z_of(k) * PLANE + p, t))
    for k in far_first(PLANE):
        pl.semaphore_signal(barrier, inc=1, **at(z * PLANE + p_of(k), t))
    for k in far_first(tps):
        pl.semaphore_signal(barrier, inc=1, **at(rep, t_of(k)))

    def load(source, target, k):
        return pltpu.make_async_copy(source, target, load_sem.at[k])

    def x_load(b):
        part = pl.ds(b * rows, rows)
        return load(x_hbm.at[part], x.at[part], b)

    def w_load(j):
        columns = pl.ds(pl.multiple_of(t_of(j) * HEAD, HEAD), HEAD)
        return (
            load(wk_hbm.at[:, columns], w.at[j, :, pl.ds(0, HEAD)], BLOCKS + 2 * j),
            load(wv_hbm.at[:, columns], w.at[j, :, pl.ds(HEAD, HEAD)], BLOCKS + 2 * j + 1),
        )

    k0 = BLOCKS + 2 * 4
    q_load = load(q_hbm, q, k0)
    d_load = load(d_hbm, d, k0 + 1)
    kpool_load = load(kpool_hbm, kpool, k0 + 2)
    vpool_load = load(vpool_hbm, vpool, k0 + 3)
    small = [
        load(source, target, k0 + 4 + i)
        for i, (source, target) in enumerate(
            (
                (owner_hbm, owner_ref),
                (slot_hbm, slot_ref),
                (length_hbm, length_ref),
                (pslot_hbm, pslot_ref),
                (up_hbm, up_ref),
                (pfirst_hbm, pfirst_ref),
                (low_hbm, low_ref),
                (high_hbm, high_ref),
                (table_hbm, table_ref),
            )
        )
    ]
    head_load = load(x_hbm.at[pl.ds(0, decodes)], x.at[pl.ds(0, decodes)], k0 + 4 + len(small))
    for c in small[:3]:
        c.start()
    head_load.start()
    for c in small[3:]:
        c.start()
    rest = pl.ds(decodes, rows - decodes)
    load(x_hbm.at[rest], x.at[rest], 0).start()
    d_load.start()
    for c in w_load(2):
        c.start()
    for b in (1, 2, 3):
        x_load(b).start()
    for j in (3, 1, 0):
        for c in w_load(j):
            c.start()
    for c in (q_load, kpool_load, vpool_load):
        c.start()

    for c in small[:3]:
        c.wait()

    eye = iota((decodes, decodes), 0) == iota((decodes, decodes), 1)

    def column(row):
        return jnp.sum(jnp.where(eye, jnp.broadcast_to(row, eye.shape), 0.0), axis=1, keepdims=True)

    owner_row = owner_ref[...].astype(F32)
    owner_col = column(owner_row)
    same = owner_col == owner_row
    before_col = iota(eye.shape, 1) < iota(eye.shape, 0)
    before_row = iota(eye.shape, 0) < iota(eye.shape, 1)
    rank_col = jnp.sum(jnp.where(same & before_col, 1.0, 0.0), axis=1, keepdims=True)
    rank_row = jnp.sum(jnp.where(same & before_row, 1.0, 0.0), axis=0, keepdims=True)

    def plane_first(owner, turn):
        owner = owner.astype(jnp.int32)
        return (owner & (PLANE - 1)) * 16 + (owner >> 3) * 2 + turn.astype(jnp.int32)

    slot_of = iota((slots, decodes), 0)
    placing = (
        one_hot((2.0 * owner_row + rank_row).astype(jnp.int32) == slot_of),
        one_hot(plane_first(owner_row, rank_row) == slot_of),
    )
    placing_back = one_hot(plane_first(owner_col, rank_col) == iota((decodes, slots), 1))
    codes = jnp.broadcast_to(column(slot_ref[...].astype(F32)) + 1.0, (decodes, HEAD)).astype(BF16)
    lens[...] = jnp.broadcast_to(column(length_ref[...].astype(F32)), (decodes, HEAD))

    head_load.wait()
    for c in range(CHUNKS):
        placed = mm(placing[c], x[0:decodes, c * width : (c + 1) * width]).astype(BF16)
        s1[c][:, :, 0:width] = placed.reshape(planes, 16, width)
    s1a[:, :, width : width + HEAD] = mm(placing[0], codes).astype(BF16).reshape(planes, 16, HEAD)

    for c in small[3:5]:
        c.wait()
    pairs = up_ref[...]
    count = pairs.shape[0] // 2
    pick = iota((count, 2 * count), 1) - 2 * iota((count, 2 * count), 0)
    rank = uall.shape[1]
    uall[:, :, 0:HEAD] = mm(one_hot(pick == 0), pairs).astype(BF16).reshape(-1, rank, HEAD)
    uall[:, :, HEAD:] = mm(one_hot(pick == 1), pairs).astype(BF16).reshape(-1, rank, HEAD)
    selected = pslot_ref[0]
    ug[t] = uall[selected]

    def copy(source, target, send, recv, where):
        return pltpu.make_async_remote_copy(source, target, send, recv, **where)

    class Exchange:
        def __init__(self, sent, got, me, of, place, send, recv):
            self.sent, self.got, self.me, self.send, self.recv = sent, got, me, send, recv
            self.of, self.place = of, place

        def start(self):
            for k in far_first(PLANE):
                to = self.of(k)
                copy(self.sent.at[to], self.got.at[self.me], self.send, self.recv, self.place(to)).start()
            self.got[self.me] = self.sent[self.me]

        def all(self):
            most = pl.ds(0, PLANE - 1)
            return copy(self.sent.at[most], self.got.at[most], self.send, self.recv, self.place(self.of(1)))

    def over_z(sent, got, k):
        return Exchange(sent, got, z, z_of, lambda to: at(to * PLANE + p, t), ex_s.at[k], ex_r.at[k])

    def over_plane(sent, got, k):
        return Exchange(sent, got, p, p_of, lambda to: at(z * PLANE + to, t), ex_s.at[k], ex_r.at[k])

    first_hop = (over_z(s1a, r1a, 0), over_plane(s1b, r1b, 1))
    second_hop = (over_plane(s2a, r2a, 2), over_z(s2b, r2b, 3))
    back_hop = (over_z(s3, r3, 4), over_plane(s4, r4, 5))

    def up_copy(k):
        return pltpu.make_async_remote_copy(
            ug.at[t], ug.at[t], us.at[k], ur.at[k], **at(rep, t_of(k))
        )

    def low_copy(k):
        return pltpu.make_async_remote_copy(
            ysend, yrecv.at[k - 1], ns.at[k], nr.at[k], **at(rep, t_of(k))
        )

    def ahead(b):
        return 1 + 2 * lax.div(b, 2)

    def back(b):
        return 3 - 2 * lax.div(b, 2)

    def relay_copy(b):
        return pltpu.make_async_remote_copy(
            sr.at[b], rr.at[b], ys.at[0, b], yr.at[0, b], **at(rep, t_of(ahead(b)))
        )

    def direct_copy(b):
        return pltpu.make_async_remote_copy(
            sd.at[b], rd.at[b], ys.at[1, b], yr.at[1, b], **at(rep, t_of(back(b)))
        )

    def sum_copy(b):
        return pltpu.make_async_remote_copy(
            sc.at[b], rc.at[b], ys.at[2, b], yr.at[2, b], **at(rep, t_of(ahead(b)))
        )

    pl.semaphore_wait(barrier, planes - 1 + PLANE - 1 + tps - 1)
    first_hop[0].start()
    first_hop[1].start()
    for k in far_first(tps):
        up_copy(k).start()

    for c in small[5:8]:
        c.wait()
    first = pfirst_ref[0]
    high = high_ref[pl.ds(lax.div(first, PIECE), 1), :]
    low = low_ref[pl.ds(lax.rem(first, PIECE), 1), :]

    def turn(a, b):
        ca, sa, cb, sb = a[:, 0:HEAD], a[:, HEAD:], b[:, 0:HEAD], b[:, HEAD:]
        return ca * cb - sa * sb, sa * cb + ca * sb

    c0, s0 = turn(high, low)
    steps = high_ref[0:16, :]
    cb, sb = steps[:, 0:HEAD], steps[:, HEAD:]
    base[:, 0:HEAD] = c0 * cb - s0 * sb
    base[:, HEAD:] = s0 * cb + c0 * sb

    swap_out = iota((slots, slots), 0)
    swap_in = iota((slots, slots), 1)
    swap = one_hot(
        swap_in == ((swap_out >> 1) & 7) * 16 + (swap_out >> 4) * 2 + (swap_out & 1)
    )

    d_load.wait()
    for c in w_load(2):
        c.wait()

    def part_of(b, j):
        here = pl.ds(pl.multiple_of(b * rows, rows), rows)
        return mm(x[here, :], w[j]) + mm(lrp[here, :], ug[t_of(j)])

    def relay_step(b):
        here = pl.ds(pl.multiple_of(b * rows, rows), rows)

        @pl.when(b == 0)
        def _():
            load(x_hbm.at[rest], x.at[rest], 0).wait()

        @pl.when(b > 0)
        def _():
            x_load(b).wait()

        low_rank = mt(x[here, :], d[selected])
        row = iota(low_rank.shape, 0) + b * rows
        lrp[here, :] = jnp.where(row >= decodes, low_rank, 0.0).astype(BF16)
        part = mm(x[here, :], w[2])

        @pl.when(b == 0)
        def _():
            for k in far_first(tps):
                up_copy(k).wait_recv()

        sr[b] = (part + mm(lrp[here, :], ug[t_of(2)])).astype(BF16)
        relay_copy(b).start()

    def direct_step(b):
        sd[b] = part_of(b, back(b)).astype(BF16)
        direct_copy(b).start()

    def sum_step(b):
        part = part_of(b, ahead(b))
        relay_copy(b).wait_recv()
        sc[b] = (part + rr[b].astype(F32)).astype(BF16)
        sum_copy(b).start()

    def own_step(b):
        own[pl.ds(pl.multiple_of(b * rows, rows), rows), :] = part_of(b, 0)

    def order(i):
        return lax.div(i, 2) + 2 * lax.rem(i, 2)

    each(0, BLOCKS, lambda i: relay_step(order(i)))
    for j in (3, 1):
        for c in w_load(j):
            c.wait()
    each(0, BLOCKS, lambda i: direct_step(order(i)))

    def forward(c):
        first_hop[c].all().wait_recv()
        moved = mm(swap, first_hop[c].got[...].reshape(slots, -1)).astype(BF16)
        second_hop[c].sent[...] = moved.reshape(PLANE, 16, -1)
        second_hop[c].start()

    forward(1)
    each(0, BLOCKS, lambda i: sum_step(order(i)))
    forward(0)
    for c in w_load(0):
        c.wait()
    each(0, BLOCKS, own_step)

    for c in (q_load, kpool_load, vpool_load, small[8]):
        c.wait()
    maxp, page = table_ref.shape[0], kpool.shape[1]
    span = maxp * page

    def gather(i):
        for j in range(maxp):
            number = table_ref[j, i]
            here = pl.ds(pl.multiple_of((i * maxp + j) * page, page), page)
            kbuf[here, :] = kpool[number]
            vbuf[here, :] = vpool[number]

    each(0, decodes, gather)
    heads = q.shape[1] // HEAD
    scale = HEAD**-0.5

    def queries_of(i):
        here = pl.ds(pl.multiple_of(i * GROUP, GROUP), GROUP)
        return jnp.concatenate(
            [q[here, g * HEAD : (g + 1) * HEAD] for g in range(heads)], axis=0
        )

    def cached(i):
        here = pl.ds(pl.multiple_of(i * GROUP * span, GROUP * span), GROUP * span)
        scores = mt(queries_of(i), kbuf[here, :]) * scale
        length = lens[pl.ds(pl.multiple_of(i * GROUP, GROUP), GROUP), 0:1]
        length = jnp.concatenate([length] * heads, axis=0)
        begin = (iota(length.shape, 0) & (GROUP - 1)) * span
        end = begin + length.astype(jnp.int32)
        place = iota(scores.shape, 1)
        scores = jnp.where((place >= begin) & (place < end), scores, -1e30)
        top = jnp.max(scores, axis=1, keepdims=True)
        weights = jnp.exp(scores - top)
        o_s[i] = mm(weights.astype(BF16), vbuf[here, :])
        m_s[i] = jnp.broadcast_to(top, (GROUP * heads, HEAD))
        l_s[i] = jnp.broadcast_to(jnp.sum(weights, axis=1, keepdims=True), (GROUP * heads, HEAD))

    each(0, decodes // GROUP, cached)
    def factors_of(c):
        return d[:, :, c * width : (c + 1) * width].reshape(-1, width)

    second_hop[0].all().wait_recv()
    got = mm(swap, r2a[...].reshape(slots, -1)).astype(BF16)
    partial = mt(got[:, 0:width], factors_of(0))
    code = got[:, width:].astype(F32)
    second_hop[1].all().wait_recv()
    partial = partial + mt(r2b[...].reshape(slots, width), factors_of(1))
    lane_slot = (iota((slots, HEAD), 1) >> 6) + 1
    lane_slot = lane_slot.astype(F32)
    low_half = code == lane_slot
    high_half = code == lane_slot + 2.0
    mine = jnp.where(low_half, partial[:, 0:HEAD], 0.0) + jnp.where(
        high_half, partial[:, HEAD:], 0.0
    )
    ysend[...] = mine.astype(BF16)
    for k in far_first(tps):
        low_copy(k).start()

    sign = jnp.where(iota((1, HEAD), 1) < HALF, -1.0, 1.0)

    def rotated(keys, cosine, sine):
        return keys * cosine + pltpu.roll(keys, HALF, 1) * (sine * sign)

    def finish(b):
        here = pl.ds(pl.multiple_of(b * rows, rows), rows)
        direct_copy(b).wait_recv()
        sum_copy(b).wait_recv()
        total = own[here, :] + rd[b].astype(F32) + rc[b].astype(F32)
        own[here, :] = total
        low_c, low_s = low_ref[0:PIECE, 0:HEAD], low_ref[0:PIECE, HEAD:]
        for i in range(rows // PIECE):
            if b == 0 and i == 0:
                continue
            a = b * (rows // PIECE) + i - 1
            ca, sa = base[a : a + 1, 0:HEAD], base[a : a + 1, HEAD:]
            piece = total[i * PIECE : (i + 1) * PIECE]
            keys = rotated(piece[:, 0:HEAD], ca * low_c - sa * low_s, sa * low_c + ca * low_s)
            stage[pl.ds(2 * i * PIECE, PIECE, stride=2), :] = keys
            stage[pl.ds(2 * i * PIECE + 1, PIECE, stride=2), :] = piece[:, HEAD:]
        skip = 2 * PIECE if b == 0 else 0
        begin = 2 * (b * rows - decodes) + skip
        pre_out[begin : begin + 2 * rows - skip, :] = stage[skip:, :].astype(BF16)

    finish(0)

    for k in far_first(tps):
        low_copy(k).wait_recv()
    whole = mine
    for k in range(3):
        whole = whole + yrecv[k].astype(F32)
    wide = jnp.concatenate(
        [jnp.where(low_half, whole, 0.0), jnp.where(high_half, whole, 0.0)], axis=1
    )
    coarse = wide.astype(BF16)
    fine = (wide - coarse.astype(F32)).astype(BF16)
    factors = uall[...].reshape(-1, 2 * HEAD)
    delta = mm(coarse, factors) + mm(fine, factors)
    s3[...] = delta.astype(BF16).reshape(planes, 16, 2 * HEAD)
    back_hop[0].start()

    finish(2)
    finish(1)

    back_hop[0].all().wait_recv()
    s4[...] = mm(swap, r3[...].reshape(slots, -1)).astype(BF16).reshape(PLANE, 16, -1)
    back_hop[1].start()

    finish(3)

    chosen = lens[:, 0:1] == iota((decodes, low_ref.shape[0]), 1).astype(F32)
    angles = lax.dot_general(
        jnp.where(chosen, 1.0, 0.0),
        low_ref[...],
        (((1,), (0,)), ((), ())),
        precision=lax.Precision.HIGHEST,
        preferred_element_type=F32,
    )
    back_hop[1].all().wait_recv()
    both = own[0:decodes, :] + mm(placing_back, r4[...].reshape(slots, -1))
    keys = rotated(both[:, 0:HEAD], angles[:, 0:HEAD], angles[:, HEAD:]).astype(BF16).astype(F32)
    values = both[:, HEAD:].astype(BF16).astype(F32)
    dec[pl.ds(0, decodes, stride=2), :] = keys
    dec[pl.ds(1, decodes, stride=2), :] = values
    dec_out[...] = dec[...].astype(BF16)
    for i in range(decodes // GROUP):
        key = jnp.concatenate([keys[i * GROUP : (i + 1) * GROUP]] * heads, axis=0)
        value = jnp.concatenate([values[i * GROUP : (i + 1) * GROUP]] * heads, axis=0)
        score = jnp.sum(queries_of(i).astype(F32) * key, axis=1, keepdims=True) * scale
        old = m_s[i]
        top = jnp.maximum(old, score)
        shrink = jnp.exp(old - top)
        share = jnp.exp(score - top)
        result = (o_s[i] * shrink + share * value) / (l_s[i] * shrink + share)
        for g in range(heads):
            att_out[i * GROUP : (i + 1) * GROUP, g * HEAD : (g + 1) * HEAD] = result[
                g * GROUP : (g + 1) * GROUP
            ].astype(BF16)

    for hop in first_hop + second_hop + back_hop:
        hop.all().wait_send()
    for k in far_first(tps):
        up_copy(k).wait_send()
        low_copy(k).wait_send()

    def sent(b):
        relay_copy(b).wait_send()
        direct_copy(b).wait_send()
        sum_copy(b).wait_send()

    each(0, BLOCKS, sent)


def shards(
    normed_input_rows,
    key_projection_weight,
    value_projection_weight,
    adapter_down_factors,
    adapter_up_factors,
    request_owner_replica,
    request_adapter_slot,
    prefill_adapter_slot,
    prefill_first_row,
    context_length,
    request_page_table,
    queries,
    rotated_cache_keys,
    paged_cache_values,
):
    total, width = normed_input_rows.shape
    decodes = request_adapter_slot.shape[0]
    adapters, _, rank = adapter_down_factors.shape
    pages, page, local = rotated_cache_keys.shape
    slots = 2 * lax.axis_size("rep")
    planes = lax.axis_size("rep") // PLANE
    tps = lax.axis_size("tp")
    rows = total // BLOCKS
    part = width // CHUNKS
    prefills = total - decodes
    groups = decodes // GROUP
    heads = queries.shape[1] // HEAD
    span = decodes * request_page_table.shape[1] * page
    vmem = pl.BlockSpec(memory_space=pltpu.VMEM)
    hbm = pl.BlockSpec(memory_space=pltpu.HBM)
    dma = pltpu.SemaphoreType.DMA

    def bf(*shape):
        return pltpu.VMEM(shape, BF16)

    def fl(*shape):
        return pltpu.VMEM(shape, F32)

    decode_kv, prefill_kv, attended = pl.pallas_call(
        kernel,
        out_shape=(
            jax.ShapeDtypeStruct((2 * decodes, HEAD), BF16),
            jax.ShapeDtypeStruct((2 * prefills, HEAD), BF16),
            jax.ShapeDtypeStruct(queries.shape, BF16),
        ),
        in_specs=[hbm] * 16,
        out_specs=(vmem, vmem, vmem),
        scratch_shapes=[
            bf(2 * adapters * rank, HEAD),
            pltpu.VMEM((1, decodes), jnp.int32),
            pltpu.VMEM((1, decodes), jnp.int32),
            pltpu.SMEM((1,), jnp.int32),
            pltpu.SMEM((1,), jnp.int32),
            pltpu.VMEM((1, decodes), jnp.int32),
            pltpu.SMEM(request_page_table.shape[::-1], jnp.int32),
            fl(128, 2 * HEAD),
            fl(64, 2 * HEAD),
            bf(total, width),
            bf(tps, width, 2 * HEAD),
            bf(adapters, rank, width),
            bf(*queries.shape),
            bf(pages, page, local),
            bf(pages, page, local),
            bf(span, HEAD),
            bf(span, HEAD),
            bf(planes, 16, part + HEAD),
            bf(planes, 16, part),
            bf(planes, 16, part + HEAD),
            bf(planes, 16, part),
            bf(PLANE, 16, part + HEAD),
            bf(PLANE, 16, part),
            bf(PLANE, 16, part + HEAD),
            bf(PLANE, 16, part),
            bf(PLANE, 16, 2 * HEAD),
            bf(PLANE, 16, 2 * HEAD),
            bf(planes, 16, 2 * HEAD),
            bf(planes, 16, 2 * HEAD),
            bf(adapters, rank, 2 * HEAD),
            bf(tps, rank, 2 * HEAD),
            bf(slots, HEAD),
            bf(tps - 1, slots, HEAD),
        ]
        + [bf(BLOCKS, rows, 2 * HEAD)] * 6
        + [
            bf(total, rank),
            fl(total, 2 * HEAD),
            fl(2 * rows, HEAD),
            fl(2 * decodes, HEAD),
            fl(16, 2 * HEAD),
            fl(decodes, HEAD),
            fl(groups, GROUP * heads, HEAD),
            fl(groups, GROUP * heads, HEAD),
            fl(groups, GROUP * heads, HEAD),
            dma((BLOCKS + 2 * 4 + 4 + 10,)),
            dma((6,)),
            dma((6,)),
            dma((tps,)),
            dma((tps,)),
            dma((3, BLOCKS)),
            dma((3, BLOCKS)),
            dma((tps,)),
            dma((tps,)),
        ],
        compiler_params=pltpu.CompilerParams(
            collective_id=0, has_side_effects=True, vmem_limit_bytes=60 * 1024 * 1024
        ),
    )(
        normed_input_rows,
        key_projection_weight,
        value_projection_weight,
        jnp.swapaxes(adapter_down_factors, 1, 2),
        adapter_up_factors.reshape(-1, HEAD),
        request_owner_replica.reshape(1, -1),
        request_adapter_slot.reshape(1, -1),
        prefill_adapter_slot,
        prefill_first_row,
        context_length.reshape(1, -1),
        request_page_table.T,
        queries,
        rotated_cache_keys,
        paged_cache_values,
        jnp.asarray(trig(1, 128)),
        jnp.asarray(trig(PIECE, 64)),
    )
    return (
        decode_kv.reshape(decodes, 2, HEAD),
        prefill_kv.reshape(prefills, 2, HEAD),
        attended,
    )


def solution(mesh):
    in_specs = (
        P("rep", "tp"),
        P("tp", None),
        P("tp", None),
        P("rep", "tp", None),
        P("rep", None, None, "tp"),
        P("rep", None),
        P("rep"),
        P("rep"),
        P("rep"),
        P("rep"),
        P("rep", None),
        P("rep", "tp"),
        P("rep", None, "tp"),
        P("rep", None, "tp"),
    )
    out_specs = (P("rep", None, "tp"), P("rep", None, "tp"), P("rep", "tp"))
    return jax.shard_map(shards, mesh=mesh, in_specs=in_specs, out_specs=out_specs, check_vma=False)
```

```python
import jax
import jax.numpy as jnp
import numpy as np
from jax import lax
from jax.experimental import pallas as pl
from jax.experimental.pallas import tpu as pltpu
from jax.sharding import PartitionSpec as P

HEAD = 128
HALF = HEAD // 2
ROPE_BASE = 500000.0
PLANE = 8
BLOCKS = 4
CHUNKS = 2
GROUP = 16
PIECE = 64
MESH = pl.DeviceIdType.MESH
F32 = jnp.float32
BF16 = jnp.bfloat16


def mm(a, b):
    return lax.dot_general(a, b, (((1,), (0,)), ((), ())), preferred_element_type=F32)


def mt(a, b):
    return lax.dot_general(a, b, (((1,), (1,)), ((), ())), preferred_element_type=F32)


def iota(shape, axis):
    return lax.broadcasted_iota(jnp.int32, shape, axis)


def one_hot(condition):
    return jnp.where(condition, 1.0, 0.0).astype(BF16)


def trig(step, count):
    frequency = ROPE_BASE ** (-2.0 * np.arange(HALF) / HEAD)
    angles = step * np.arange(count)[:, None] * np.tile(frequency, 2)[None, :]
    return np.concatenate([np.cos(angles), np.sin(angles)], axis=1).astype(np.float32)


def kernel(
    x_hbm,
    wk_hbm,
    wv_hbm,
    d_hbm,
    up_hbm,
    owner_hbm,
    slot_hbm,
    pslot_hbm,
    pfirst_hbm,
    length_hbm,
    table_hbm,
    q_hbm,
    kpool_hbm,
    vpool_hbm,
    low_hbm,
    high_hbm,
    dec_out,
    pre_out,
    att_out,
    up_ref,
    owner_ref,
    slot_ref,
    pslot_ref,
    pfirst_ref,
    length_ref,
    table_ref,
    low_ref,
    high_ref,
    x,
    w,
    d,
    q,
    kpool,
    vpool,
    kbuf,
    vbuf,
    s1a,
    s1b,
    r1a,
    r1b,
    s2a,
    s2b,
    r2a,
    r2b,
    s3,
    r3,
    s4,
    r4,
    uall,
    ug,
    ysend,
    yrecv,
    sr,
    sd,
    sc,
    rr,
    rd,
    rc,
    lrp,
    own,
    stage,
    dec,
    dec_half,
    pre,
    att,
    base,
    lens,
    m_s,
    l_s,
    o_s,
    load_sem,
    ex_s,
    ex_r,
    us,
    ur,
    ys,
    yr,
    ns,
    nr,
):
    t = lax.axis_index("tp")
    rep = lax.axis_index("rep")
    tps = lax.axis_size("tp")
    planes = lax.axis_size("rep") // PLANE
    z = lax.div(rep, PLANE)
    p = lax.rem(rep, PLANE)
    rows = x.shape[0] // BLOCKS
    decodes = q.shape[0]
    slots = 2 * lax.axis_size("rep")
    width = x.shape[1] // CHUNKS
    s1 = (s1a, s1b)

    barrier = pltpu.get_barrier_semaphore()

    def at(rep_to, tp_to):
        return dict(device_id=(rep_to, tp_to), device_id_type=MESH)

    def z_of(dd):
        return lax.rem(z + dd, planes)

    def p_of(dd):
        return lax.rem(p + dd, PLANE)

    def t_of(dd):
        return lax.rem(t + dd, tps)

    def each(low, high, body):
        lax.fori_loop(low, high, lambda i, c: (body(i), c)[1], 0)

    def far_first(count):
        return sorted(range(1, count), key=lambda k: -min(k, count - k))

    for k in far_first(planes):
        pl.semaphore_signal(barrier, inc=1, **at(z_of(k) * PLANE + p, t))
    for k in far_first(PLANE):
        pl.semaphore_signal(barrier, inc=1, **at(z * PLANE + p_of(k), t))
    for k in far_first(tps):
        pl.semaphore_signal(barrier, inc=1, **at(rep, t_of(k)))

    def load(source, target, k):
        return pltpu.make_async_copy(source, target, load_sem.at[k])

    def x_load(b):
        part = pl.ds(b * rows, rows)
        return load(x_hbm.at[part], x.at[part], b)

    def w_load(j):
        columns = pl.ds(pl.multiple_of(t_of(j) * HEAD, HEAD), HEAD)
        return (
            load(wk_hbm.at[:, columns], w.at[j, :, pl.ds(0, HEAD)], BLOCKS + 2 * j),
            load(wv_hbm.at[:, columns], w.at[j, :, pl.ds(HEAD, HEAD)], BLOCKS + 2 * j + 1),
        )

    k0 = BLOCKS + 2 * 4
    q_load = load(q_hbm, q, k0)
    d_load = load(d_hbm, d, k0 + 1)
    kpool_load = load(kpool_hbm, kpool, k0 + 2)
    vpool_load = load(vpool_hbm, vpool, k0 + 3)
    small = [
        load(source, target, k0 + 4 + i)
        for i, (source, target) in enumerate(
            (
                (owner_hbm, owner_ref),
                (slot_hbm, slot_ref),
                (length_hbm, length_ref),
                (pslot_hbm, pslot_ref),
                (up_hbm, up_ref),
                (pfirst_hbm, pfirst_ref),
                (low_hbm, low_ref),
                (high_hbm, high_ref),
                (table_hbm, table_ref),
            )
        )
    ]
    head_load = load(x_hbm.at[pl.ds(0, decodes)], x.at[pl.ds(0, decodes)], k0 + 4 + len(small))
    for c in small[:3]:
        c.start()
    head_load.start()
    for c in small[3:]:
        c.start()
    rest = pl.ds(decodes, rows - decodes)
    load(x_hbm.at[rest], x.at[rest], 0).start()
    d_load.start()
    for c in w_load(2):
        c.start()
    for b in (1, 2, 3):
        x_load(b).start()
    for j in (3, 1, 0):
        for c in w_load(j):
            c.start()
    for c in (q_load, kpool_load, vpool_load):
        c.start()

    for c in small[:3]:
        c.wait()

    eye = iota((decodes, decodes), 0) == iota((decodes, decodes), 1)

    def column(row):
        return jnp.sum(jnp.where(eye, jnp.broadcast_to(row, eye.shape), 0.0), axis=1, keepdims=True)

    owner_row = owner_ref[...].astype(F32)
    owner_col = column(owner_row)
    same = owner_col == owner_row
    before_col = iota(eye.shape, 1) < iota(eye.shape, 0)
    before_row = iota(eye.shape, 0) < iota(eye.shape, 1)
    rank_col = jnp.sum(jnp.where(same & before_col, 1.0, 0.0), axis=1, keepdims=True)
    rank_row = jnp.sum(jnp.where(same & before_row, 1.0, 0.0), axis=0, keepdims=True)

    def plane_first(owner, turn):
        owner = owner.astype(jnp.int32)
        return (owner & (PLANE - 1)) * 16 + (owner >> 3) * 2 + turn.astype(jnp.int32)

    slot_of = iota((slots, decodes), 0)
    placing = (
        one_hot((2.0 * owner_row + rank_row).astype(jnp.int32) == slot_of),
        one_hot(plane_first(owner_row, rank_row) == slot_of),
    )
    placing_back = one_hot(plane_first(owner_col, rank_col) == iota((decodes, slots), 1))
    codes = jnp.broadcast_to(column(slot_ref[...].astype(F32)) + 1.0, (decodes, HEAD)).astype(BF16)
    lens[...] = jnp.broadcast_to(column(length_ref[...].astype(F32)), (decodes, HEAD))

    head_load.wait()
    for c in range(CHUNKS):
        placed = mm(placing[c], x[0:decodes, c * width : (c + 1) * width]).astype(BF16)
        s1[c][:, :, 0:width] = placed.reshape(planes, 16, width)
    s1a[:, :, width : width + HEAD] = mm(placing[0], codes).astype(BF16).reshape(planes, 16, HEAD)

    for c in small[3:5]:
        c.wait()
    pairs = up_ref[...]
    count = pairs.shape[0] // 2
    pick = iota((count, 2 * count), 1) - 2 * iota((count, 2 * count), 0)
    rank = uall.shape[1]
    uall[:, :, 0:HEAD] = mm(one_hot(pick == 0), pairs).astype(BF16).reshape(-1, rank, HEAD)
    uall[:, :, HEAD:] = mm(one_hot(pick == 1), pairs).astype(BF16).reshape(-1, rank, HEAD)
    selected = pslot_ref[0]
    ug[t] = uall[selected]

    def copy(source, target, send, recv, where):
        return pltpu.make_async_remote_copy(source, target, send, recv, **where)

    class Exchange:
        def __init__(self, sent, got, me, of, place, send, recv):
            self.sent, self.got, self.me, self.send, self.recv = sent, got, me, send, recv
            self.of, self.place = of, place

        def start(self):
            for k in far_first(PLANE):
                to = self.of(k)
                copy(self.sent.at[to], self.got.at[self.me], self.send, self.recv, self.place(to)).start()
            self.got[self.me] = self.sent[self.me]

        def all(self):
            most = pl.ds(0, PLANE - 1)
            return copy(self.sent.at[most], self.got.at[most], self.send, self.recv, self.place(self.of(1)))

    def over_z(sent, got, k):
        return Exchange(sent, got, z, z_of, lambda to: at(to * PLANE + p, t), ex_s.at[k], ex_r.at[k])

    def over_plane(sent, got, k):
        return Exchange(sent, got, p, p_of, lambda to: at(z * PLANE + to, t), ex_s.at[k], ex_r.at[k])

    first_hop = (over_z(s1a, r1a, 0), over_plane(s1b, r1b, 1))
    second_hop = (over_plane(s2a, r2a, 2), over_z(s2b, r2b, 3))
    back_hop = (over_z(s3, r3, 4), over_plane(s4, r4, 5))

    def up_copy(k):
        return pltpu.make_async_remote_copy(
            ug.at[t], ug.at[t], us.at[k], ur.at[k], **at(rep, t_of(k))
        )

    def low_copy(k):
        return pltpu.make_async_remote_copy(
            ysend, yrecv.at[k - 1], ns.at[k], nr.at[k], **at(rep, t_of(k))
        )

    def ahead(b):
        return 1 + 2 * lax.div(b, 2)

    def back(b):
        return 3 - 2 * lax.div(b, 2)

    def relay_copy(b):
        return pltpu.make_async_remote_copy(
            sr.at[b], rr.at[b], ys.at[0, b], yr.at[0, b], **at(rep, t_of(ahead(b)))
        )

    def direct_copy(b):
        return pltpu.make_async_remote_copy(
            sd.at[b], rd.at[b], ys.at[1, b], yr.at[1, b], **at(rep, t_of(back(b)))
        )

    def sum_copy(b):
        return pltpu.make_async_remote_copy(
            sc.at[b], rc.at[b], ys.at[2, b], yr.at[2, b], **at(rep, t_of(ahead(b)))
        )

    pl.semaphore_wait(barrier, planes - 1 + PLANE - 1 + tps - 1)
    first_hop[0].start()
    first_hop[1].start()
    for k in far_first(tps):
        up_copy(k).start()

    for c in small[5:8]:
        c.wait()
    first = pfirst_ref[0]
    high = high_ref[pl.ds(lax.div(first, PIECE), 1), :]
    low = low_ref[pl.ds(lax.rem(first, PIECE), 1), :]

    def turn(a, b):
        ca, sa, cb, sb = a[:, 0:HEAD], a[:, HEAD:], b[:, 0:HEAD], b[:, HEAD:]
        return ca * cb - sa * sb, sa * cb + ca * sb

    c0, s0 = turn(high, low)
    steps = high_ref[0:16, :]
    cb, sb = steps[:, 0:HEAD], steps[:, HEAD:]
    base[:, 0:HEAD] = c0 * cb - s0 * sb
    base[:, HEAD:] = s0 * cb + c0 * sb

    swap_out = iota((slots, slots), 0)
    swap_in = iota((slots, slots), 1)
    swap = one_hot(
        swap_in == ((swap_out >> 1) & 7) * 16 + (swap_out >> 4) * 2 + (swap_out & 1)
    )

    d_load.wait()
    for c in w_load(2):
        c.wait()

    def part_of(b, j):
        here = pl.ds(pl.multiple_of(b * rows, rows), rows)
        return mm(x[here, :], w[j]) + mm(lrp[here, :], ug[t_of(j)])

    def relay_step(b):
        here = pl.ds(pl.multiple_of(b * rows, rows), rows)

        @pl.when(b == 0)
        def _():
            load(x_hbm.at[rest], x.at[rest], 0).wait()

        @pl.when(b > 0)
        def _():
            x_load(b).wait()

        low_rank = mt(x[here, :], d[selected])
        row = iota(low_rank.shape, 0) + b * rows
        lrp[here, :] = jnp.where(row >= decodes, low_rank, 0.0).astype(BF16)
        own[here, :] = mm(x[here, :], w[2])

    def relay_send(b):
        here = pl.ds(pl.multiple_of(b * rows, rows), rows)
        sr[b] = (own[here, :] + mm(lrp[here, :], ug[t_of(2)])).astype(BF16)
        relay_copy(b).start()

    def direct_step(b):
        sd[b] = part_of(b, back(b)).astype(BF16)
        direct_copy(b).start()

    def sum_step(b):
        part = part_of(b, ahead(b))
        relay_copy(b).wait_recv()
        sc[b] = (part + rr[b].astype(F32)).astype(BF16)

    def own_step(b):
        own[pl.ds(pl.multiple_of(b * rows, rows), rows), :] = part_of(b, 0)

    def order(i):
        return lax.div(i, 2) + 2 * lax.rem(i, 2)

    each(0, BLOCKS, lambda i: relay_step(order(i)))
    for k in far_first(tps):
        up_copy(k).wait_recv()
    each(0, BLOCKS, lambda i: relay_send(order(i)))
    for j in (3, 1):
        for c in w_load(j):
            c.wait()
    each(0, 2, lambda i: direct_step(order(i)))

    def forward(c):
        first_hop[c].all().wait_recv()
        moved = mm(swap, first_hop[c].got[...].reshape(slots, -1)).astype(BF16)
        second_hop[c].sent[...] = moved.reshape(PLANE, 16, -1)
        second_hop[c].start()

    forward(1)
    each(2, BLOCKS, lambda i: direct_step(order(i)))
    each(0, BLOCKS, lambda i: sum_step(order(i)))
    for b in (0, 2):
        sum_copy(b).start()
    forward(0)
    for c in w_load(0):
        c.wait()
    each(0, BLOCKS, own_step)

    for c in (q_load, kpool_load, vpool_load, small[8]):
        c.wait()
    maxp, page = table_ref.shape[0], kpool.shape[1]
    span = maxp * page

    def gather(i):
        for j in range(maxp):
            number = table_ref[j, i]
            here = pl.ds(pl.multiple_of((i * maxp + j) * page, page), page)
            kbuf[here, :] = kpool[number]
            vbuf[here, :] = vpool[number]

    each(0, decodes, gather)
    heads = q.shape[1] // HEAD
    scale = HEAD**-0.5

    def queries_of(i):
        here = pl.ds(pl.multiple_of(i * GROUP, GROUP), GROUP)
        return jnp.concatenate(
            [q[here, g * HEAD : (g + 1) * HEAD] for g in range(heads)], axis=0
        )

    def cached(i):
        here = pl.ds(pl.multiple_of(i * GROUP * span, GROUP * span), GROUP * span)
        scores = mt(queries_of(i), kbuf[here, :]) * scale
        length = lens[pl.ds(pl.multiple_of(i * GROUP, GROUP), GROUP), 0:1]
        length = jnp.concatenate([length] * heads, axis=0)
        begin = (iota(length.shape, 0) & (GROUP - 1)) * span
        end = begin + length.astype(jnp.int32)
        place = iota(scores.shape, 1)
        scores = jnp.where((place >= begin) & (place < end), scores, -1e30)
        top = jnp.max(scores, axis=1, keepdims=True)
        weights = jnp.exp(scores - top)
        o_s[i] = mm(weights.astype(BF16), vbuf[here, :])
        m_s[i] = jnp.broadcast_to(top, (GROUP * heads, HEAD))
        l_s[i] = jnp.broadcast_to(jnp.sum(weights, axis=1, keepdims=True), (GROUP * heads, HEAD))

    each(0, decodes // GROUP, cached)
    def factors_of(c):
        return d[:, :, c * width : (c + 1) * width].reshape(-1, width)

    second_hop[0].all().wait_recv()
    got = mm(swap, r2a[...].reshape(slots, -1)).astype(BF16)
    partial = mt(got[:, 0:width], factors_of(0))
    code = got[:, width:].astype(F32)
    second_hop[1].all().wait_recv()
    partial = partial + mt(r2b[...].reshape(slots, width), factors_of(1))
    lane_slot = (iota((slots, HEAD), 1) >> 6) + 1
    lane_slot = lane_slot.astype(F32)
    low_half = code == lane_slot
    high_half = code == lane_slot + 2.0
    mine = jnp.where(low_half, partial[:, 0:HEAD], 0.0) + jnp.where(
        high_half, partial[:, HEAD:], 0.0
    )
    ysend[...] = mine.astype(BF16)
    for k in far_first(tps):
        low_copy(k).start()
    for b in (1, 3):
        sum_copy(b).start()

    written = []
    sign = jnp.where(iota((1, HEAD), 1) < HALF, -1.0, 1.0)

    def rotated(keys, cosine, sine):
        return keys * cosine + pltpu.roll(keys, HALF, 1) * (sine * sign)

    def finish(b):
        here = pl.ds(pl.multiple_of(b * rows, rows), rows)
        direct_copy(b).wait_recv()
        sum_copy(b).wait_recv()
        total = own[here, :] + rd[b].astype(F32) + rc[b].astype(F32)
        own[here, :] = total
        low_c, low_s = low_ref[0:PIECE, 0:HEAD], low_ref[0:PIECE, HEAD:]
        for i in range(rows // PIECE):
            if b == 0 and i == 0:
                continue
            a = b * (rows // PIECE) + i - 1
            ca, sa = base[a : a + 1, 0:HEAD], base[a : a + 1, HEAD:]
            piece = total[i * PIECE : (i + 1) * PIECE]
            keys = rotated(piece[:, 0:HEAD], ca * low_c - sa * low_s, sa * low_c + ca * low_s)
            stage[pl.ds(2 * i * PIECE, PIECE, stride=2), :] = keys
            stage[pl.ds(2 * i * PIECE + 1, PIECE, stride=2), :] = piece[:, HEAD:]
        skip = 2 * PIECE if b == 0 else 0
        begin = 2 * (b * rows - decodes) + skip
        pre[begin : begin + 2 * rows - skip, :] = stage[skip:, :].astype(BF16)
        here = pl.ds(begin, 2 * rows - skip)
        written.append(load(pre.at[here], pre_out.at[here], b))
        written[-1].start()

    finish(0)
    finish(2)

    for k in far_first(tps):
        low_copy(k).wait_recv()
    whole = mine
    for k in range(3):
        whole = whole + yrecv[k].astype(F32)
    wide = jnp.concatenate(
        [jnp.where(low_half, whole, 0.0), jnp.where(high_half, whole, 0.0)], axis=1
    )
    coarse = wide.astype(BF16)
    fine = (wide - coarse.astype(F32)).astype(BF16)
    factors = uall[...].reshape(-1, 2 * HEAD)
    delta = mm(coarse, factors) + mm(fine, factors)
    s3[...] = delta.astype(BF16).reshape(planes, 16, 2 * HEAD)
    back_hop[0].start()

    finish(1)
    finish(3)

    back_hop[0].all().wait_recv()
    s4[...] = mm(swap, r3[...].reshape(slots, -1)).astype(BF16).reshape(PLANE, 16, -1)
    back_hop[1].start()

    chosen = lens[:, 0:1] == iota((decodes, low_ref.shape[0]), 1).astype(F32)
    angles = lax.dot_general(
        jnp.where(chosen, 1.0, 0.0),
        low_ref[...],
        (((1,), (0,)), ((), ())),
        precision=lax.Precision.HIGHEST,
        preferred_element_type=F32,
    )
    back_hop[1].all().wait_recv()
    both = own[0:decodes, :] + mm(placing_back, r4[...].reshape(slots, -1))
    keys = rotated(both[:, 0:HEAD], angles[:, 0:HEAD], angles[:, HEAD:]).astype(BF16).astype(F32)
    values = both[:, HEAD:].astype(BF16).astype(F32)
    dec[pl.ds(0, decodes, stride=2), :] = keys
    dec[pl.ds(1, decodes, stride=2), :] = values
    dec_half[...] = dec[...].astype(BF16)
    written.append(load(dec_half, dec_out, BLOCKS))
    written[-1].start()
    for i in range(decodes // GROUP):
        key = jnp.concatenate([keys[i * GROUP : (i + 1) * GROUP]] * heads, axis=0)
        value = jnp.concatenate([values[i * GROUP : (i + 1) * GROUP]] * heads, axis=0)
        score = jnp.sum(queries_of(i).astype(F32) * key, axis=1, keepdims=True) * scale
        old = m_s[i]
        top = jnp.maximum(old, score)
        shrink = jnp.exp(old - top)
        share = jnp.exp(score - top)
        result = (o_s[i] * shrink + share * value) / (l_s[i] * shrink + share)
        for g in range(heads):
            att[i * GROUP : (i + 1) * GROUP, g * HEAD : (g + 1) * HEAD] = result[
                g * GROUP : (g + 1) * GROUP
            ].astype(BF16)
    written.append(load(att, att_out, BLOCKS + 1))
    written[-1].start()

    for hop in first_hop + second_hop + back_hop:
        hop.all().wait_send()
    for k in far_first(tps):
        up_copy(k).wait_send()
        low_copy(k).wait_send()

    def sent(b):
        relay_copy(b).wait_send()
        direct_copy(b).wait_send()
        sum_copy(b).wait_send()

    each(0, BLOCKS, sent)
    for c in written:
        c.wait()


def hand_over(dec, pre, att, dec_out, pre_out, att_out, pre_held, att_held, dec_held, sem):
    ways = ((pre, pre_held, pre_out), (att, att_held, att_out), (dec, dec_held, dec_out))
    fetched = [pltpu.make_async_copy(a, b, sem.at[0, i]) for i, (a, b, _) in enumerate(ways)]
    written = [pltpu.make_async_copy(b, c, sem.at[1, i]) for i, (_, b, c) in enumerate(ways)]
    for c in fetched:
        c.start()
    for c, e in zip(fetched, written):
        c.wait()
        e.start()
    for e in written:
        e.wait()


def shards(
    normed_input_rows,
    key_projection_weight,
    value_projection_weight,
    adapter_down_factors,
    adapter_up_factors,
    request_owner_replica,
    request_adapter_slot,
    prefill_adapter_slot,
    prefill_first_row,
    context_length,
    request_page_table,
    queries,
    rotated_cache_keys,
    paged_cache_values,
):
    total, width = normed_input_rows.shape
    decodes = request_adapter_slot.shape[0]
    adapters, _, rank = adapter_down_factors.shape
    pages, page, local = rotated_cache_keys.shape
    slots = 2 * lax.axis_size("rep")
    planes = lax.axis_size("rep") // PLANE
    tps = lax.axis_size("tp")
    rows = total // BLOCKS
    part = width // CHUNKS
    prefills = total - decodes
    groups = decodes // GROUP
    heads = queries.shape[1] // HEAD
    span = decodes * request_page_table.shape[1] * page
    hbm = pl.BlockSpec(memory_space=pltpu.HBM)
    dma = pltpu.SemaphoreType.DMA

    def bf(*shape):
        return pltpu.VMEM(shape, BF16)

    def fl(*shape):
        return pltpu.VMEM(shape, F32)

    decode_kv, prefill_kv, attended = pl.pallas_call(
        kernel,
        out_shape=(
            jax.ShapeDtypeStruct((2 * decodes, HEAD), BF16),
            jax.ShapeDtypeStruct((2 * prefills, HEAD), BF16),
            jax.ShapeDtypeStruct(queries.shape, BF16),
        ),
        in_specs=[hbm] * 16,
        out_specs=(hbm, hbm, hbm),
        scratch_shapes=[
            bf(2 * adapters * rank, HEAD),
            pltpu.VMEM((1, decodes), jnp.int32),
            pltpu.VMEM((1, decodes), jnp.int32),
            pltpu.SMEM((1,), jnp.int32),
            pltpu.SMEM((1,), jnp.int32),
            pltpu.VMEM((1, decodes), jnp.int32),
            pltpu.SMEM(request_page_table.shape[::-1], jnp.int32),
            fl(128, 2 * HEAD),
            fl(64, 2 * HEAD),
            bf(total, width),
            bf(tps, width, 2 * HEAD),
            bf(adapters, rank, width),
            bf(*queries.shape),
            bf(pages, page, local),
            bf(pages, page, local),
            bf(span, HEAD),
            bf(span, HEAD),
            bf(planes, 16, part + HEAD),
            bf(planes, 16, part),
            bf(planes, 16, part + HEAD),
            bf(planes, 16, part),
            bf(PLANE, 16, part + HEAD),
            bf(PLANE, 16, part),
            bf(PLANE, 16, part + HEAD),
            bf(PLANE, 16, part),
            bf(PLANE, 16, 2 * HEAD),
            bf(PLANE, 16, 2 * HEAD),
            bf(planes, 16, 2 * HEAD),
            bf(planes, 16, 2 * HEAD),
            bf(adapters, rank, 2 * HEAD),
            bf(tps, rank, 2 * HEAD),
            bf(slots, HEAD),
            bf(tps - 1, slots, HEAD),
        ]
        + [bf(BLOCKS, rows, 2 * HEAD)] * 6
        + [
            bf(total, rank),
            fl(total, 2 * HEAD),
            fl(2 * rows, HEAD),
            fl(2 * decodes, HEAD),
            bf(2 * decodes, HEAD),
            bf(2 * prefills, HEAD),
            bf(*queries.shape),
            fl(16, 2 * HEAD),
            fl(decodes, HEAD),
            fl(groups, GROUP * heads, HEAD),
            fl(groups, GROUP * heads, HEAD),
            fl(groups, GROUP * heads, HEAD),
            dma((BLOCKS + 2 * 4 + 4 + 10,)),
            dma((6,)),
            dma((6,)),
            dma((tps,)),
            dma((tps,)),
            dma((3, BLOCKS)),
            dma((3, BLOCKS)),
            dma((tps,)),
            dma((tps,)),
        ],
        compiler_params=pltpu.CompilerParams(
            collective_id=0, has_side_effects=True, vmem_limit_bytes=60 * 1024 * 1024
        ),
    )(
        normed_input_rows,
        key_projection_weight,
        value_projection_weight,
        jnp.swapaxes(adapter_down_factors, 1, 2),
        adapter_up_factors.reshape(-1, HEAD),
        request_owner_replica.reshape(1, -1),
        request_adapter_slot.reshape(1, -1),
        prefill_adapter_slot,
        prefill_first_row,
        context_length.reshape(1, -1),
        request_page_table.T,
        queries,
        rotated_cache_keys,
        paged_cache_values,
        jnp.asarray(trig(1, 128)),
        jnp.asarray(trig(PIECE, 64)),
    )
    decode_kv, prefill_kv, attended = pl.pallas_call(
        hand_over,
        out_shape=tuple(jax.ShapeDtypeStruct(a.shape, BF16) for a in (decode_kv, prefill_kv, attended)),
        in_specs=[hbm] * 3,
        out_specs=(hbm,) * 3,
        scratch_shapes=[bf(*a.shape) for a in (prefill_kv, attended, decode_kv)] + [dma((2, 3))],
        compiler_params=pltpu.CompilerParams(vmem_limit_bytes=60 * 1024 * 1024),
    )(decode_kv, prefill_kv, attended)
    return (
        decode_kv.reshape(decodes, 2, HEAD),
        prefill_kv.reshape(prefills, 2, HEAD),
        attended,
    )


def solution(mesh):
    in_specs = (
        P("rep", "tp"),
        P("tp", None),
        P("tp", None),
        P("rep", "tp", None),
        P("rep", None, None, "tp"),
        P("rep", None),
        P("rep"),
        P("rep"),
        P("rep"),
        P("rep"),
        P("rep", None),
        P("rep", "tp"),
        P("rep", None, "tp"),
        P("rep", None, "tp"),
    )
    out_specs = (P("rep", None, "tp"), P("rep", None, "tp"), P("rep", "tp"))
    return jax.shard_map(shards, mesh=mesh, in_specs=in_specs, out_specs=out_specs, check_vma=False)
```

```python
import jax
import jax.numpy as jnp
import numpy as np
from jax import lax
from jax.experimental import pallas as pl
from jax.experimental.pallas import tpu as pltpu
from jax.sharding import PartitionSpec as P

HEAD = 128
HALF = HEAD // 2
ROPE_BASE = 500000.0
PLANE = 8
BLOCKS = 4
CHUNKS = 2
GROUP = 16
PIECE = 64
MESH = pl.DeviceIdType.MESH
F32 = jnp.float32
BF16 = jnp.bfloat16


def mm(a, b):
    return lax.dot_general(a, b, (((1,), (0,)), ((), ())), preferred_element_type=F32)


def mt(a, b):
    return lax.dot_general(a, b, (((1,), (1,)), ((), ())), preferred_element_type=F32)


def iota(shape, axis):
    return lax.broadcasted_iota(jnp.int32, shape, axis)


def one_hot(condition):
    return jnp.where(condition, 1.0, 0.0).astype(BF16)


def trig(step, count):
    frequency = ROPE_BASE ** (-2.0 * np.arange(HALF) / HEAD)
    angles = step * np.arange(count)[:, None] * np.tile(frequency, 2)[None, :]
    return np.concatenate([np.cos(angles), np.sin(angles)], axis=1).astype(np.float32)


def kernel(
    x_hbm,
    wk_hbm,
    wv_hbm,
    d_hbm,
    up_hbm,
    owner_hbm,
    slot_hbm,
    pslot_hbm,
    pfirst_hbm,
    length_hbm,
    table_hbm,
    q_hbm,
    kpool_hbm,
    vpool_hbm,
    low_hbm,
    high_hbm,
    dec_out,
    pre_out,
    att_out,
    up_ref,
    owner_ref,
    slot_ref,
    pslot_ref,
    pfirst_ref,
    length_ref,
    table_ref,
    low_ref,
    high_ref,
    x,
    w,
    d,
    q,
    kpool,
    vpool,
    kbuf,
    vbuf,
    s1a,
    s1b,
    r1a,
    r1b,
    s2a,
    s2b,
    r2a,
    r2b,
    s3,
    r3,
    s4,
    r4,
    uall,
    ug,
    ysend,
    yrecv,
    sr,
    sd,
    sc,
    rr,
    rd,
    rc,
    lrp,
    own,
    stage,
    dec,
    dec_half,
    pre,
    att,
    base,
    lens,
    m_s,
    l_s,
    o_s,
    load_sem,
    ex_s,
    ex_r,
    us,
    ur,
    ys,
    yr,
    ns,
    nr,
):
    t = lax.axis_index("tp")
    rep = lax.axis_index("rep")
    tps = lax.axis_size("tp")
    planes = lax.axis_size("rep") // PLANE
    z = lax.div(rep, PLANE)
    p = lax.rem(rep, PLANE)
    rows = x.shape[0] // BLOCKS
    decodes = q.shape[0]
    slots = 2 * lax.axis_size("rep")
    width = x.shape[1] // CHUNKS
    s1 = (s1a, s1b)

    barrier = pltpu.get_barrier_semaphore()

    def at(rep_to, tp_to):
        return dict(device_id=(rep_to, tp_to), device_id_type=MESH)

    def z_of(dd):
        return lax.rem(z + dd, planes)

    def p_of(dd):
        return lax.rem(p + dd, PLANE)

    def t_of(dd):
        return lax.rem(t + dd, tps)

    def each(low, high, body):
        lax.fori_loop(low, high, lambda i, c: (body(i), c)[1], 0)

    def far_first(count):
        return sorted(range(1, count), key=lambda k: -min(k, count - k))

    def load(source, target, k):
        return pltpu.make_async_copy(source, target, load_sem.at[k])

    def x_load(b):
        part = pl.ds(b * rows, rows)
        return load(x_hbm.at[part], x.at[part], b)

    def w_load(j):
        columns = pl.ds(pl.multiple_of(t_of(j) * HEAD, HEAD), HEAD)
        return (
            load(wk_hbm.at[:, columns], w.at[j, :, pl.ds(0, HEAD)], BLOCKS + 2 * j),
            load(wv_hbm.at[:, columns], w.at[j, :, pl.ds(HEAD, HEAD)], BLOCKS + 2 * j + 1),
        )

    k0 = BLOCKS + 2 * 4
    q_load = load(q_hbm, q, k0)
    d_load = load(d_hbm, d, k0 + 1)
    kpool_load = load(kpool_hbm, kpool, k0 + 2)
    vpool_load = load(vpool_hbm, vpool, k0 + 3)
    small = [
        load(source, target, k0 + 4 + i)
        for i, (source, target) in enumerate(
            (
                (owner_hbm, owner_ref),
                (slot_hbm, slot_ref),
                (length_hbm, length_ref),
                (pslot_hbm, pslot_ref),
                (up_hbm, up_ref),
                (pfirst_hbm, pfirst_ref),
                (low_hbm, low_ref),
                (high_hbm, high_ref),
                (table_hbm, table_ref),
            )
        )
    ]
    head_load = load(x_hbm.at[pl.ds(0, decodes)], x.at[pl.ds(0, decodes)], k0 + 4 + len(small))
    small[0].start()
    head_load.start()
    for c in small[1:3]:
        c.start()
    for k in far_first(planes):
        pl.semaphore_signal(barrier, inc=1, **at(z_of(k) * PLANE + p, t))
    for k in far_first(PLANE):
        pl.semaphore_signal(barrier, inc=1, **at(z * PLANE + p_of(k), t))
    for k in far_first(tps):
        pl.semaphore_signal(barrier, inc=1, **at(rep, t_of(k)))
    for c in small[3:]:
        c.start()
    rest = pl.ds(decodes, rows - decodes)
    load(x_hbm.at[rest], x.at[rest], 0).start()
    d_load.start()
    for c in w_load(2):
        c.start()
    for b in (1, 2, 3):
        x_load(b).start()
    for j in (3, 1, 0):
        for c in w_load(j):
            c.start()
    for c in (q_load, kpool_load, vpool_load):
        c.start()

    for c in small[:3]:
        c.wait()

    eye = iota((decodes, decodes), 0) == iota((decodes, decodes), 1)

    def column(row):
        return jnp.sum(jnp.where(eye, jnp.broadcast_to(row, eye.shape), 0.0), axis=1, keepdims=True)

    owner_row = owner_ref[...].astype(F32)
    owner_col = column(owner_row)
    same = owner_col == owner_row
    before_col = iota(eye.shape, 1) < iota(eye.shape, 0)
    before_row = iota(eye.shape, 0) < iota(eye.shape, 1)
    rank_col = jnp.sum(jnp.where(same & before_col, 1.0, 0.0), axis=1, keepdims=True)
    rank_row = jnp.sum(jnp.where(same & before_row, 1.0, 0.0), axis=0, keepdims=True)

    def plane_first(owner, turn):
        owner = owner.astype(jnp.int32)
        return (owner & (PLANE - 1)) * 16 + (owner >> 3) * 2 + turn.astype(jnp.int32)

    slot_of = iota((slots, decodes), 0)
    placing = (
        one_hot((2.0 * owner_row + rank_row).astype(jnp.int32) == slot_of),
        one_hot(plane_first(owner_row, rank_row) == slot_of),
    )
    placing_back = one_hot(plane_first(owner_col, rank_col) == iota((decodes, slots), 1))
    codes = jnp.broadcast_to(column(slot_ref[...].astype(F32)) + 1.0, (decodes, HEAD)).astype(BF16)

    head_load.wait()
    for c in range(CHUNKS):
        placed = mm(placing[c], x[0:decodes, c * width : (c + 1) * width]).astype(BF16)
        s1[c][:, :, 0:width] = placed.reshape(planes, 16, width)
    s1a[:, :, width : width + HEAD] = mm(placing[0], codes).astype(BF16).reshape(planes, 16, HEAD)

    def copy(source, target, send, recv, where):
        return pltpu.make_async_remote_copy(source, target, send, recv, **where)

    class Exchange:
        def __init__(self, sent, got, me, of, place, send, recv):
            self.sent, self.got, self.me, self.send, self.recv = sent, got, me, send, recv
            self.of, self.place = of, place

        def start(self):
            for k in far_first(PLANE):
                to = self.of(k)
                copy(self.sent.at[to], self.got.at[self.me], self.send, self.recv, self.place(to)).start()
            self.got[self.me] = self.sent[self.me]

        def all(self):
            most = pl.ds(0, PLANE - 1)
            return copy(self.sent.at[most], self.got.at[most], self.send, self.recv, self.place(self.of(1)))

    def over_z(sent, got, k):
        return Exchange(sent, got, z, z_of, lambda to: at(to * PLANE + p, t), ex_s.at[k], ex_r.at[k])

    def over_plane(sent, got, k):
        return Exchange(sent, got, p, p_of, lambda to: at(z * PLANE + to, t), ex_s.at[k], ex_r.at[k])

    first_hop = (over_z(s1a, r1a, 0), over_plane(s1b, r1b, 1))
    second_hop = (over_plane(s2a, r2a, 2), over_z(s2b, r2b, 3))
    back_hop = (over_z(s3, r3, 4), over_plane(s4, r4, 5))

    def up_copy(k):
        return pltpu.make_async_remote_copy(
            ug.at[t], ug.at[t], us.at[k], ur.at[k], **at(rep, t_of(k))
        )

    def low_copy(k):
        return pltpu.make_async_remote_copy(
            ysend, yrecv.at[k - 1], ns.at[k], nr.at[k], **at(rep, t_of(k))
        )

    def ahead(b):
        return 1 + 2 * lax.div(b, 2)

    def back(b):
        return 3 - 2 * lax.div(b, 2)

    def relay_copy(b):
        return pltpu.make_async_remote_copy(
            sr.at[b], rr.at[b], ys.at[0, b], yr.at[0, b], **at(rep, t_of(ahead(b)))
        )

    def direct_copy(b):
        return pltpu.make_async_remote_copy(
            sd.at[b], rd.at[b], ys.at[1, b], yr.at[1, b], **at(rep, t_of(back(b)))
        )

    def sum_copy(b):
        return pltpu.make_async_remote_copy(
            sc.at[b], rc.at[b], ys.at[2, b], yr.at[2, b], **at(rep, t_of(ahead(b)))
        )

    pl.semaphore_wait(barrier, planes - 1 + PLANE - 1 + tps - 1)
    first_hop[0].start()
    first_hop[1].start()

    for c in small[3:5]:
        c.wait()
    pairs = up_ref[...]
    count = pairs.shape[0] // 2
    pick = iota((count, 2 * count), 1) - 2 * iota((count, 2 * count), 0)
    rank = uall.shape[1]
    uall[:, :, 0:HEAD] = mm(one_hot(pick == 0), pairs).astype(BF16).reshape(-1, rank, HEAD)
    uall[:, :, HEAD:] = mm(one_hot(pick == 1), pairs).astype(BF16).reshape(-1, rank, HEAD)
    selected = pslot_ref[0]
    ug[t] = uall[selected]
    for k in far_first(tps):
        up_copy(k).start()

    lens[...] = jnp.broadcast_to(column(length_ref[...].astype(F32)), (decodes, HEAD))

    for c in small[5:8]:
        c.wait()
    first = pfirst_ref[0]
    high = high_ref[pl.ds(lax.div(first, PIECE), 1), :]
    low = low_ref[pl.ds(lax.rem(first, PIECE), 1), :]

    def turn(a, b):
        ca, sa, cb, sb = a[:, 0:HEAD], a[:, HEAD:], b[:, 0:HEAD], b[:, HEAD:]
        return ca * cb - sa * sb, sa * cb + ca * sb

    c0, s0 = turn(high, low)
    steps = high_ref[0:16, :]
    cb, sb = steps[:, 0:HEAD], steps[:, HEAD:]
    base[:, 0:HEAD] = c0 * cb - s0 * sb
    base[:, HEAD:] = s0 * cb + c0 * sb

    swap_out = iota((slots, slots), 0)
    swap_in = iota((slots, slots), 1)
    swap = one_hot(
        swap_in == ((swap_out >> 1) & 7) * 16 + (swap_out >> 4) * 2 + (swap_out & 1)
    )

    d_load.wait()
    for c in w_load(2):
        c.wait()

    def part_of(b, j):
        here = pl.ds(pl.multiple_of(b * rows, rows), rows)
        return mm(x[here, :], w[j]) + mm(lrp[here, :], ug[t_of(j)])

    def relay_step(b):
        here = pl.ds(pl.multiple_of(b * rows, rows), rows)

        @pl.when(b == 0)
        def _():
            load(x_hbm.at[rest], x.at[rest], 0).wait()

        @pl.when(b > 0)
        def _():
            x_load(b).wait()

        low_rank = mt(x[here, :], d[selected])
        row = iota(low_rank.shape, 0) + b * rows
        lrp[here, :] = jnp.where(row >= decodes, low_rank, 0.0).astype(BF16)
        own[here, :] = mm(x[here, :], w[2])

    def relay_send(b):
        here = pl.ds(pl.multiple_of(b * rows, rows), rows)
        sr[b] = (own[here, :] + mm(lrp[here, :], ug[t_of(2)])).astype(BF16)
        relay_copy(b).start()

    def direct_step(b):
        sd[b] = part_of(b, back(b)).astype(BF16)
        direct_copy(b).start()

    def sum_step(b):
        part = part_of(b, ahead(b))
        relay_copy(b).wait_recv()
        sc[b] = (part + rr[b].astype(F32)).astype(BF16)

    def own_step(b):
        own[pl.ds(pl.multiple_of(b * rows, rows), rows), :] = part_of(b, 0)

    def order(i):
        return lax.div(i, 2) + 2 * lax.rem(i, 2)

    each(0, BLOCKS, lambda i: relay_step(order(i)))
    for k in far_first(tps):
        up_copy(k).wait_recv()
    each(0, BLOCKS, lambda i: relay_send(order(i)))
    for j in (3, 1):
        for c in w_load(j):
            c.wait()
    each(0, 2, lambda i: direct_step(order(i)))

    def forward(c):
        first_hop[c].all().wait_recv()
        moved = mm(swap, first_hop[c].got[...].reshape(slots, -1)).astype(BF16)
        second_hop[c].sent[...] = moved.reshape(PLANE, 16, -1)
        second_hop[c].start()

    forward(1)
    each(2, BLOCKS, lambda i: direct_step(order(i)))
    for c in w_load(0):
        c.wait()
    each(0, BLOCKS, own_step)
    each(0, 2, lambda i: sum_step(order(i)))
    forward(0)
    each(2, BLOCKS, lambda i: sum_step(order(i)))

    for c in (q_load, kpool_load, vpool_load, small[8]):
        c.wait()
    maxp, page = table_ref.shape[0], kpool.shape[1]
    span = maxp * page

    def gather(i):
        for j in range(maxp):
            number = table_ref[j, i]
            here = pl.ds(pl.multiple_of((i * maxp + j) * page, page), page)
            kbuf[here, :] = kpool[number]
            vbuf[here, :] = vpool[number]

    each(0, decodes, gather)
    heads = q.shape[1] // HEAD
    scale = HEAD**-0.5

    def queries_of(i):
        here = pl.ds(pl.multiple_of(i * GROUP, GROUP), GROUP)
        return jnp.concatenate(
            [q[here, g * HEAD : (g + 1) * HEAD] for g in range(heads)], axis=0
        )

    def cached(i):
        here = pl.ds(pl.multiple_of(i * GROUP * span, GROUP * span), GROUP * span)
        scores = mt(queries_of(i), kbuf[here, :]) * scale
        length = lens[pl.ds(pl.multiple_of(i * GROUP, GROUP), GROUP), 0:1]
        length = jnp.concatenate([length] * heads, axis=0)
        begin = (iota(length.shape, 0) & (GROUP - 1)) * span
        end = begin + length.astype(jnp.int32)
        place = iota(scores.shape, 1)
        scores = jnp.where((place >= begin) & (place < end), scores, -1e30)
        top = jnp.max(scores, axis=1, keepdims=True)
        weights = jnp.exp(scores - top)
        o_s[i] = mm(weights.astype(BF16), vbuf[here, :])
        m_s[i] = jnp.broadcast_to(top, (GROUP * heads, HEAD))
        l_s[i] = jnp.broadcast_to(jnp.sum(weights, axis=1, keepdims=True), (GROUP * heads, HEAD))

    each(0, decodes // GROUP, cached)
    def factors_of(c):
        return d[:, :, c * width : (c + 1) * width].reshape(-1, width)

    second_hop[0].all().wait_recv()
    got = mm(swap, r2a[...].reshape(slots, -1)).astype(BF16)
    partial = mt(got[:, 0:width], factors_of(0))
    code = got[:, width:].astype(F32)
    second_hop[1].all().wait_recv()
    partial = partial + mt(r2b[...].reshape(slots, width), factors_of(1))
    lane_slot = (iota((slots, HEAD), 1) >> 6) + 1
    lane_slot = lane_slot.astype(F32)
    low_half = code == lane_slot
    high_half = code == lane_slot + 2.0
    mine = jnp.where(low_half, partial[:, 0:HEAD], 0.0) + jnp.where(
        high_half, partial[:, HEAD:], 0.0
    )
    ysend[...] = mine.astype(BF16)
    for k in far_first(tps):
        low_copy(k).start()
    for b in (0, 2, 1, 3):
        sum_copy(b).start()

    written = []
    sign = jnp.where(iota((1, HEAD), 1) < HALF, -1.0, 1.0)

    def rotated(keys, cosine, sine):
        return keys * cosine + pltpu.roll(keys, HALF, 1) * (sine * sign)

    def finish(b):
        here = pl.ds(pl.multiple_of(b * rows, rows), rows)
        direct_copy(b).wait_recv()
        sum_copy(b).wait_recv()
        total = own[here, :] + rd[b].astype(F32) + rc[b].astype(F32)
        own[here, :] = total
        low_c, low_s = low_ref[0:PIECE, 0:HEAD], low_ref[0:PIECE, HEAD:]
        for i in range(rows // PIECE):
            if b == 0 and i == 0:
                continue
            a = b * (rows // PIECE) + i - 1
            ca, sa = base[a : a + 1, 0:HEAD], base[a : a + 1, HEAD:]
            piece = total[i * PIECE : (i + 1) * PIECE]
            keys = rotated(piece[:, 0:HEAD], ca * low_c - sa * low_s, sa * low_c + ca * low_s)
            stage[pl.ds(2 * i * PIECE, PIECE, stride=2), :] = keys
            stage[pl.ds(2 * i * PIECE + 1, PIECE, stride=2), :] = piece[:, HEAD:]
        skip = 2 * PIECE if b == 0 else 0
        begin = 2 * (b * rows - decodes) + skip
        pre[begin : begin + 2 * rows - skip, :] = stage[skip:, :].astype(BF16)
        here = pl.ds(begin, 2 * rows - skip)
        written.append(load(pre.at[here], pre_out.at[here], b))
        written[-1].start()

    for k in far_first(tps):
        low_copy(k).wait_recv()
    whole = mine
    for k in range(3):
        whole = whole + yrecv[k].astype(F32)
    wide = jnp.concatenate(
        [jnp.where(low_half, whole, 0.0), jnp.where(high_half, whole, 0.0)], axis=1
    )
    coarse = wide.astype(BF16)
    fine = (wide - coarse.astype(F32)).astype(BF16)
    factors = uall[...].reshape(-1, 2 * HEAD)
    delta = mm(coarse, factors) + mm(fine, factors)
    s3[...] = delta.astype(BF16).reshape(planes, 16, 2 * HEAD)
    back_hop[0].start()

    back_hop[0].all().wait_recv()
    s4[...] = mm(swap, r3[...].reshape(slots, -1)).astype(BF16).reshape(PLANE, 16, -1)
    back_hop[1].start()

    for b in (0, 2, 1, 3):
        finish(b)

    chosen = lens[:, 0:1] == iota((decodes, low_ref.shape[0]), 1).astype(F32)
    angles = lax.dot_general(
        jnp.where(chosen, 1.0, 0.0),
        low_ref[...],
        (((1,), (0,)), ((), ())),
        precision=lax.Precision.HIGHEST,
        preferred_element_type=F32,
    )
    back_hop[1].all().wait_recv()
    both = own[0:decodes, :] + mm(placing_back, r4[...].reshape(slots, -1))
    keys = rotated(both[:, 0:HEAD], angles[:, 0:HEAD], angles[:, HEAD:]).astype(BF16).astype(F32)
    values = both[:, HEAD:].astype(BF16).astype(F32)
    dec[pl.ds(0, decodes, stride=2), :] = keys
    dec[pl.ds(1, decodes, stride=2), :] = values
    dec_half[...] = dec[...].astype(BF16)
    written.append(load(dec_half, dec_out, BLOCKS))
    written[-1].start()
    for i in range(decodes // GROUP):
        key = jnp.concatenate([keys[i * GROUP : (i + 1) * GROUP]] * heads, axis=0)
        value = jnp.concatenate([values[i * GROUP : (i + 1) * GROUP]] * heads, axis=0)
        score = jnp.sum(queries_of(i).astype(F32) * key, axis=1, keepdims=True) * scale
        old = m_s[i]
        top = jnp.maximum(old, score)
        shrink = jnp.exp(old - top)
        share = jnp.exp(score - top)
        result = (o_s[i] * shrink + share * value) / (l_s[i] * shrink + share)
        for g in range(heads):
            att[i * GROUP : (i + 1) * GROUP, g * HEAD : (g + 1) * HEAD] = result[
                g * GROUP : (g + 1) * GROUP
            ].astype(BF16)
    written.append(load(att, att_out, BLOCKS + 1))
    written[-1].start()

    for hop in first_hop + second_hop + back_hop:
        hop.all().wait_send()
    for k in far_first(tps):
        up_copy(k).wait_send()
        low_copy(k).wait_send()

    def sent(b):
        relay_copy(b).wait_send()
        direct_copy(b).wait_send()
        sum_copy(b).wait_send()

    each(0, BLOCKS, sent)
    for c in written:
        c.wait()


def hand_over(dec, pre, att, dec_out, pre_out, att_out, pre_held, att_held, dec_held, sem):
    ways = ((pre, pre_held, pre_out), (att, att_held, att_out), (dec, dec_held, dec_out))
    fetched = [pltpu.make_async_copy(a, b, sem.at[0, i]) for i, (a, b, _) in enumerate(ways)]
    written = [pltpu.make_async_copy(b, c, sem.at[1, i]) for i, (_, b, c) in enumerate(ways)]
    for c in fetched:
        c.start()
    for c, e in zip(fetched, written):
        c.wait()
        e.start()
    for e in written:
        e.wait()


def shards(
    normed_input_rows,
    key_projection_weight,
    value_projection_weight,
    adapter_down_factors,
    adapter_up_factors,
    request_owner_replica,
    request_adapter_slot,
    prefill_adapter_slot,
    prefill_first_row,
    context_length,
    request_page_table,
    queries,
    rotated_cache_keys,
    paged_cache_values,
):
    total, width = normed_input_rows.shape
    decodes = request_adapter_slot.shape[0]
    adapters, _, rank = adapter_down_factors.shape
    pages, page, local = rotated_cache_keys.shape
    slots = 2 * lax.axis_size("rep")
    planes = lax.axis_size("rep") // PLANE
    tps = lax.axis_size("tp")
    rows = total // BLOCKS
    part = width // CHUNKS
    prefills = total - decodes
    groups = decodes // GROUP
    heads = queries.shape[1] // HEAD
    span = decodes * request_page_table.shape[1] * page
    hbm = pl.BlockSpec(memory_space=pltpu.HBM)
    dma = pltpu.SemaphoreType.DMA

    def bf(*shape):
        return pltpu.VMEM(shape, BF16)

    def fl(*shape):
        return pltpu.VMEM(shape, F32)

    decode_kv, prefill_kv, attended = pl.pallas_call(
        kernel,
        out_shape=(
            jax.ShapeDtypeStruct((2 * decodes, HEAD), BF16),
            jax.ShapeDtypeStruct((2 * prefills, HEAD), BF16),
            jax.ShapeDtypeStruct(queries.shape, BF16),
        ),
        in_specs=[hbm] * 16,
        out_specs=(hbm, hbm, hbm),
        scratch_shapes=[
            bf(2 * adapters * rank, HEAD),
            pltpu.VMEM((1, decodes), jnp.int32),
            pltpu.VMEM((1, decodes), jnp.int32),
            pltpu.SMEM((1,), jnp.int32),
            pltpu.SMEM((1,), jnp.int32),
            pltpu.VMEM((1, decodes), jnp.int32),
            pltpu.SMEM(request_page_table.shape[::-1], jnp.int32),
            fl(128, 2 * HEAD),
            fl(64, 2 * HEAD),
            bf(total, width),
            bf(tps, width, 2 * HEAD),
            bf(adapters, rank, width),
            bf(*queries.shape),
            bf(pages, page, local),
            bf(pages, page, local),
            bf(span, HEAD),
            bf(span, HEAD),
            bf(planes, 16, part + HEAD),
            bf(planes, 16, part),
            bf(planes, 16, part + HEAD),
            bf(planes, 16, part),
            bf(PLANE, 16, part + HEAD),
            bf(PLANE, 16, part),
            bf(PLANE, 16, part + HEAD),
            bf(PLANE, 16, part),
            bf(PLANE, 16, 2 * HEAD),
            bf(PLANE, 16, 2 * HEAD),
            bf(planes, 16, 2 * HEAD),
            bf(planes, 16, 2 * HEAD),
            bf(adapters, rank, 2 * HEAD),
            bf(tps, rank, 2 * HEAD),
            bf(slots, HEAD),
            bf(tps - 1, slots, HEAD),
        ]
        + [bf(BLOCKS, rows, 2 * HEAD)] * 6
        + [
            bf(total, rank),
            fl(total, 2 * HEAD),
            fl(2 * rows, HEAD),
            fl(2 * decodes, HEAD),
            bf(2 * decodes, HEAD),
            bf(2 * prefills, HEAD),
            bf(*queries.shape),
            fl(16, 2 * HEAD),
            fl(decodes, HEAD),
            fl(groups, GROUP * heads, HEAD),
            fl(groups, GROUP * heads, HEAD),
            fl(groups, GROUP * heads, HEAD),
            dma((BLOCKS + 2 * 4 + 4 + 10,)),
            dma((6,)),
            dma((6,)),
            dma((tps,)),
            dma((tps,)),
            dma((3, BLOCKS)),
            dma((3, BLOCKS)),
            dma((tps,)),
            dma((tps,)),
        ],
        compiler_params=pltpu.CompilerParams(
            collective_id=0, has_side_effects=True, vmem_limit_bytes=60 * 1024 * 1024
        ),
    )(
        normed_input_rows,
        key_projection_weight,
        value_projection_weight,
        jnp.swapaxes(adapter_down_factors, 1, 2),
        adapter_up_factors.reshape(-1, HEAD),
        request_owner_replica.reshape(1, -1),
        request_adapter_slot.reshape(1, -1),
        prefill_adapter_slot,
        prefill_first_row,
        context_length.reshape(1, -1),
        request_page_table.T,
        queries,
        rotated_cache_keys,
        paged_cache_values,
        jnp.asarray(trig(1, 128)),
        jnp.asarray(trig(PIECE, 64)),
    )
    decode_kv, prefill_kv, attended = pl.pallas_call(
        hand_over,
        out_shape=tuple(jax.ShapeDtypeStruct(a.shape, BF16) for a in (decode_kv, prefill_kv, attended)),
        in_specs=[hbm] * 3,
        out_specs=(hbm,) * 3,
        scratch_shapes=[bf(*a.shape) for a in (prefill_kv, attended, decode_kv)] + [dma((2, 3))],
        compiler_params=pltpu.CompilerParams(vmem_limit_bytes=60 * 1024 * 1024),
    )(decode_kv, prefill_kv, attended)
    return (
        decode_kv.reshape(decodes, 2, HEAD),
        prefill_kv.reshape(prefills, 2, HEAD),
        attended,
    )


def solution(mesh):
    in_specs = (
        P("rep", "tp"),
        P("tp", None),
        P("tp", None),
        P("rep", "tp", None),
        P("rep", None, None, "tp"),
        P("rep", None),
        P("rep"),
        P("rep"),
        P("rep"),
        P("rep"),
        P("rep", None),
        P("rep", "tp"),
        P("rep", None, "tp"),
        P("rep", None, "tp"),
    )
    out_specs = (P("rep", None, "tp"), P("rep", None, "tp"), P("rep", "tp"))
    return jax.shard_map(shards, mesh=mesh, in_specs=in_specs, out_specs=out_specs, check_vma=False)
```

```python
import jax
import jax.numpy as jnp
import numpy as np
from jax import lax
from jax.experimental import pallas as pl
from jax.experimental.pallas import tpu as pltpu
from jax.sharding import PartitionSpec as P

HEAD = 128
HALF = HEAD // 2
ROPE_BASE = 500000.0
PLANE = 8
BLOCKS = 4
CHUNKS = 2
GROUP = 16
PIECE = 64
MESH = pl.DeviceIdType.MESH
F32 = jnp.float32
BF16 = jnp.bfloat16


def mm(a, b):
    return lax.dot_general(a, b, (((1,), (0,)), ((), ())), preferred_element_type=F32)


def mt(a, b):
    return lax.dot_general(a, b, (((1,), (1,)), ((), ())), preferred_element_type=F32)


def iota(shape, axis):
    return lax.broadcasted_iota(jnp.int32, shape, axis)


def one_hot(condition):
    return jnp.where(condition, 1.0, 0.0).astype(BF16)


def trig(step, count):
    frequency = ROPE_BASE ** (-2.0 * np.arange(HALF) / HEAD)
    angles = step * np.arange(count)[:, None] * np.tile(frequency, 2)[None, :]
    return np.concatenate([np.cos(angles), np.sin(angles)], axis=1).astype(np.float32)


def kernel(
    x_hbm,
    wk_hbm,
    wv_hbm,
    d_hbm,
    up_hbm,
    owner_hbm,
    slot_hbm,
    pslot_hbm,
    pfirst_hbm,
    length_hbm,
    table_hbm,
    q_hbm,
    kpool_hbm,
    vpool_hbm,
    low_hbm,
    high_hbm,
    dec_out,
    pre_out,
    att_out,
    up_ref,
    owner_ref,
    slot_ref,
    pslot_ref,
    pfirst_ref,
    length_ref,
    table_ref,
    low_ref,
    high_ref,
    x,
    w,
    d,
    q,
    kpool,
    vpool,
    kbuf,
    vbuf,
    s1a,
    s1b,
    r1a,
    r1b,
    s2a,
    s2b,
    r2a,
    r2b,
    s3,
    r3,
    s4,
    r4,
    uall,
    ug,
    ysend,
    yrecv,
    sr,
    sd,
    sc,
    rr,
    rd,
    rc,
    lrp,
    own,
    stage,
    dec,
    dec_half,
    pre,
    att,
    base,
    lens,
    m_s,
    l_s,
    o_s,
    load_sem,
    ex_s,
    ex_r,
    us,
    ur,
    ys,
    yr,
    ns,
    nr,
):
    t = lax.axis_index("tp")
    rep = lax.axis_index("rep")
    tps = lax.axis_size("tp")
    planes = lax.axis_size("rep") // PLANE
    z = lax.div(rep, PLANE)
    p = lax.rem(rep, PLANE)
    rows = x.shape[0] // BLOCKS
    decodes = q.shape[0]
    slots = 2 * lax.axis_size("rep")
    width = x.shape[1] // CHUNKS
    s1 = (s1a, s1b)

    barrier = pltpu.get_barrier_semaphore()

    def at(rep_to, tp_to):
        return dict(device_id=(rep_to, tp_to), device_id_type=MESH)

    def z_of(dd):
        return lax.rem(z + dd, planes)

    def p_of(dd):
        return lax.rem(p + dd, PLANE)

    def t_of(dd):
        return lax.rem(t + dd, tps)

    def each(low, high, body):
        lax.fori_loop(low, high, lambda i, c: (body(i), c)[1], 0)

    def far_first(count):
        return sorted(range(1, count), key=lambda k: -min(k, count - k))

    def load(source, target, k):
        return pltpu.make_async_copy(source, target, load_sem.at[k])

    def x_load(b):
        part = pl.ds(b * rows, rows)
        return load(x_hbm.at[part], x.at[part], b)

    def w_load(j):
        columns = pl.ds(pl.multiple_of(t_of(j) * HEAD, HEAD), HEAD)
        return (
            load(wk_hbm.at[:, columns], w.at[j, :, pl.ds(0, HEAD)], BLOCKS + 2 * j),
            load(wv_hbm.at[:, columns], w.at[j, :, pl.ds(HEAD, HEAD)], BLOCKS + 2 * j + 1),
        )

    k0 = BLOCKS + 2 * 4
    q_load = load(q_hbm, q, k0)
    d_load = load(d_hbm, d, k0 + 1)
    kpool_load = load(kpool_hbm, kpool, k0 + 2)
    vpool_load = load(vpool_hbm, vpool, k0 + 3)
    small = [
        load(source, target, k0 + 4 + i)
        for i, (source, target) in enumerate(
            (
                (owner_hbm, owner_ref),
                (slot_hbm, slot_ref),
                (length_hbm, length_ref),
                (pslot_hbm, pslot_ref),
                (up_hbm, up_ref),
                (pfirst_hbm, pfirst_ref),
                (low_hbm, low_ref),
                (high_hbm, high_ref),
                (table_hbm, table_ref),
            )
        )
    ]
    head_load = load(x_hbm.at[pl.ds(0, decodes)], x.at[pl.ds(0, decodes)], k0 + 4 + len(small))
    small[0].start()
    head_load.start()
    for c in small[1:3]:
        c.start()
    for k in far_first(planes):
        pl.semaphore_signal(barrier, inc=1, **at(z_of(k) * PLANE + p, t))
    for k in far_first(PLANE):
        pl.semaphore_signal(barrier, inc=1, **at(z * PLANE + p_of(k), t))
    for k in far_first(tps):
        pl.semaphore_signal(barrier, inc=1, **at(rep, t_of(k)))
    for c in small[3:]:
        c.start()
    rest = pl.ds(decodes, rows - decodes)
    load(x_hbm.at[rest], x.at[rest], 0).start()
    d_load.start()
    for c in w_load(2):
        c.start()
    for b in (1, 2, 3):
        x_load(b).start()
    for j in (3, 1, 0):
        for c in w_load(j):
            c.start()
    for c in (q_load, kpool_load, vpool_load):
        c.start()

    for c in small[:3]:
        c.wait()

    eye = iota((decodes, decodes), 0) == iota((decodes, decodes), 1)

    def column(row):
        return jnp.sum(jnp.where(eye, jnp.broadcast_to(row, eye.shape), 0.0), axis=1, keepdims=True)

    owner_row = owner_ref[...].astype(F32)
    owner_col = column(owner_row)
    same = owner_col == owner_row
    before_col = iota(eye.shape, 1) < iota(eye.shape, 0)
    before_row = iota(eye.shape, 0) < iota(eye.shape, 1)
    rank_col = jnp.sum(jnp.where(same & before_col, 1.0, 0.0), axis=1, keepdims=True)
    rank_row = jnp.sum(jnp.where(same & before_row, 1.0, 0.0), axis=0, keepdims=True)

    def plane_first(owner, turn):
        owner = owner.astype(jnp.int32)
        return (owner & (PLANE - 1)) * 16 + (owner >> 3) * 2 + turn.astype(jnp.int32)

    slot_of = iota((slots, decodes), 0)
    placing = (
        one_hot((2.0 * owner_row + rank_row).astype(jnp.int32) == slot_of),
        one_hot(plane_first(owner_row, rank_row) == slot_of),
    )
    placing_back = one_hot(plane_first(owner_col, rank_col) == iota((decodes, slots), 1))
    codes = jnp.broadcast_to(column(slot_ref[...].astype(F32)) + 1.0, (decodes, HEAD)).astype(BF16)

    head_load.wait()
    for c in range(CHUNKS):
        placed = mm(placing[c], x[0:decodes, c * width : (c + 1) * width]).astype(BF16)
        s1[c][:, :, 0:width] = placed.reshape(planes, 16, width)
    s1a[:, :, width : width + HEAD] = mm(placing[0], codes).astype(BF16).reshape(planes, 16, HEAD)

    def copy(source, target, send, recv, where):
        return pltpu.make_async_remote_copy(source, target, send, recv, **where)

    class Exchange:
        def __init__(self, sent, got, me, of, place, send, recv):
            self.sent, self.got, self.me, self.send, self.recv = sent, got, me, send, recv
            self.of, self.place = of, place

        def start(self):
            for k in far_first(PLANE):
                to = self.of(k)
                copy(self.sent.at[to], self.got.at[self.me], self.send, self.recv, self.place(to)).start()
            self.got[self.me] = self.sent[self.me]

        def all(self):
            most = pl.ds(0, PLANE - 1)
            return copy(self.sent.at[most], self.got.at[most], self.send, self.recv, self.place(self.of(1)))

    def over_z(sent, got, k):
        return Exchange(sent, got, z, z_of, lambda to: at(to * PLANE + p, t), ex_s.at[k], ex_r.at[k])

    def over_plane(sent, got, k):
        return Exchange(sent, got, p, p_of, lambda to: at(z * PLANE + to, t), ex_s.at[k], ex_r.at[k])

    first_hop = (over_z(s1a, r1a, 0), over_plane(s1b, r1b, 1))
    second_hop = (over_plane(s2a, r2a, 2), over_z(s2b, r2b, 3))
    back_hop = (over_z(s3, r3, 4), over_plane(s4, r4, 5))

    def up_copy(k):
        return pltpu.make_async_remote_copy(
            ug.at[t], ug.at[t], us.at[k], ur.at[k], **at(rep, t_of(k))
        )

    def low_copy(k):
        return pltpu.make_async_remote_copy(
            ysend, yrecv.at[k - 1], ns.at[k], nr.at[k], **at(rep, t_of(k))
        )

    def ahead(b):
        return 1 + 2 * lax.div(b, 2)

    def back(b):
        return 3 - 2 * lax.div(b, 2)

    def relay_copy(b):
        return pltpu.make_async_remote_copy(
            sr.at[b], rr.at[b], ys.at[0, b], yr.at[0, b], **at(rep, t_of(ahead(b)))
        )

    def direct_copy(b):
        return pltpu.make_async_remote_copy(
            sd.at[b], rd.at[b], ys.at[1, b], yr.at[1, b], **at(rep, t_of(back(b)))
        )

    def sum_copy(b):
        return pltpu.make_async_remote_copy(
            sc.at[b], rc.at[b], ys.at[2, b], yr.at[2, b], **at(rep, t_of(ahead(b)))
        )

    pl.semaphore_wait(barrier, planes - 1 + PLANE - 1 + tps - 1)
    first_hop[0].start()
    first_hop[1].start()

    for c in small[3:5]:
        c.wait()
    pairs = up_ref[...]
    count = pairs.shape[0] // 2
    pick = iota((count, 2 * count), 1) - 2 * iota((count, 2 * count), 0)
    rank = uall.shape[1]
    uall[:, :, 0:HEAD] = mm(one_hot(pick == 0), pairs).astype(BF16).reshape(-1, rank, HEAD)
    uall[:, :, HEAD:] = mm(one_hot(pick == 1), pairs).astype(BF16).reshape(-1, rank, HEAD)
    selected = pslot_ref[0]
    ug[t] = uall[selected]
    for k in far_first(tps):
        up_copy(k).start()

    lens[...] = jnp.broadcast_to(column(length_ref[...].astype(F32)), (decodes, HEAD))

    for c in small[5:8]:
        c.wait()
    first = pfirst_ref[0]
    high = high_ref[pl.ds(lax.div(first, PIECE), 1), :]
    low = low_ref[pl.ds(lax.rem(first, PIECE), 1), :]

    def turn(a, b):
        ca, sa, cb, sb = a[:, 0:HEAD], a[:, HEAD:], b[:, 0:HEAD], b[:, HEAD:]
        return ca * cb - sa * sb, sa * cb + ca * sb

    c0, s0 = turn(high, low)
    steps = high_ref[0:16, :]
    cb, sb = steps[:, 0:HEAD], steps[:, HEAD:]
    base[:, 0:HEAD] = c0 * cb - s0 * sb
    base[:, HEAD:] = s0 * cb + c0 * sb

    swap_out = iota((slots, slots), 0)
    swap_in = iota((slots, slots), 1)
    swap = one_hot(
        swap_in == ((swap_out >> 1) & 7) * 16 + (swap_out >> 4) * 2 + (swap_out & 1)
    )

    d_load.wait()
    for c in w_load(2):
        c.wait()

    def part_of(b, j):
        here = pl.ds(pl.multiple_of(b * rows, rows), rows)
        return mm(x[here, :], w[j]) + mm(lrp[here, :], ug[t_of(j)])

    def relay_step(b):
        here = pl.ds(pl.multiple_of(b * rows, rows), rows)

        @pl.when(b == 0)
        def _():
            load(x_hbm.at[rest], x.at[rest], 0).wait()

        @pl.when(b > 0)
        def _():
            x_load(b).wait()

        low_rank = mt(x[here, :], d[selected])
        row = iota(low_rank.shape, 0) + b * rows
        lrp[here, :] = jnp.where(row >= decodes, low_rank, 0.0).astype(BF16)
        own[here, :] = mm(x[here, :], w[2])

    def relay_sum(b):
        here = pl.ds(pl.multiple_of(b * rows, rows), rows)
        sr[b] = (own[here, :] + mm(lrp[here, :], ug[t_of(2)])).astype(BF16)

    def direct_step(b):
        sd[b] = part_of(b, back(b)).astype(BF16)

    def sum_step(b):
        part = part_of(b, ahead(b))
        relay_copy(b).wait_recv()
        sc[b] = (part + rr[b].astype(F32)).astype(BF16)

    def own_step(b):
        own[pl.ds(pl.multiple_of(b * rows, rows), rows), :] = part_of(b, 0)

    def order(i):
        return lax.div(i, 2) + 2 * lax.rem(i, 2)

    each(0, BLOCKS, lambda i: relay_step(order(i)))
    for k in far_first(tps):
        up_copy(k).wait_recv()
    each(0, 2, lambda i: relay_sum(order(i)))
    for b in (0, 2):
        relay_copy(b).start()
    each(2, BLOCKS, lambda i: relay_sum(order(i)))
    for j in (3, 1):
        for c in w_load(j):
            c.wait()
    each(0, 2, lambda i: direct_step(order(i)))

    def forward(c):
        first_hop[c].all().wait_recv()
        moved = mm(swap, first_hop[c].got[...].reshape(slots, -1)).astype(BF16)
        second_hop[c].sent[...] = moved.reshape(PLANE, 16, -1)
        second_hop[c].start()

    forward(1)
    for b in (1, 3):
        relay_copy(b).start()
    each(2, BLOCKS, lambda i: direct_step(order(i)))
    for c in w_load(0):
        c.wait()
    each(0, BLOCKS, own_step)
    each(0, 2, lambda i: sum_step(order(i)))
    forward(0)
    for b in (0, 2, 1, 3):
        direct_copy(b).start()
    each(2, BLOCKS, lambda i: sum_step(order(i)))

    for c in (q_load, kpool_load, vpool_load, small[8]):
        c.wait()
    maxp, page = table_ref.shape[0], kpool.shape[1]
    span = maxp * page

    def gather(i):
        for j in range(maxp):
            number = table_ref[j, i]
            here = pl.ds(pl.multiple_of((i * maxp + j) * page, page), page)
            kbuf[here, :] = kpool[number]
            vbuf[here, :] = vpool[number]

    each(0, decodes, gather)
    heads = q.shape[1] // HEAD
    scale = HEAD**-0.5

    def queries_of(i):
        here = pl.ds(pl.multiple_of(i * GROUP, GROUP), GROUP)
        return jnp.concatenate(
            [q[here, g * HEAD : (g + 1) * HEAD] for g in range(heads)], axis=0
        )

    def cached(i):
        here = pl.ds(pl.multiple_of(i * GROUP * span, GROUP * span), GROUP * span)
        scores = mt(queries_of(i), kbuf[here, :]) * scale
        length = lens[pl.ds(pl.multiple_of(i * GROUP, GROUP), GROUP), 0:1]
        length = jnp.concatenate([length] * heads, axis=0)
        begin = (iota(length.shape, 0) & (GROUP - 1)) * span
        end = begin + length.astype(jnp.int32)
        place = iota(scores.shape, 1)
        scores = jnp.where((place >= begin) & (place < end), scores, -1e30)
        top = jnp.max(scores, axis=1, keepdims=True)
        weights = jnp.exp(scores - top)
        o_s[i] = mm(weights.astype(BF16), vbuf[here, :])
        m_s[i] = jnp.broadcast_to(top, (GROUP * heads, HEAD))
        l_s[i] = jnp.broadcast_to(jnp.sum(weights, axis=1, keepdims=True), (GROUP * heads, HEAD))

    each(0, decodes // GROUP, cached)
    def factors_of(c):
        return d[:, :, c * width : (c + 1) * width].reshape(-1, width)

    second_hop[0].all().wait_recv()
    got = mm(swap, r2a[...].reshape(slots, -1)).astype(BF16)
    partial = mt(got[:, 0:width], factors_of(0))
    code = got[:, width:].astype(F32)
    second_hop[1].all().wait_recv()
    partial = partial + mt(r2b[...].reshape(slots, width), factors_of(1))
    lane_slot = (iota((slots, HEAD), 1) >> 6) + 1
    lane_slot = lane_slot.astype(F32)
    low_half = code == lane_slot
    high_half = code == lane_slot + 2.0
    mine = jnp.where(low_half, partial[:, 0:HEAD], 0.0) + jnp.where(
        high_half, partial[:, HEAD:], 0.0
    )
    ysend[...] = mine.astype(BF16)
    for k in far_first(tps):
        low_copy(k).start()
    for b in (0, 2, 1, 3):
        sum_copy(b).start()

    written = []
    sign = jnp.where(iota((1, HEAD), 1) < HALF, -1.0, 1.0)

    def rotated(keys, cosine, sine):
        return keys * cosine + pltpu.roll(keys, HALF, 1) * (sine * sign)

    def finish(b):
        here = pl.ds(pl.multiple_of(b * rows, rows), rows)
        direct_copy(b).wait_recv()
        sum_copy(b).wait_recv()
        total = own[here, :] + rd[b].astype(F32) + rc[b].astype(F32)
        own[here, :] = total
        low_c, low_s = low_ref[0:PIECE, 0:HEAD], low_ref[0:PIECE, HEAD:]
        for i in range(rows // PIECE):
            if b == 0 and i == 0:
                continue
            a = b * (rows // PIECE) + i - 1
            ca, sa = base[a : a + 1, 0:HEAD], base[a : a + 1, HEAD:]
            piece = total[i * PIECE : (i + 1) * PIECE]
            keys = rotated(piece[:, 0:HEAD], ca * low_c - sa * low_s, sa * low_c + ca * low_s)
            stage[pl.ds(2 * i * PIECE, PIECE, stride=2), :] = keys
            stage[pl.ds(2 * i * PIECE + 1, PIECE, stride=2), :] = piece[:, HEAD:]
        skip = 2 * PIECE if b == 0 else 0
        begin = 2 * (b * rows - decodes) + skip
        pre[begin : begin + 2 * rows - skip, :] = stage[skip:, :].astype(BF16)
        here = pl.ds(begin, 2 * rows - skip)
        written.append(load(pre.at[here], pre_out.at[here], b))
        written[-1].start()

    for k in far_first(tps):
        low_copy(k).wait_recv()
    whole = mine
    for k in range(3):
        whole = whole + yrecv[k].astype(F32)
    wide = jnp.concatenate(
        [jnp.where(low_half, whole, 0.0), jnp.where(high_half, whole, 0.0)], axis=1
    )
    coarse = wide.astype(BF16)
    fine = (wide - coarse.astype(F32)).astype(BF16)
    factors = uall[...].reshape(-1, 2 * HEAD)
    delta = mm(coarse, factors) + mm(fine, factors)
    s3[...] = delta.astype(BF16).reshape(planes, 16, 2 * HEAD)
    back_hop[0].start()

    back_hop[0].all().wait_recv()
    s4[...] = mm(swap, r3[...].reshape(slots, -1)).astype(BF16).reshape(PLANE, 16, -1)
    back_hop[1].start()

    for b in (0, 2, 1, 3):
        finish(b)

    chosen = lens[:, 0:1] == iota((decodes, low_ref.shape[0]), 1).astype(F32)
    angles = lax.dot_general(
        jnp.where(chosen, 1.0, 0.0),
        low_ref[...],
        (((1,), (0,)), ((), ())),
        precision=lax.Precision.HIGHEST,
        preferred_element_type=F32,
    )
    back_hop[1].all().wait_recv()
    both = own[0:decodes, :] + mm(placing_back, r4[...].reshape(slots, -1))
    keys = rotated(both[:, 0:HEAD], angles[:, 0:HEAD], angles[:, HEAD:]).astype(BF16).astype(F32)
    values = both[:, HEAD:].astype(BF16).astype(F32)
    dec[pl.ds(0, decodes, stride=2), :] = keys
    dec[pl.ds(1, decodes, stride=2), :] = values
    dec_half[...] = dec[...].astype(BF16)
    written.append(load(dec_half, dec_out, BLOCKS))
    written[-1].start()
    for i in range(decodes // GROUP):
        key = jnp.concatenate([keys[i * GROUP : (i + 1) * GROUP]] * heads, axis=0)
        value = jnp.concatenate([values[i * GROUP : (i + 1) * GROUP]] * heads, axis=0)
        score = jnp.sum(queries_of(i).astype(F32) * key, axis=1, keepdims=True) * scale
        old = m_s[i]
        top = jnp.maximum(old, score)
        shrink = jnp.exp(old - top)
        share = jnp.exp(score - top)
        result = (o_s[i] * shrink + share * value) / (l_s[i] * shrink + share)
        for g in range(heads):
            att[i * GROUP : (i + 1) * GROUP, g * HEAD : (g + 1) * HEAD] = result[
                g * GROUP : (g + 1) * GROUP
            ].astype(BF16)
    written.append(load(att, att_out, BLOCKS + 1))
    written[-1].start()

    for hop in first_hop + second_hop + back_hop:
        hop.all().wait_send()
    for k in far_first(tps):
        up_copy(k).wait_send()
        low_copy(k).wait_send()

    def sent(b):
        relay_copy(b).wait_send()
        direct_copy(b).wait_send()
        sum_copy(b).wait_send()

    each(0, BLOCKS, sent)
    for c in written:
        c.wait()


def hand_over(dec, pre, att, dec_out, pre_out, att_out, pre_held, att_held, dec_held, sem):
    ways = ((pre, pre_held, pre_out), (att, att_held, att_out), (dec, dec_held, dec_out))
    fetched = [pltpu.make_async_copy(a, b, sem.at[0, i]) for i, (a, b, _) in enumerate(ways)]
    written = [pltpu.make_async_copy(b, c, sem.at[1, i]) for i, (_, b, c) in enumerate(ways)]
    for c in fetched:
        c.start()
    for c, e in zip(fetched, written):
        c.wait()
        e.start()
    for e in written:
        e.wait()


def shards(
    normed_input_rows,
    key_projection_weight,
    value_projection_weight,
    adapter_down_factors,
    adapter_up_factors,
    request_owner_replica,
    request_adapter_slot,
    prefill_adapter_slot,
    prefill_first_row,
    context_length,
    request_page_table,
    queries,
    rotated_cache_keys,
    paged_cache_values,
):
    total, width = normed_input_rows.shape
    decodes = request_adapter_slot.shape[0]
    adapters, _, rank = adapter_down_factors.shape
    pages, page, local = rotated_cache_keys.shape
    slots = 2 * lax.axis_size("rep")
    planes = lax.axis_size("rep") // PLANE
    tps = lax.axis_size("tp")
    rows = total // BLOCKS
    part = width // CHUNKS
    prefills = total - decodes
    groups = decodes // GROUP
    heads = queries.shape[1] // HEAD
    span = decodes * request_page_table.shape[1] * page
    hbm = pl.BlockSpec(memory_space=pltpu.HBM)
    dma = pltpu.SemaphoreType.DMA

    def bf(*shape):
        return pltpu.VMEM(shape, BF16)

    def fl(*shape):
        return pltpu.VMEM(shape, F32)

    decode_kv, prefill_kv, attended = pl.pallas_call(
        kernel,
        out_shape=(
            jax.ShapeDtypeStruct((2 * decodes, HEAD), BF16),
            jax.ShapeDtypeStruct((2 * prefills, HEAD), BF16),
            jax.ShapeDtypeStruct(queries.shape, BF16),
        ),
        in_specs=[hbm] * 16,
        out_specs=(hbm, hbm, hbm),
        scratch_shapes=[
            bf(2 * adapters * rank, HEAD),
            pltpu.VMEM((1, decodes), jnp.int32),
            pltpu.VMEM((1, decodes), jnp.int32),
            pltpu.SMEM((1,), jnp.int32),
            pltpu.SMEM((1,), jnp.int32),
            pltpu.VMEM((1, decodes), jnp.int32),
            pltpu.SMEM(request_page_table.shape[::-1], jnp.int32),
            fl(128, 2 * HEAD),
            fl(64, 2 * HEAD),
            bf(total, width),
            bf(tps, width, 2 * HEAD),
            bf(adapters, rank, width),
            bf(*queries.shape),
            bf(pages, page, local),
            bf(pages, page, local),
            bf(span, HEAD),
            bf(span, HEAD),
            bf(planes, 16, part + HEAD),
            bf(planes, 16, part),
            bf(planes, 16, part + HEAD),
            bf(planes, 16, part),
            bf(PLANE, 16, part + HEAD),
            bf(PLANE, 16, part),
            bf(PLANE, 16, part + HEAD),
            bf(PLANE, 16, part),
            bf(PLANE, 16, 2 * HEAD),
            bf(PLANE, 16, 2 * HEAD),
            bf(planes, 16, 2 * HEAD),
            bf(planes, 16, 2 * HEAD),
            bf(adapters, rank, 2 * HEAD),
            bf(tps, rank, 2 * HEAD),
            bf(slots, HEAD),
            bf(tps - 1, slots, HEAD),
        ]
        + [bf(BLOCKS, rows, 2 * HEAD)] * 6
        + [
            bf(total, rank),
            fl(total, 2 * HEAD),
            fl(2 * rows, HEAD),
            fl(2 * decodes, HEAD),
            bf(2 * decodes, HEAD),
            bf(2 * prefills, HEAD),
            bf(*queries.shape),
            fl(16, 2 * HEAD),
            fl(decodes, HEAD),
            fl(groups, GROUP * heads, HEAD),
            fl(groups, GROUP * heads, HEAD),
            fl(groups, GROUP * heads, HEAD),
            dma((BLOCKS + 2 * 4 + 4 + 10,)),
            dma((6,)),
            dma((6,)),
            dma((tps,)),
            dma((tps,)),
            dma((3, BLOCKS)),
            dma((3, BLOCKS)),
            dma((tps,)),
            dma((tps,)),
        ],
        compiler_params=pltpu.CompilerParams(
            collective_id=0, has_side_effects=True, vmem_limit_bytes=60 * 1024 * 1024
        ),
    )(
        normed_input_rows,
        key_projection_weight,
        value_projection_weight,
        jnp.swapaxes(adapter_down_factors, 1, 2),
        adapter_up_factors.reshape(-1, HEAD),
        request_owner_replica.reshape(1, -1),
        request_adapter_slot.reshape(1, -1),
        prefill_adapter_slot,
        prefill_first_row,
        context_length.reshape(1, -1),
        request_page_table.T,
        queries,
        rotated_cache_keys,
        paged_cache_values,
        jnp.asarray(trig(1, 128)),
        jnp.asarray(trig(PIECE, 64)),
    )
    decode_kv, prefill_kv, attended = pl.pallas_call(
        hand_over,
        out_shape=tuple(jax.ShapeDtypeStruct(a.shape, BF16) for a in (decode_kv, prefill_kv, attended)),
        in_specs=[hbm] * 3,
        out_specs=(hbm,) * 3,
        scratch_shapes=[bf(*a.shape) for a in (prefill_kv, attended, decode_kv)] + [dma((2, 3))],
        compiler_params=pltpu.CompilerParams(vmem_limit_bytes=60 * 1024 * 1024),
    )(decode_kv, prefill_kv, attended)
    return (
        decode_kv.reshape(decodes, 2, HEAD),
        prefill_kv.reshape(prefills, 2, HEAD),
        attended,
    )


def solution(mesh):
    in_specs = (
        P("rep", "tp"),
        P("tp", None),
        P("tp", None),
        P("rep", "tp", None),
        P("rep", None, None, "tp"),
        P("rep", None),
        P("rep"),
        P("rep"),
        P("rep"),
        P("rep"),
        P("rep", None),
        P("rep", "tp"),
        P("rep", None, "tp"),
        P("rep", None, "tp"),
    )
    out_specs = (P("rep", None, "tp"), P("rep", None, "tp"), P("rep", "tp"))
    return jax.shard_map(shards, mesh=mesh, in_specs=in_specs, out_specs=out_specs, check_vma=False)
```

```python
import jax
import jax.numpy as jnp
import numpy as np
from jax import lax
from jax.experimental import pallas as pl
from jax.experimental.pallas import tpu as pltpu
from jax.sharding import PartitionSpec as P

HEAD = 128
HALF = HEAD // 2
ROPE_BASE = 500000.0
PLANE = 8
BLOCKS = 4
CHUNKS = 2
GROUP = 16
PIECE = 64
LIMIT = 40 * 1024 * 1024
MESH = pl.DeviceIdType.MESH
F32 = jnp.float32
BF16 = jnp.bfloat16


def mm(a, b):
    return lax.dot_general(a, b, (((1,), (0,)), ((), ())), preferred_element_type=F32)


def mt(a, b):
    return lax.dot_general(a, b, (((1,), (1,)), ((), ())), preferred_element_type=F32)


def iota(shape, axis):
    return lax.broadcasted_iota(jnp.int32, shape, axis)


def one_hot(condition):
    return jnp.where(condition, 1.0, 0.0).astype(BF16)


def trig(step, count):
    frequency = ROPE_BASE ** (-2.0 * np.arange(HALF) / HEAD)
    angles = step * np.arange(count)[:, None] * np.tile(frequency, 2)[None, :]
    return np.concatenate([np.cos(angles), np.sin(angles)], axis=1).astype(np.float32)


def kernel(
    x_hbm,
    wk_hbm,
    wv_hbm,
    d_hbm,
    up_hbm,
    owner_hbm,
    slot_hbm,
    pslot_hbm,
    pfirst_hbm,
    length_hbm,
    table_hbm,
    q_hbm,
    kpool_hbm,
    vpool_hbm,
    low_hbm,
    high_hbm,
    out,
    up_ref,
    owner_ref,
    slot_ref,
    pslot_ref,
    pfirst_ref,
    length_ref,
    table_ref,
    low_ref,
    high_ref,
    x,
    w,
    d,
    q,
    kpool,
    vpool,
    kbuf,
    vbuf,
    s1a,
    s1b,
    r1a,
    r1b,
    s2a,
    s2b,
    r2a,
    r2b,
    s3,
    r3,
    s4,
    r4,
    uall,
    ug,
    ysend,
    yrecv,
    sr,
    sd,
    sc,
    rr,
    rd,
    rc,
    lrp,
    own,
    stage,
    dec,
    base,
    lens,
    m_s,
    l_s,
    o_s,
    load_sem,
    ex_s,
    ex_r,
    us,
    ur,
    ys,
    yr,
    ns,
    nr,
):
    t = lax.axis_index("tp")
    rep = lax.axis_index("rep")
    tps = lax.axis_size("tp")
    planes = lax.axis_size("rep") // PLANE
    z = lax.div(rep, PLANE)
    p = lax.rem(rep, PLANE)
    rows = x.shape[0] // BLOCKS
    decodes = q.shape[0]
    slots = 2 * lax.axis_size("rep")
    width = x.shape[1] // CHUNKS
    s1 = (s1a, s1b)

    barrier = pltpu.get_barrier_semaphore()

    def at(rep_to, tp_to):
        return dict(device_id=(rep_to, tp_to), device_id_type=MESH)

    def z_of(dd):
        return lax.rem(z + dd, planes)

    def p_of(dd):
        return lax.rem(p + dd, PLANE)

    def t_of(dd):
        return lax.rem(t + dd, tps)

    def each(low, high, body):
        lax.fori_loop(low, high, lambda i, c: (body(i), c)[1], 0)

    def far_first(count):
        return sorted(range(1, count), key=lambda k: -min(k, count - k))

    def load(source, target, k):
        return pltpu.make_async_copy(source, target, load_sem.at[k])

    def x_load(b):
        part = pl.ds(b * rows, rows)
        return load(x_hbm.at[part], x.at[part], b)

    def w_load(j):
        columns = pl.ds(pl.multiple_of(t_of(j) * HEAD, HEAD), HEAD)
        return (
            load(wk_hbm.at[:, columns], w.at[j, :, pl.ds(0, HEAD)], BLOCKS + 2 * j),
            load(wv_hbm.at[:, columns], w.at[j, :, pl.ds(HEAD, HEAD)], BLOCKS + 2 * j + 1),
        )

    k0 = BLOCKS + 2 * 4
    q_load = load(q_hbm, q, k0)
    d_load = load(d_hbm, d, k0 + 1)
    kpool_load = load(kpool_hbm, kpool, k0 + 2)
    vpool_load = load(vpool_hbm, vpool, k0 + 3)
    small = [
        load(source, target, k0 + 4 + i)
        for i, (source, target) in enumerate(
            (
                (owner_hbm, owner_ref),
                (slot_hbm, slot_ref),
                (length_hbm, length_ref),
                (pslot_hbm, pslot_ref),
                (up_hbm, up_ref),
                (pfirst_hbm, pfirst_ref),
                (low_hbm, low_ref),
                (high_hbm, high_ref),
                (table_hbm, table_ref),
            )
        )
    ]
    head_load = load(x_hbm.at[pl.ds(0, decodes)], x.at[pl.ds(0, decodes)], k0 + 4 + len(small))
    small[0].start()
    head_load.start()
    for c in small[1:3]:
        c.start()
    for k in far_first(planes):
        pl.semaphore_signal(barrier, inc=1, **at(z_of(k) * PLANE + p, t))
    for k in far_first(PLANE):
        pl.semaphore_signal(barrier, inc=1, **at(z * PLANE + p_of(k), t))
    for k in far_first(tps):
        pl.semaphore_signal(barrier, inc=1, **at(rep, t_of(k)))
    for c in small[3:]:
        c.start()
    rest = pl.ds(decodes, rows - decodes)
    load(x_hbm.at[rest], x.at[rest], 0).start()
    d_load.start()
    for c in w_load(2):
        c.start()
    for b in (1, 2, 3):
        x_load(b).start()
    for j in (3, 1, 0):
        for c in w_load(j):
            c.start()
    for c in (q_load, kpool_load, vpool_load):
        c.start()

    for c in small[:3]:
        c.wait()

    eye = iota((decodes, decodes), 0) == iota((decodes, decodes), 1)

    def column(row):
        return jnp.sum(jnp.where(eye, jnp.broadcast_to(row, eye.shape), 0.0), axis=1, keepdims=True)

    owner_row = owner_ref[...].astype(F32)
    owner_col = column(owner_row)
    same = owner_col == owner_row
    before_col = iota(eye.shape, 1) < iota(eye.shape, 0)
    before_row = iota(eye.shape, 0) < iota(eye.shape, 1)
    rank_col = jnp.sum(jnp.where(same & before_col, 1.0, 0.0), axis=1, keepdims=True)
    rank_row = jnp.sum(jnp.where(same & before_row, 1.0, 0.0), axis=0, keepdims=True)

    def plane_first(owner, turn):
        owner = owner.astype(jnp.int32)
        return (owner & (PLANE - 1)) * 16 + (owner >> 3) * 2 + turn.astype(jnp.int32)

    slot_of = iota((slots, decodes), 0)
    placing = (
        one_hot((2.0 * owner_row + rank_row).astype(jnp.int32) == slot_of),
        one_hot(plane_first(owner_row, rank_row) == slot_of),
    )
    placing_back = one_hot(plane_first(owner_col, rank_col) == iota((decodes, slots), 1))
    codes = jnp.broadcast_to(column(slot_ref[...].astype(F32)) + 1.0, (decodes, HEAD)).astype(BF16)

    head_load.wait()
    for c in range(CHUNKS):
        placed = mm(placing[c], x[0:decodes, c * width : (c + 1) * width]).astype(BF16)
        s1[c][:, :, 0:width] = placed.reshape(planes, 16, width)
    s1a[:, :, width : width + HEAD] = mm(placing[0], codes).astype(BF16).reshape(planes, 16, HEAD)

    def copy(source, target, send, recv, where):
        return pltpu.make_async_remote_copy(source, target, send, recv, **where)

    class Exchange:
        def __init__(self, sent, got, me, of, place, send, recv):
            self.sent, self.got, self.me, self.send, self.recv = sent, got, me, send, recv
            self.of, self.place = of, place

        def start(self):
            for k in far_first(PLANE):
                to = self.of(k)
                copy(self.sent.at[to], self.got.at[self.me], self.send, self.recv, self.place(to)).start()
            self.got[self.me] = self.sent[self.me]

        def all(self):
            most = pl.ds(0, PLANE - 1)
            return copy(self.sent.at[most], self.got.at[most], self.send, self.recv, self.place(self.of(1)))

    def over_z(sent, got, k):
        return Exchange(sent, got, z, z_of, lambda to: at(to * PLANE + p, t), ex_s.at[k], ex_r.at[k])

    def over_plane(sent, got, k):
        return Exchange(sent, got, p, p_of, lambda to: at(z * PLANE + to, t), ex_s.at[k], ex_r.at[k])

    first_hop = (over_z(s1a, r1a, 0), over_plane(s1b, r1b, 1))
    second_hop = (over_plane(s2a, r2a, 2), over_z(s2b, r2b, 3))
    back_hop = (over_z(s3, r3, 4), over_plane(s4, r4, 5))

    def up_copy(k):
        return pltpu.make_async_remote_copy(
            ug.at[t], ug.at[t], us.at[k], ur.at[k], **at(rep, t_of(k))
        )

    def low_copy(k):
        return pltpu.make_async_remote_copy(
            ysend, yrecv.at[k - 1], ns.at[k], nr.at[k], **at(rep, t_of(k))
        )

    def ahead(b):
        return 1 + 2 * lax.div(b, 2)

    def back(b):
        return 3 - 2 * lax.div(b, 2)

    def relay_copy(b):
        return pltpu.make_async_remote_copy(
            sr.at[b], rr.at[b], ys.at[0, b], yr.at[0, b], **at(rep, t_of(ahead(b)))
        )

    def direct_copy(b):
        return pltpu.make_async_remote_copy(
            sd.at[b], rd.at[b], ys.at[1, b], yr.at[1, b], **at(rep, t_of(back(b)))
        )

    def sum_copy(b):
        return pltpu.make_async_remote_copy(
            sc.at[b], rc.at[b], ys.at[2, b], yr.at[2, b], **at(rep, t_of(ahead(b)))
        )

    pl.semaphore_wait(barrier, planes - 1 + PLANE - 1 + tps - 1)
    first_hop[0].start()
    first_hop[1].start()

    for c in small[3:5]:
        c.wait()
    pairs = up_ref[...]
    count = pairs.shape[0] // 2
    pick = iota((count, 2 * count), 1) - 2 * iota((count, 2 * count), 0)
    rank = uall.shape[1]
    uall[:, :, 0:HEAD] = mm(one_hot(pick == 0), pairs).astype(BF16).reshape(-1, rank, HEAD)
    uall[:, :, HEAD:] = mm(one_hot(pick == 1), pairs).astype(BF16).reshape(-1, rank, HEAD)
    selected = pslot_ref[0]
    ug[t] = uall[selected]
    for k in far_first(tps):
        up_copy(k).start()

    lens[...] = jnp.broadcast_to(column(length_ref[...].astype(F32)), (decodes, HEAD))

    for c in small[5:8]:
        c.wait()
    first = pfirst_ref[0]
    high = high_ref[pl.ds(lax.div(first, PIECE), 1), :]
    low = low_ref[pl.ds(lax.rem(first, PIECE), 1), :]

    def turn(a, b):
        ca, sa, cb, sb = a[:, 0:HEAD], a[:, HEAD:], b[:, 0:HEAD], b[:, HEAD:]
        return ca * cb - sa * sb, sa * cb + ca * sb

    c0, s0 = turn(high, low)
    steps = high_ref[0:16, :]
    cb, sb = steps[:, 0:HEAD], steps[:, HEAD:]
    base[:, 0:HEAD] = c0 * cb - s0 * sb
    base[:, HEAD:] = s0 * cb + c0 * sb

    swap_out = iota((slots, slots), 0)
    swap_in = iota((slots, slots), 1)
    swap = one_hot(
        swap_in == ((swap_out >> 1) & 7) * 16 + (swap_out >> 4) * 2 + (swap_out & 1)
    )

    d_load.wait()
    for c in w_load(2):
        c.wait()

    def part_of(b, j):
        here = pl.ds(pl.multiple_of(b * rows, rows), rows)
        return mm(x[here, :], w[j]) + mm(lrp[here, :], ug[t_of(j)])

    def relay_step(b):
        here = pl.ds(pl.multiple_of(b * rows, rows), rows)

        @pl.when(b == 0)
        def _():
            load(x_hbm.at[rest], x.at[rest], 0).wait()

        @pl.when(b > 0)
        def _():
            x_load(b).wait()

        low_rank = mt(x[here, :], d[selected])
        row = iota(low_rank.shape, 0) + b * rows
        lrp[here, :] = jnp.where(row >= decodes, low_rank, 0.0).astype(BF16)
        own[here, :] = mm(x[here, :], w[2])

    def relay_sum(b):
        here = pl.ds(pl.multiple_of(b * rows, rows), rows)
        sr[b] = (own[here, :] + mm(lrp[here, :], ug[t_of(2)])).astype(BF16)

    def direct_step(b):
        sd[b] = part_of(b, back(b)).astype(BF16)

    def sum_step(b):
        part = part_of(b, ahead(b))
        relay_copy(b).wait_recv()
        sc[b] = (part + rr[b].astype(F32)).astype(BF16)

    def own_step(b):
        own[pl.ds(pl.multiple_of(b * rows, rows), rows), :] = part_of(b, 0)

    def order(i):
        return lax.div(i, 2) + 2 * lax.rem(i, 2)

    each(0, BLOCKS, lambda i: relay_step(order(i)))
    for k in far_first(tps):
        up_copy(k).wait_recv()
    each(0, 2, lambda i: relay_sum(order(i)))
    for b in (0, 2):
        relay_copy(b).start()
    each(2, BLOCKS, lambda i: relay_sum(order(i)))
    for j in (3, 1):
        for c in w_load(j):
            c.wait()
    each(0, 2, lambda i: direct_step(order(i)))

    def forward(c):
        first_hop[c].all().wait_recv()
        moved = mm(swap, first_hop[c].got[...].reshape(slots, -1)).astype(BF16)
        second_hop[c].sent[...] = moved.reshape(PLANE, 16, -1)
        second_hop[c].start()

    forward(1)
    for b in (1, 3):
        relay_copy(b).start()
    each(2, BLOCKS, lambda i: direct_step(order(i)))
    for c in w_load(0):
        c.wait()
    each(0, BLOCKS, own_step)
    each(0, 2, lambda i: sum_step(order(i)))
    forward(0)
    for b in (0, 2, 1, 3):
        direct_copy(b).start()
    each(2, BLOCKS, lambda i: sum_step(order(i)))

    for c in (q_load, kpool_load, vpool_load, small[8]):
        c.wait()
    maxp, page = table_ref.shape[0], kpool.shape[1]
    span = maxp * page

    def gather(i):
        for j in range(maxp):
            number = table_ref[j, i]
            here = pl.ds(pl.multiple_of((i * maxp + j) * page, page), page)
            kbuf[here, :] = kpool[number]
            vbuf[here, :] = vpool[number]

    each(0, decodes, gather)
    heads = q.shape[1] // HEAD
    scale = HEAD**-0.5

    def queries_of(i):
        here = pl.ds(pl.multiple_of(i * GROUP, GROUP), GROUP)
        return jnp.concatenate(
            [q[here, g * HEAD : (g + 1) * HEAD] for g in range(heads)], axis=0
        )

    def cached(i):
        here = pl.ds(pl.multiple_of(i * GROUP * span, GROUP * span), GROUP * span)
        scores = mt(queries_of(i), kbuf[here, :]) * scale
        length = lens[pl.ds(pl.multiple_of(i * GROUP, GROUP), GROUP), 0:1]
        length = jnp.concatenate([length] * heads, axis=0)
        begin = (iota(length.shape, 0) & (GROUP - 1)) * span
        end = begin + length.astype(jnp.int32)
        place = iota(scores.shape, 1)
        scores = jnp.where((place >= begin) & (place < end), scores, -1e30)
        top = jnp.max(scores, axis=1, keepdims=True)
        weights = jnp.exp(scores - top)
        o_s[i] = mm(weights.astype(BF16), vbuf[here, :])
        m_s[i] = jnp.broadcast_to(top, (GROUP * heads, HEAD))
        l_s[i] = jnp.broadcast_to(jnp.sum(weights, axis=1, keepdims=True), (GROUP * heads, HEAD))

    each(0, decodes // GROUP, cached)
    def factors_of(c):
        return d[:, :, c * width : (c + 1) * width].reshape(-1, width)

    second_hop[0].all().wait_recv()
    got = mm(swap, r2a[...].reshape(slots, -1)).astype(BF16)
    partial = mt(got[:, 0:width], factors_of(0))
    code = got[:, width:].astype(F32)
    second_hop[1].all().wait_recv()
    partial = partial + mt(r2b[...].reshape(slots, width), factors_of(1))
    lane_slot = (iota((slots, HEAD), 1) >> 6) + 1
    lane_slot = lane_slot.astype(F32)
    low_half = code == lane_slot
    high_half = code == lane_slot + 2.0
    mine = jnp.where(low_half, partial[:, 0:HEAD], 0.0) + jnp.where(
        high_half, partial[:, HEAD:], 0.0
    )
    ysend[...] = mine.astype(BF16)
    for k in far_first(tps):
        low_copy(k).start()
    for b in (0, 2, 1, 3):
        sum_copy(b).start()

    sign = jnp.where(iota((1, HEAD), 1) < HALF, -1.0, 1.0)

    def rotated(keys, cosine, sine):
        return keys * cosine + pltpu.roll(keys, HALF, 1) * (sine * sign)

    def finish(b):
        here = pl.ds(pl.multiple_of(b * rows, rows), rows)
        direct_copy(b).wait_recv()
        sum_copy(b).wait_recv()
        total = own[here, :] + rd[b].astype(F32) + rc[b].astype(F32)
        own[here, :] = total
        low_c, low_s = low_ref[0:PIECE, 0:HEAD], low_ref[0:PIECE, HEAD:]
        for i in range(rows // PIECE):
            if b == 0 and i == 0:
                continue
            a = b * (rows // PIECE) + i - 1
            ca, sa = base[a : a + 1, 0:HEAD], base[a : a + 1, HEAD:]
            piece = total[i * PIECE : (i + 1) * PIECE]
            keys = rotated(piece[:, 0:HEAD], ca * low_c - sa * low_s, sa * low_c + ca * low_s)
            stage[pl.ds(2 * i * PIECE, PIECE, stride=2), :] = keys
            stage[pl.ds(2 * i * PIECE + 1, PIECE, stride=2), :] = piece[:, HEAD:]
        skip = 2 * PIECE if b == 0 else 0
        begin = 2 * (b * rows - decodes) + skip
        begin = begin + 2 * decodes
        out[begin : begin + 2 * rows - skip, :] = stage[skip:, :].astype(BF16)

    for k in far_first(tps):
        low_copy(k).wait_recv()
    whole = mine
    for k in range(3):
        whole = whole + yrecv[k].astype(F32)
    wide = jnp.concatenate(
        [jnp.where(low_half, whole, 0.0), jnp.where(high_half, whole, 0.0)], axis=1
    )
    coarse = wide.astype(BF16)
    fine = (wide - coarse.astype(F32)).astype(BF16)
    factors = uall[...].reshape(-1, 2 * HEAD)
    delta = mm(coarse, factors) + mm(fine, factors)
    s3[...] = delta.astype(BF16).reshape(planes, 16, 2 * HEAD)
    back_hop[0].start()

    back_hop[0].all().wait_recv()
    s4[...] = mm(swap, r3[...].reshape(slots, -1)).astype(BF16).reshape(PLANE, 16, -1)
    back_hop[1].start()

    for b in (0, 2, 1, 3):
        finish(b)

    chosen = lens[:, 0:1] == iota((decodes, low_ref.shape[0]), 1).astype(F32)
    angles = lax.dot_general(
        jnp.where(chosen, 1.0, 0.0),
        low_ref[...],
        (((1,), (0,)), ((), ())),
        precision=lax.Precision.HIGHEST,
        preferred_element_type=F32,
    )
    back_hop[1].all().wait_recv()
    both = own[0:decodes, :] + mm(placing_back, r4[...].reshape(slots, -1))
    keys = rotated(both[:, 0:HEAD], angles[:, 0:HEAD], angles[:, HEAD:]).astype(BF16).astype(F32)
    values = both[:, HEAD:].astype(BF16).astype(F32)
    dec[pl.ds(0, decodes, stride=2), :] = keys
    dec[pl.ds(1, decodes, stride=2), :] = values
    out[0 : 2 * decodes, :] = dec[...].astype(BF16)
    for i in range(decodes // GROUP):
        key = jnp.concatenate([keys[i * GROUP : (i + 1) * GROUP]] * heads, axis=0)
        value = jnp.concatenate([values[i * GROUP : (i + 1) * GROUP]] * heads, axis=0)
        score = jnp.sum(queries_of(i).astype(F32) * key, axis=1, keepdims=True) * scale
        old = m_s[i]
        top = jnp.maximum(old, score)
        shrink = jnp.exp(old - top)
        share = jnp.exp(score - top)
        result = (o_s[i] * shrink + share * value) / (l_s[i] * shrink + share)
        for g in range(heads):
            begin = 2 * x.shape[0] + g * decodes + i * GROUP
            out[begin : begin + GROUP, :] = result[g * GROUP : (g + 1) * GROUP].astype(BF16)

    for hop in first_hop + second_hop + back_hop:
        hop.all().wait_send()
    for k in far_first(tps):
        up_copy(k).wait_send()
        low_copy(k).wait_send()

    def sent(b):
        relay_copy(b).wait_send()
        direct_copy(b).wait_send()
        sum_copy(b).wait_send()

    each(0, BLOCKS, sent)


def hand_over(held, dec_out, pre_out, att_out, sem):
    decodes = att_out.shape[0]
    middle = 2 * decodes + pre_out.shape[0]
    copies = [
        pltpu.make_async_copy(held.at[pl.ds(0, 2 * decodes)], dec_out, sem.at[0]),
        pltpu.make_async_copy(held.at[pl.ds(2 * decodes, pre_out.shape[0])], pre_out, sem.at[1]),
    ]
    for g in range(att_out.shape[1] // HEAD):
        source = held.at[pl.ds(middle + g * decodes, decodes)]
        target = att_out.at[:, pl.ds(g * HEAD, HEAD)]
        copies.append(pltpu.make_async_copy(source, target, sem.at[2 + g]))
    for c in copies:
        c.start()
    for c in copies:
        c.wait()


def shards(
    normed_input_rows,
    key_projection_weight,
    value_projection_weight,
    adapter_down_factors,
    adapter_up_factors,
    request_owner_replica,
    request_adapter_slot,
    prefill_adapter_slot,
    prefill_first_row,
    context_length,
    request_page_table,
    queries,
    rotated_cache_keys,
    paged_cache_values,
):
    total, width = normed_input_rows.shape
    decodes = request_adapter_slot.shape[0]
    adapters, _, rank = adapter_down_factors.shape
    pages, page, local = rotated_cache_keys.shape
    slots = 2 * lax.axis_size("rep")
    planes = lax.axis_size("rep") // PLANE
    tps = lax.axis_size("tp")
    rows = total // BLOCKS
    part = width // CHUNKS
    prefills = total - decodes
    groups = decodes // GROUP
    heads = queries.shape[1] // HEAD
    span = decodes * request_page_table.shape[1] * page
    vmem = pl.BlockSpec(memory_space=pltpu.VMEM)
    hbm = pl.BlockSpec(memory_space=pltpu.HBM)
    dma = pltpu.SemaphoreType.DMA

    def bf(*shape):
        return pltpu.VMEM(shape, BF16)

    def fl(*shape):
        return pltpu.VMEM(shape, F32)

    held = pl.pallas_call(
        kernel,
        out_shape=jax.ShapeDtypeStruct((2 * total + decodes * heads, HEAD), BF16),
        in_specs=[hbm] * 16,
        out_specs=vmem,
        scratch_shapes=[
            bf(2 * adapters * rank, HEAD),
            pltpu.VMEM((1, decodes), jnp.int32),
            pltpu.VMEM((1, decodes), jnp.int32),
            pltpu.SMEM((1,), jnp.int32),
            pltpu.SMEM((1,), jnp.int32),
            pltpu.VMEM((1, decodes), jnp.int32),
            pltpu.SMEM(request_page_table.shape[::-1], jnp.int32),
            fl(128, 2 * HEAD),
            fl(64, 2 * HEAD),
            bf(total, width),
            bf(tps, width, 2 * HEAD),
            bf(adapters, rank, width),
            bf(*queries.shape),
            bf(pages, page, local),
            bf(pages, page, local),
            bf(span, HEAD),
            bf(span, HEAD),
            bf(planes, 16, part + HEAD),
            bf(planes, 16, part),
            bf(planes, 16, part + HEAD),
            bf(planes, 16, part),
            bf(PLANE, 16, part + HEAD),
            bf(PLANE, 16, part),
            bf(PLANE, 16, part + HEAD),
            bf(PLANE, 16, part),
            bf(PLANE, 16, 2 * HEAD),
            bf(PLANE, 16, 2 * HEAD),
            bf(planes, 16, 2 * HEAD),
            bf(planes, 16, 2 * HEAD),
            bf(adapters, rank, 2 * HEAD),
            bf(tps, rank, 2 * HEAD),
            bf(slots, HEAD),
            bf(tps - 1, slots, HEAD),
        ]
        + [bf(BLOCKS, rows, 2 * HEAD)] * 6
        + [
            bf(total, rank),
            fl(total, 2 * HEAD),
            fl(2 * rows, HEAD),
            fl(2 * decodes, HEAD),
            fl(16, 2 * HEAD),
            fl(decodes, HEAD),
            fl(groups, GROUP * heads, HEAD),
            fl(groups, GROUP * heads, HEAD),
            fl(groups, GROUP * heads, HEAD),
            dma((BLOCKS + 2 * 4 + 4 + 10,)),
            dma((6,)),
            dma((6,)),
            dma((tps,)),
            dma((tps,)),
            dma((3, BLOCKS)),
            dma((3, BLOCKS)),
            dma((tps,)),
            dma((tps,)),
        ],
        compiler_params=pltpu.CompilerParams(
            collective_id=0, has_side_effects=True, vmem_limit_bytes=LIMIT
        ),
    )(*(a if a.size == 1 else pltpu.with_memory_space_constraint(a, pltpu.HBM) for a in (
        normed_input_rows,
        key_projection_weight,
        value_projection_weight,
        jnp.swapaxes(adapter_down_factors, 1, 2),
        adapter_up_factors.reshape(-1, HEAD),
        request_owner_replica.reshape(1, -1),
        request_adapter_slot.reshape(1, -1),
        prefill_adapter_slot,
        prefill_first_row,
        context_length.reshape(1, -1),
        request_page_table.T,
        queries,
        rotated_cache_keys,
        paged_cache_values,
        jnp.asarray(trig(1, 128)),
        jnp.asarray(trig(PIECE, 64)),
        )))
    decode_kv, prefill_kv, attended = pl.pallas_call(
        hand_over,
        out_shape=(
            jax.ShapeDtypeStruct((2 * decodes, HEAD), BF16),
            jax.ShapeDtypeStruct((2 * prefills, HEAD), BF16),
            jax.ShapeDtypeStruct(queries.shape, BF16),
        ),
        in_specs=[vmem],
        out_specs=(hbm,) * 3,
        scratch_shapes=[dma((2 + heads,))],
        compiler_params=pltpu.CompilerParams(vmem_limit_bytes=LIMIT),
    )(held)
    return (
        decode_kv.reshape(decodes, 2, HEAD),
        prefill_kv.reshape(prefills, 2, HEAD),
        attended,
    )


def solution(mesh):
    in_specs = (
        P("rep", "tp"),
        P("tp", None),
        P("tp", None),
        P("rep", "tp", None),
        P("rep", None, None, "tp"),
        P("rep", None),
        P("rep"),
        P("rep"),
        P("rep"),
        P("rep"),
        P("rep", None),
        P("rep", "tp"),
        P("rep", None, "tp"),
        P("rep", None, "tp"),
    )
    out_specs = (P("rep", None, "tp"), P("rep", None, "tp"), P("rep", "tp"))
    return jax.shard_map(shards, mesh=mesh, in_specs=in_specs, out_specs=out_specs, check_vma=False)
```

```python
import jax
import jax.numpy as jnp
import numpy as np
from jax import lax
from jax.experimental import pallas as pl
from jax.experimental.pallas import tpu as pltpu
from jax.sharding import PartitionSpec as P

HEAD = 128
HALF = HEAD // 2
ROPE_BASE = 500000.0
CORES = 2
COLUMNS = 4
PLANE = CORES * COLUMNS
BLOCKS = 4
CHUNKS = 2
GROUP = 16
PIECE = 64
LIMIT = 40 * 1024 * 1024
MESH = pl.DeviceIdType.MESH
F32 = jnp.float32
BF16 = jnp.bfloat16


def mm(a, b):
    return lax.dot_general(a, b, (((1,), (0,)), ((), ())), preferred_element_type=F32)


def mt(a, b):
    return lax.dot_general(a, b, (((1,), (1,)), ((), ())), preferred_element_type=F32)


def iota(shape, axis):
    return lax.broadcasted_iota(jnp.int32, shape, axis)


def one_hot(condition):
    return jnp.where(condition, 1.0, 0.0).astype(BF16)


def trig(step, count):
    frequency = ROPE_BASE ** (-2.0 * np.arange(HALF) / HEAD)
    angles = step * np.arange(count)[:, None] * np.tile(frequency, 2)[None, :]
    return np.concatenate([np.cos(angles), np.sin(angles)], axis=1).astype(np.float32)


def kernel(
    x_hbm,
    wk_hbm,
    wv_hbm,
    d_hbm,
    up_hbm,
    owner_hbm,
    slot_hbm,
    pslot_hbm,
    pfirst_hbm,
    length_hbm,
    table_hbm,
    q_hbm,
    kpool_hbm,
    vpool_hbm,
    low_hbm,
    high_hbm,
    out,
    up_ref,
    owner_ref,
    slot_ref,
    pslot_ref,
    pfirst_ref,
    length_ref,
    table_ref,
    low_ref,
    high_ref,
    x,
    w,
    d,
    q,
    kpool,
    vpool,
    kbuf,
    vbuf,
    s1a,
    s1b,
    r1a,
    r1b,
    s2a,
    s2b,
    r2a,
    r2b,
    s3,
    r3,
    s4,
    r4,
    uall,
    uall_other,
    d_other,
    ug,
    ysend,
    yrecv,
    sr,
    sd,
    sc,
    rr,
    rd,
    rc,
    lrp,
    own,
    stage,
    dec,
    base,
    lens,
    m_s,
    l_s,
    o_s,
    load_sem,
    ex_s,
    ex_r,
    us,
    ur,
    ys,
    yr,
    ns,
    nr,
):
    t = lax.axis_index("tp")
    rep = lax.axis_index("rep")
    tps = lax.axis_size("tp")
    planes = lax.axis_size("rep") // PLANE
    z = lax.div(rep, PLANE)
    p = lax.rem(rep, PLANE)
    column_of = lax.div(p, CORES)
    core = lax.rem(p, CORES)
    rows = x.shape[0] // BLOCKS
    decodes = q.shape[0]
    slots = 2 * lax.axis_size("rep")
    width = x.shape[1] // CHUNKS
    s1 = (s1a, s1b)

    barrier = pltpu.get_barrier_semaphore()

    def at(rep_to, tp_to):
        return dict(device_id=(rep_to, tp_to), device_id_type=MESH)

    def z_of(dd):
        return lax.rem(z + dd, planes)

    def x_of(dd):
        return lax.rem(column_of + dd, COLUMNS)

    def at_x(to):
        return at(z * PLANE + to * CORES + core, t)

    def at_other_core():
        return at(z * PLANE + column_of * CORES + 1 - core, t)

    def t_of(dd):
        return lax.rem(t + dd, tps)

    def each(low, high, body):
        lax.fori_loop(low, high, lambda i, c: (body(i), c)[1], 0)

    def far_first(count):
        return sorted(range(1, count), key=lambda k: -min(k, count - k))

    def load(source, target, k):
        return pltpu.make_async_copy(source, target, load_sem.at[k])

    def x_load(b):
        part = pl.ds(b * rows, rows)
        return load(x_hbm.at[part], x.at[part], b)

    def w_load(j):
        columns = pl.ds(pl.multiple_of(t_of(j) * HEAD, HEAD), HEAD)
        return (
            load(wk_hbm.at[:, columns], w.at[j, :, pl.ds(0, HEAD)], BLOCKS + 2 * j),
            load(wv_hbm.at[:, columns], w.at[j, :, pl.ds(HEAD, HEAD)], BLOCKS + 2 * j + 1),
        )

    k0 = BLOCKS + 2 * 4
    q_load = load(q_hbm, q, k0)
    d_load = load(d_hbm, d, k0 + 1)
    kpool_load = load(kpool_hbm, kpool, k0 + 2)
    vpool_load = load(vpool_hbm, vpool, k0 + 3)
    small = [
        load(source, target, k0 + 4 + i)
        for i, (source, target) in enumerate(
            (
                (owner_hbm, owner_ref),
                (slot_hbm, slot_ref),
                (length_hbm, length_ref),
                (pslot_hbm, pslot_ref),
                (up_hbm, up_ref),
                (pfirst_hbm, pfirst_ref),
                (low_hbm, low_ref),
                (high_hbm, high_ref),
                (table_hbm, table_ref),
            )
        )
    ]
    head_load = load(x_hbm.at[pl.ds(0, decodes)], x.at[pl.ds(0, decodes)], k0 + 4 + len(small))
    small[0].start()
    head_load.start()
    for c in small[1:3]:
        c.start()
    for k in far_first(planes):
        pl.semaphore_signal(barrier, inc=1, **at(z_of(k) * PLANE + p, t))
    for k in far_first(COLUMNS):
        pl.semaphore_signal(barrier, inc=1, **at_x(x_of(k)))
    pl.semaphore_signal(barrier, inc=1, **at_other_core())
    for k in far_first(tps):
        pl.semaphore_signal(barrier, inc=1, **at(rep, t_of(k)))
    for c in small[3:]:
        c.start()
    rest = pl.ds(decodes, rows - decodes)
    load(x_hbm.at[rest], x.at[rest], 0).start()
    d_load.start()
    for c in w_load(2):
        c.start()
    for b in (1, 2, 3):
        x_load(b).start()
    for j in (3, 1, 0):
        for c in w_load(j):
            c.start()
    for c in (q_load, kpool_load, vpool_load):
        c.start()

    for c in small[:3]:
        c.wait()

    eye = iota((decodes, decodes), 0) == iota((decodes, decodes), 1)

    def column(row):
        return jnp.sum(jnp.where(eye, jnp.broadcast_to(row, eye.shape), 0.0), axis=1, keepdims=True)

    owner_row = owner_ref[...].astype(F32)
    owner_col = column(owner_row)
    same = owner_col == owner_row
    before_col = iota(eye.shape, 1) < iota(eye.shape, 0)
    before_row = iota(eye.shape, 0) < iota(eye.shape, 1)
    rank_col = jnp.sum(jnp.where(same & before_col, 1.0, 0.0), axis=1, keepdims=True)
    rank_row = jnp.sum(jnp.where(same & before_row, 1.0, 0.0), axis=0, keepdims=True)

    def x_first(owner, turn):
        owner = owner.astype(jnp.int32)
        place = ((owner >> 1) & 3) * 32 + (owner >> 3) * 4 + (owner & 1) * 2
        return place + turn.astype(jnp.int32)

    slot_of = iota((slots, decodes), 0)
    placing = (
        one_hot((2.0 * owner_row + rank_row).astype(jnp.int32) == slot_of),
        one_hot(x_first(owner_row, rank_row) == slot_of),
    )
    placing_back = one_hot(x_first(owner_col, rank_col) == iota((decodes, slots), 1))
    codes = jnp.broadcast_to(column(slot_ref[...].astype(F32)) + 1.0, (decodes, HEAD)).astype(BF16)

    head_load.wait()
    for c in range(CHUNKS):
        placed = mm(placing[c], x[0:decodes, c * width : (c + 1) * width]).astype(BF16)
        s1[c][:, :, 0:width] = placed.reshape(s1[c].shape[:2] + (width,))
    s1a[:, :, width : width + HEAD] = mm(placing[0], codes).astype(BF16).reshape(planes, 16, HEAD)

    def copy(source, target, send, recv, where):
        return pltpu.make_async_remote_copy(source, target, send, recv, **where)

    class Exchange:
        def __init__(self, sent, got, me, of, place, k):
            self.sent, self.got, self.me, self.of, self.place = sent, got, me, of, place
            self.send, self.recv, self.count = ex_s.at[k], ex_r.at[k], sent.shape[0]

        def start(self):
            for k in far_first(self.count):
                to = self.of(k)
                copy(self.sent.at[to], self.got.at[self.me], self.send, self.recv, self.place(to)).start()
            self.got[self.me] = self.sent[self.me]

        def all(self):
            most = pl.ds(0, self.count - 1)
            return copy(self.sent.at[most], self.got.at[most], self.send, self.recv, self.place(self.of(1)))

    def over_z(sent, got, k):
        return Exchange(sent, got, z, z_of, lambda to: at(to * PLANE + p, t), k)

    def over_x(sent, got, k):
        return Exchange(sent, got, column_of, x_of, at_x, k)

    first_hop = (over_z(s1a, r1a, 0), over_x(s1b, r1b, 1))
    second_hop = (over_x(s2a, r2a, 2), over_z(s2b, r2b, 3))
    back_hop = (over_z(s3, r3, 4), over_x(s4, r4, 5))

    down_copy = copy(d_hbm, d_other, ex_s.at[6], ex_r.at[6], at_other_core())
    both_up_copy = copy(uall, uall_other, ex_s.at[7], ex_r.at[7], at_other_core())

    def up_copy(k):
        return pltpu.make_async_remote_copy(
            ug.at[t], ug.at[t], us.at[k], ur.at[k], **at(rep, t_of(k))
        )

    def low_copy(k):
        return pltpu.make_async_remote_copy(
            ysend, yrecv.at[k - 1], ns.at[k], nr.at[k], **at(rep, t_of(k))
        )

    def ahead(b):
        return 1 + 2 * lax.div(b, 2)

    def back(b):
        return 3 - 2 * lax.div(b, 2)

    def relay_copy(b):
        return pltpu.make_async_remote_copy(
            sr.at[b], rr.at[b], ys.at[0, b], yr.at[0, b], **at(rep, t_of(ahead(b)))
        )

    def direct_copy(b):
        return pltpu.make_async_remote_copy(
            sd.at[b], rd.at[b], ys.at[1, b], yr.at[1, b], **at(rep, t_of(back(b)))
        )

    def sum_copy(b):
        return pltpu.make_async_remote_copy(
            sc.at[b], rc.at[b], ys.at[2, b], yr.at[2, b], **at(rep, t_of(ahead(b)))
        )

    pl.semaphore_wait(barrier, planes - 1 + COLUMNS - 1 + 1 + tps - 1)
    first_hop[0].start()
    first_hop[1].start()

    for c in small[3:5]:
        c.wait()
    pairs = up_ref[...]
    count = pairs.shape[0] // 2
    pick = iota((count, 2 * count), 1) - 2 * iota((count, 2 * count), 0)
    rank = uall.shape[1]
    uall[:, :, 0:HEAD] = mm(one_hot(pick == 0), pairs).astype(BF16).reshape(-1, rank, HEAD)
    uall[:, :, HEAD:] = mm(one_hot(pick == 1), pairs).astype(BF16).reshape(-1, rank, HEAD)
    selected = pslot_ref[0]
    ug[t] = uall[selected]
    for k in far_first(tps):
        up_copy(k).start()
    both_up_copy.start()
    down_copy.start()

    lens[...] = jnp.broadcast_to(column(length_ref[...].astype(F32)), (decodes, HEAD))

    for c in small[5:8]:
        c.wait()
    first = pfirst_ref[0]
    high = high_ref[pl.ds(lax.div(first, PIECE), 1), :]
    low = low_ref[pl.ds(lax.rem(first, PIECE), 1), :]

    def turn(a, b):
        ca, sa, cb, sb = a[:, 0:HEAD], a[:, HEAD:], b[:, 0:HEAD], b[:, HEAD:]
        return ca * cb - sa * sb, sa * cb + ca * sb

    c0, s0 = turn(high, low)
    steps = high_ref[0:16, :]
    cb, sb = steps[:, 0:HEAD], steps[:, HEAD:]
    base[:, 0:HEAD] = c0 * cb - s0 * sb
    base[:, HEAD:] = s0 * cb + c0 * sb

    out_at = iota((slots, slots), 0)
    in_at = iota((slots, slots), 1)
    to_x = one_hot(in_at == ((out_at >> 2) & 7) * 16 + (out_at >> 5) * 4 + (out_at & 3))
    to_z = one_hot(in_at == ((out_at >> 2) & 3) * 32 + (out_at >> 4) * 4 + (out_at & 3))

    d_load.wait()
    for c in w_load(2):
        c.wait()

    def part_of(b, j):
        here = pl.ds(pl.multiple_of(b * rows, rows), rows)
        return mm(x[here, :], w[j]) + mm(lrp[here, :], ug[t_of(j)])

    def relay_step(b):
        here = pl.ds(pl.multiple_of(b * rows, rows), rows)

        @pl.when(b == 0)
        def _():
            load(x_hbm.at[rest], x.at[rest], 0).wait()

        @pl.when(b > 0)
        def _():
            x_load(b).wait()

        low_rank = mt(x[here, :], d[selected])
        row = iota(low_rank.shape, 0) + b * rows
        lrp[here, :] = jnp.where(row >= decodes, low_rank, 0.0).astype(BF16)
        own[here, :] = mm(x[here, :], w[2])

    def relay_sum(b):
        here = pl.ds(pl.multiple_of(b * rows, rows), rows)
        sr[b] = (own[here, :] + mm(lrp[here, :], ug[t_of(2)])).astype(BF16)

    def direct_step(b):
        sd[b] = part_of(b, back(b)).astype(BF16)

    def sum_step(b):
        part = part_of(b, ahead(b))
        relay_copy(b).wait_recv()
        sc[b] = (part + rr[b].astype(F32)).astype(BF16)

    def own_step(b):
        own[pl.ds(pl.multiple_of(b * rows, rows), rows), :] = part_of(b, 0)

    def order(i):
        return lax.div(i, 2) + 2 * lax.rem(i, 2)

    each(0, BLOCKS, lambda i: relay_step(order(i)))
    for k in far_first(tps):
        up_copy(k).wait_recv()
    each(0, 2, lambda i: relay_sum(order(i)))
    for b in (0, 2):
        relay_copy(b).start()
    each(2, BLOCKS, lambda i: relay_sum(order(i)))
    for j in (3, 1):
        for c in w_load(j):
            c.wait()
    each(0, 2, lambda i: direct_step(order(i)))

    def forward(c):
        first_hop[c].all().wait_recv()
        moved = mm((to_x, to_z)[c], first_hop[c].got[...].reshape(slots, -1)).astype(BF16)
        second_hop[c].sent[...] = moved.reshape(second_hop[c].sent.shape)
        second_hop[c].start()

    forward(1)
    for b in (1, 3):
        relay_copy(b).start()
    each(2, BLOCKS, lambda i: direct_step(order(i)))
    for c in w_load(0):
        c.wait()
    each(0, BLOCKS, own_step)
    each(0, 2, lambda i: sum_step(order(i)))
    forward(0)
    for b in (0, 2, 1, 3):
        direct_copy(b).start()
    each(2, BLOCKS, lambda i: sum_step(order(i)))

    for c in (q_load, kpool_load, vpool_load, small[8]):
        c.wait()
    maxp, page = table_ref.shape[0], kpool.shape[1]
    span = maxp * page

    def gather(i):
        for j in range(maxp):
            number = table_ref[j, i]
            here = pl.ds(pl.multiple_of((i * maxp + j) * page, page), page)
            kbuf[here, :] = kpool[number]
            vbuf[here, :] = vpool[number]

    each(0, decodes, gather)
    heads = q.shape[1] // HEAD
    scale = HEAD**-0.5

    def queries_of(i):
        here = pl.ds(pl.multiple_of(i * GROUP, GROUP), GROUP)
        return jnp.concatenate(
            [q[here, g * HEAD : (g + 1) * HEAD] for g in range(heads)], axis=0
        )

    def cached(i):
        here = pl.ds(pl.multiple_of(i * GROUP * span, GROUP * span), GROUP * span)
        scores = mt(queries_of(i), kbuf[here, :]) * scale
        length = lens[pl.ds(pl.multiple_of(i * GROUP, GROUP), GROUP), 0:1]
        length = jnp.concatenate([length] * heads, axis=0)
        begin = (iota(length.shape, 0) & (GROUP - 1)) * span
        end = begin + length.astype(jnp.int32)
        place = iota(scores.shape, 1)
        scores = jnp.where((place >= begin) & (place < end), scores, -1e30)
        top = jnp.max(scores, axis=1, keepdims=True)
        weights = jnp.exp(scores - top)
        o_s[i] = mm(weights.astype(BF16), vbuf[here, :])
        m_s[i] = jnp.broadcast_to(top, (GROUP * heads, HEAD))
        l_s[i] = jnp.broadcast_to(jnp.sum(weights, axis=1, keepdims=True), (GROUP * heads, HEAD))

    each(0, decodes // GROUP, cached)
    here_core = ((iota((slots, d.shape[0] * rank), 0) >> 1) & 1) == core

    def reduced(rows_in, c):
        part = pl.ds(c * width, width)
        own_part = mt(rows_in, d[:, :, part].reshape(-1, width))
        other_part = mt(rows_in, d_other[:, :, part].reshape(-1, width))
        return jnp.where(here_core, own_part, other_part)

    down_copy.wait_recv()
    both_up_copy.wait_recv()
    second_hop[0].all().wait_recv()
    got = mm(to_z, r2a[...].reshape(slots, -1)).astype(BF16)
    partial = reduced(got[:, 0:width], 0)
    code = got[:, width:].astype(F32)
    second_hop[1].all().wait_recv()
    partial = partial + reduced(r2b[...].reshape(slots, width), 1)
    lane_slot = (iota((slots, HEAD), 1) >> 6) + 1
    lane_slot = lane_slot.astype(F32)
    low_half = code == lane_slot
    high_half = code == lane_slot + 2.0
    mine = jnp.where(low_half, partial[:, 0:HEAD], 0.0) + jnp.where(
        high_half, partial[:, HEAD:], 0.0
    )
    ysend[...] = mine.astype(BF16)
    for k in far_first(tps):
        low_copy(k).start()
    for b in (0, 2, 1, 3):
        sum_copy(b).start()

    sign = jnp.where(iota((1, HEAD), 1) < HALF, -1.0, 1.0)

    def rotated(keys, cosine, sine):
        return keys * cosine + pltpu.roll(keys, HALF, 1) * (sine * sign)

    def finish(b):
        here = pl.ds(pl.multiple_of(b * rows, rows), rows)
        direct_copy(b).wait_recv()
        sum_copy(b).wait_recv()
        total = own[here, :] + rd[b].astype(F32) + rc[b].astype(F32)
        own[here, :] = total
        low_c, low_s = low_ref[0:PIECE, 0:HEAD], low_ref[0:PIECE, HEAD:]
        for i in range(rows // PIECE):
            if b == 0 and i == 0:
                continue
            a = b * (rows // PIECE) + i - 1
            ca, sa = base[a : a + 1, 0:HEAD], base[a : a + 1, HEAD:]
            piece = total[i * PIECE : (i + 1) * PIECE]
            keys = rotated(piece[:, 0:HEAD], ca * low_c - sa * low_s, sa * low_c + ca * low_s)
            stage[pl.ds(2 * i * PIECE, PIECE, stride=2), :] = keys
            stage[pl.ds(2 * i * PIECE + 1, PIECE, stride=2), :] = piece[:, HEAD:]
        skip = 2 * PIECE if b == 0 else 0
        begin = 2 * (b * rows - decodes) + skip
        begin = begin + 2 * decodes
        out[begin : begin + 2 * rows - skip, :] = stage[skip:, :].astype(BF16)

    for k in far_first(tps):
        low_copy(k).wait_recv()
    whole = mine
    for k in range(3):
        whole = whole + yrecv[k].astype(F32)
    wide = jnp.concatenate(
        [jnp.where(low_half, whole, 0.0), jnp.where(high_half, whole, 0.0)], axis=1
    )
    coarse = wide.astype(BF16)
    fine = (wide - coarse.astype(F32)).astype(BF16)
    both_parts = jnp.concatenate([coarse, fine], axis=0)
    own_delta = mm(both_parts, uall[...].reshape(-1, 2 * HEAD))
    other_delta = mm(both_parts, uall_other[...].reshape(-1, 2 * HEAD))
    delta = jnp.where(
        here_core[:, 0 : 2 * HEAD],
        own_delta[0:slots] + own_delta[slots:],
        other_delta[0:slots] + other_delta[slots:],
    )
    s3[...] = delta.astype(BF16).reshape(planes, 16, 2 * HEAD)
    back_hop[0].start()

    back_hop[0].all().wait_recv()
    s4[...] = mm(to_x, r3[...].reshape(slots, -1)).astype(BF16).reshape(s4.shape)
    back_hop[1].start()

    for b in (0, 2, 1, 3):
        finish(b)

    chosen = lens[:, 0:1] == iota((decodes, low_ref.shape[0]), 1).astype(F32)
    angles = lax.dot_general(
        jnp.where(chosen, 1.0, 0.0),
        low_ref[...],
        (((1,), (0,)), ((), ())),
        precision=lax.Precision.HIGHEST,
        preferred_element_type=F32,
    )
    back_hop[1].all().wait_recv()
    both = own[0:decodes, :] + mm(placing_back, r4[...].reshape(slots, -1))
    keys = rotated(both[:, 0:HEAD], angles[:, 0:HEAD], angles[:, HEAD:]).astype(BF16).astype(F32)
    values = both[:, HEAD:].astype(BF16).astype(F32)
    dec[pl.ds(0, decodes, stride=2), :] = keys
    dec[pl.ds(1, decodes, stride=2), :] = values
    out[0 : 2 * decodes, :] = dec[...].astype(BF16)
    for i in range(decodes // GROUP):
        key = jnp.concatenate([keys[i * GROUP : (i + 1) * GROUP]] * heads, axis=0)
        value = jnp.concatenate([values[i * GROUP : (i + 1) * GROUP]] * heads, axis=0)
        score = jnp.sum(queries_of(i).astype(F32) * key, axis=1, keepdims=True) * scale
        old = m_s[i]
        top = jnp.maximum(old, score)
        shrink = jnp.exp(old - top)
        share = jnp.exp(score - top)
        result = (o_s[i] * shrink + share * value) / (l_s[i] * shrink + share)
        for g in range(heads):
            begin = 2 * x.shape[0] + g * decodes + i * GROUP
            out[begin : begin + GROUP, :] = result[g * GROUP : (g + 1) * GROUP].astype(BF16)

    for hop in first_hop + second_hop + back_hop:
        hop.all().wait_send()
    down_copy.wait_send()
    both_up_copy.wait_send()
    for k in far_first(tps):
        up_copy(k).wait_send()
        low_copy(k).wait_send()

    def sent(b):
        relay_copy(b).wait_send()
        direct_copy(b).wait_send()
        sum_copy(b).wait_send()

    each(0, BLOCKS, sent)


def hand_over(held, dec_out, pre_out, att_out, sem):
    decodes = att_out.shape[0]
    middle = 2 * decodes + pre_out.shape[0]
    copies = [
        pltpu.make_async_copy(held.at[pl.ds(0, 2 * decodes)], dec_out, sem.at[0]),
        pltpu.make_async_copy(held.at[pl.ds(2 * decodes, pre_out.shape[0])], pre_out, sem.at[1]),
    ]
    for g in range(att_out.shape[1] // HEAD):
        source = held.at[pl.ds(middle + g * decodes, decodes)]
        target = att_out.at[:, pl.ds(g * HEAD, HEAD)]
        copies.append(pltpu.make_async_copy(source, target, sem.at[2 + g]))
    for c in copies:
        c.start()
    for c in copies:
        c.wait()


def shards(
    normed_input_rows,
    key_projection_weight,
    value_projection_weight,
    adapter_down_factors,
    adapter_up_factors,
    request_owner_replica,
    request_adapter_slot,
    prefill_adapter_slot,
    prefill_first_row,
    context_length,
    request_page_table,
    queries,
    rotated_cache_keys,
    paged_cache_values,
):
    total, width = normed_input_rows.shape
    decodes = request_adapter_slot.shape[0]
    adapters, _, rank = adapter_down_factors.shape
    pages, page, local = rotated_cache_keys.shape
    slots = 2 * lax.axis_size("rep")
    planes = lax.axis_size("rep") // PLANE
    tps = lax.axis_size("tp")
    rows = total // BLOCKS
    part = width // CHUNKS
    prefills = total - decodes
    groups = decodes // GROUP
    heads = queries.shape[1] // HEAD
    span = decodes * request_page_table.shape[1] * page
    vmem = pl.BlockSpec(memory_space=pltpu.VMEM)
    hbm = pl.BlockSpec(memory_space=pltpu.HBM)
    dma = pltpu.SemaphoreType.DMA

    def bf(*shape):
        return pltpu.VMEM(shape, BF16)

    def fl(*shape):
        return pltpu.VMEM(shape, F32)

    held = pl.pallas_call(
        kernel,
        out_shape=jax.ShapeDtypeStruct((2 * total + decodes * heads, HEAD), BF16),
        in_specs=[hbm] * 16,
        out_specs=vmem,
        scratch_shapes=[
            bf(2 * adapters * rank, HEAD),
            pltpu.VMEM((1, decodes), jnp.int32),
            pltpu.VMEM((1, decodes), jnp.int32),
            pltpu.SMEM((1,), jnp.int32),
            pltpu.SMEM((1,), jnp.int32),
            pltpu.VMEM((1, decodes), jnp.int32),
            pltpu.SMEM(request_page_table.shape[::-1], jnp.int32),
            fl(128, 2 * HEAD),
            fl(64, 2 * HEAD),
            bf(total, width),
            bf(tps, width, 2 * HEAD),
            bf(adapters, rank, width),
            bf(*queries.shape),
            bf(pages, page, local),
            bf(pages, page, local),
            bf(span, HEAD),
            bf(span, HEAD),
            bf(planes, 16, part + HEAD),
            bf(COLUMNS, 32, part),
            bf(planes, 16, part + HEAD),
            bf(COLUMNS, 32, part),
            bf(COLUMNS, 32, part + HEAD),
            bf(planes, 16, part),
            bf(COLUMNS, 32, part + HEAD),
            bf(planes, 16, part),
            bf(planes, 16, 2 * HEAD),
            bf(planes, 16, 2 * HEAD),
            bf(COLUMNS, 32, 2 * HEAD),
            bf(COLUMNS, 32, 2 * HEAD),
            bf(adapters, rank, 2 * HEAD),
            bf(adapters, rank, 2 * HEAD),
            bf(adapters, rank, width),
            bf(tps, rank, 2 * HEAD),
            bf(slots, HEAD),
            bf(tps - 1, slots, HEAD),
        ]
        + [bf(BLOCKS, rows, 2 * HEAD)] * 6
        + [
            bf(total, rank),
            fl(total, 2 * HEAD),
            fl(2 * rows, HEAD),
            fl(2 * decodes, HEAD),
            fl(16, 2 * HEAD),
            fl(decodes, HEAD),
            fl(groups, GROUP * heads, HEAD),
            fl(groups, GROUP * heads, HEAD),
            fl(groups, GROUP * heads, HEAD),
            dma((BLOCKS + 2 * 4 + 4 + 10,)),
            dma((8,)),
            dma((8,)),
            dma((tps,)),
            dma((tps,)),
            dma((3, BLOCKS)),
            dma((3, BLOCKS)),
            dma((tps,)),
            dma((tps,)),
        ],
        compiler_params=pltpu.CompilerParams(
            collective_id=0, has_side_effects=True, vmem_limit_bytes=LIMIT
        ),
    )(*(a if a.size == 1 else pltpu.with_memory_space_constraint(a, pltpu.HBM) for a in (
        normed_input_rows,
        key_projection_weight,
        value_projection_weight,
        jnp.swapaxes(adapter_down_factors, 1, 2),
        adapter_up_factors.reshape(-1, HEAD),
        request_owner_replica.reshape(1, -1),
        request_adapter_slot.reshape(1, -1),
        prefill_adapter_slot,
        prefill_first_row,
        context_length.reshape(1, -1),
        request_page_table.T,
        queries,
        rotated_cache_keys,
        paged_cache_values,
        jnp.asarray(trig(1, 128)),
        jnp.asarray(trig(PIECE, 64)),
        )))
    decode_kv, prefill_kv, attended = pl.pallas_call(
        hand_over,
        out_shape=(
            jax.ShapeDtypeStruct((2 * decodes, HEAD), BF16),
            jax.ShapeDtypeStruct((2 * prefills, HEAD), BF16),
            jax.ShapeDtypeStruct(queries.shape, BF16),
        ),
        in_specs=[vmem],
        out_specs=(hbm,) * 3,
        scratch_shapes=[dma((2 + heads,))],
        compiler_params=pltpu.CompilerParams(vmem_limit_bytes=LIMIT),
    )(held)
    return (
        decode_kv.reshape(decodes, 2, HEAD),
        prefill_kv.reshape(prefills, 2, HEAD),
        attended,
    )


def solution(mesh):
    in_specs = (
        P("rep", "tp"),
        P("tp", None),
        P("tp", None),
        P("rep", "tp", None),
        P("rep", None, None, "tp"),
        P("rep", None),
        P("rep"),
        P("rep"),
        P("rep"),
        P("rep"),
        P("rep", None),
        P("rep", "tp"),
        P("rep", None, "tp"),
        P("rep", None, "tp"),
    )
    out_specs = (P("rep", None, "tp"), P("rep", None, "tp"), P("rep", "tp"))
    return jax.shard_map(shards, mesh=mesh, in_specs=in_specs, out_specs=out_specs, check_vma=False)
```

```python
import jax
import jax.numpy as jnp
import numpy as np
from jax import lax
from jax.experimental import pallas as pl
from jax.experimental.pallas import tpu as pltpu
from jax.sharding import PartitionSpec as P

HEAD = 128
HALF = HEAD // 2
ROPE_BASE = 500000.0
CORES = 2
COLUMNS = 4
PLANE = CORES * COLUMNS
BLOCKS = 4
CHUNKS = 2
GROUP = 16
PIECE = 64
LIMIT = 40 * 1024 * 1024
MESH = pl.DeviceIdType.MESH
F32 = jnp.float32
BF16 = jnp.bfloat16


def mm(a, b):
    return lax.dot_general(a, b, (((1,), (0,)), ((), ())), preferred_element_type=F32)


def mt(a, b):
    return lax.dot_general(a, b, (((1,), (1,)), ((), ())), preferred_element_type=F32)


def iota(shape, axis):
    return lax.broadcasted_iota(jnp.int32, shape, axis)


def one_hot(condition):
    return jnp.where(condition, 1.0, 0.0).astype(BF16)


def trig(step, count):
    frequency = ROPE_BASE ** (-2.0 * np.arange(HALF) / HEAD)
    angles = step * np.arange(count)[:, None] * np.tile(frequency, 2)[None, :]
    return np.concatenate([np.cos(angles), np.sin(angles)], axis=1).astype(np.float32)


def kernel(
    x_hbm,
    wk_hbm,
    wv_hbm,
    d_hbm,
    up_hbm,
    owner_hbm,
    slot_hbm,
    pslot_hbm,
    pfirst_hbm,
    length_hbm,
    table_hbm,
    q_hbm,
    kpool_hbm,
    vpool_hbm,
    low_hbm,
    high_hbm,
    out,
    up_ref,
    owner_ref,
    slot_ref,
    pslot_ref,
    pfirst_ref,
    length_ref,
    table_ref,
    low_ref,
    high_ref,
    x,
    w,
    d,
    q,
    kpool,
    vpool,
    kbuf,
    vbuf,
    s1a,
    s1b,
    r1a,
    r1b,
    s2a,
    s2b,
    r2a,
    r2b,
    s3,
    r3,
    s4,
    r4,
    uall,
    uall_other,
    d_other,
    ug,
    ysend,
    yrecv,
    sr,
    sd,
    sc,
    rr,
    rd,
    rc,
    lrp,
    own,
    stage,
    dec,
    base,
    lens,
    m_s,
    l_s,
    o_s,
    load_sem,
    ex_s,
    ex_r,
    us,
    ur,
    ys,
    yr,
    ns,
    nr,
):
    t = lax.axis_index("tp")
    rep = lax.axis_index("rep")
    tps = lax.axis_size("tp")
    planes = lax.axis_size("rep") // PLANE
    z = lax.div(rep, PLANE)
    p = lax.rem(rep, PLANE)
    column_of = lax.div(p, CORES)
    core = lax.rem(p, CORES)
    rows = x.shape[0] // BLOCKS
    decodes = q.shape[0]
    slots = 2 * lax.axis_size("rep")
    width = x.shape[1] // CHUNKS
    s1 = (s1a, s1b)

    barrier = pltpu.get_barrier_semaphore()

    def at(rep_to, tp_to):
        return dict(device_id=(rep_to, tp_to), device_id_type=MESH)

    def z_of(dd):
        return lax.rem(z + dd, planes)

    def x_of(dd):
        return lax.rem(column_of + dd, COLUMNS)

    def at_x(to):
        return at(z * PLANE + to * CORES + core, t)

    def at_other_core():
        return at(z * PLANE + column_of * CORES + 1 - core, t)

    def t_of(dd):
        return lax.rem(t + dd, tps)

    def each(low, high, body):
        lax.fori_loop(low, high, lambda i, c: (body(i), c)[1], 0)

    def far_first(count):
        return sorted(range(1, count), key=lambda k: -min(k, count - k))

    def load(source, target, k):
        return pltpu.make_async_copy(source, target, load_sem.at[k])

    def x_load(b):
        part = pl.ds(b * rows, rows)
        return load(x_hbm.at[part], x.at[part], b)

    def w_load(j):
        columns = pl.ds(pl.multiple_of(t_of(j) * HEAD, HEAD), HEAD)
        return (
            load(wk_hbm.at[:, columns], w.at[j, :, pl.ds(0, HEAD)], BLOCKS + 2 * j),
            load(wv_hbm.at[:, columns], w.at[j, :, pl.ds(HEAD, HEAD)], BLOCKS + 2 * j + 1),
        )

    k0 = BLOCKS + 2 * 4
    q_load = load(q_hbm, q, k0)
    d_load = load(d_hbm, d, k0 + 1)
    kpool_load = load(kpool_hbm, kpool, k0 + 2)
    vpool_load = load(vpool_hbm, vpool, k0 + 3)
    small = [
        load(source, target, k0 + 4 + i)
        for i, (source, target) in enumerate(
            (
                (owner_hbm, owner_ref),
                (slot_hbm, slot_ref),
                (length_hbm, length_ref),
                (pslot_hbm, pslot_ref),
                (up_hbm, up_ref),
                (pfirst_hbm, pfirst_ref),
                (low_hbm, low_ref),
                (high_hbm, high_ref),
                (table_hbm, table_ref),
            )
        )
    ]
    head_load = load(x_hbm.at[pl.ds(0, decodes)], x.at[pl.ds(0, decodes)], k0 + 4 + len(small))
    small[0].start()
    head_load.start()
    for c in small[1:3]:
        c.start()
    for k in far_first(planes):
        pl.semaphore_signal(barrier, inc=1, **at(z_of(k) * PLANE + p, t))
    for k in far_first(COLUMNS):
        pl.semaphore_signal(barrier, inc=1, **at_x(x_of(k)))
    pl.semaphore_signal(barrier, inc=1, **at_other_core())
    for k in far_first(tps):
        pl.semaphore_signal(barrier, inc=1, **at(rep, t_of(k)))
    for c in small[3:]:
        c.start()
    rest = pl.ds(decodes, rows - decodes)
    load(x_hbm.at[rest], x.at[rest], 0).start()
    d_load.start()
    for c in w_load(2):
        c.start()
    for b in (1, 2, 3):
        x_load(b).start()
    for j in (3, 1, 0):
        for c in w_load(j):
            c.start()
    for c in (q_load, kpool_load, vpool_load):
        c.start()

    for c in small[:3]:
        c.wait()

    eye = iota((decodes, decodes), 0) == iota((decodes, decodes), 1)

    def column(row):
        return jnp.sum(jnp.where(eye, jnp.broadcast_to(row, eye.shape), 0.0), axis=1, keepdims=True)

    owner_row = owner_ref[...].astype(F32)
    owner_col = column(owner_row)
    same = owner_col == owner_row
    before_col = iota(eye.shape, 1) < iota(eye.shape, 0)
    before_row = iota(eye.shape, 0) < iota(eye.shape, 1)
    rank_col = jnp.sum(jnp.where(same & before_col, 1.0, 0.0), axis=1, keepdims=True)
    rank_row = jnp.sum(jnp.where(same & before_row, 1.0, 0.0), axis=0, keepdims=True)

    def x_first(owner, turn):
        owner = owner.astype(jnp.int32)
        place = ((owner >> 1) & 3) * 32 + (owner >> 3) * 4 + (owner & 1) * 2
        return place + turn.astype(jnp.int32)

    slot_of = iota((slots, decodes), 0)
    placing = (
        one_hot((2.0 * owner_row + rank_row).astype(jnp.int32) == slot_of),
        one_hot(x_first(owner_row, rank_row) == slot_of),
    )
    placing_back = one_hot(x_first(owner_col, rank_col) == iota((decodes, slots), 1))
    codes = jnp.broadcast_to(column(slot_ref[...].astype(F32)) + 1.0, (decodes, HEAD)).astype(BF16)

    head_load.wait()
    for c in range(CHUNKS):
        placed = mm(placing[c], x[0:decodes, c * width : (c + 1) * width]).astype(BF16)
        s1[c][:, :, 0:width] = placed.reshape(s1[c].shape[:2] + (width,))
    s1a[:, :, width : width + HEAD] = mm(placing[0], codes).astype(BF16).reshape(planes, 16, HEAD)

    def copy(source, target, send, recv, where):
        return pltpu.make_async_remote_copy(source, target, send, recv, **where)

    class Exchange:
        def __init__(self, sent, got, me, of, place, k):
            self.sent, self.got, self.me, self.of, self.place = sent, got, me, of, place
            self.send, self.recv, self.count = ex_s.at[k], ex_r.at[k], sent.shape[0]

        def start(self):
            for k in far_first(self.count):
                to = self.of(k)
                copy(self.sent.at[to], self.got.at[self.me], self.send, self.recv, self.place(to)).start()
            self.got[self.me] = self.sent[self.me]

        def all(self):
            most = pl.ds(0, self.count - 1)
            return copy(self.sent.at[most], self.got.at[most], self.send, self.recv, self.place(self.of(1)))

    def over_z(sent, got, k):
        return Exchange(sent, got, z, z_of, lambda to: at(to * PLANE + p, t), k)

    def over_x(sent, got, k):
        return Exchange(sent, got, column_of, x_of, at_x, k)

    first_hop = (over_z(s1a, r1a, 0), over_x(s1b, r1b, 1))
    second_hop = (over_x(s2a, r2a, 2), over_z(s2b, r2b, 3))
    back_hop = (over_z(s3, r3, 4), over_x(s4, r4, 5))

    down_copy = copy(d_hbm, d_other, ex_s.at[6], ex_r.at[6], at_other_core())
    both_up_copy = copy(uall, uall_other, ex_s.at[7], ex_r.at[7], at_other_core())

    def up_copy(k):
        return pltpu.make_async_remote_copy(
            ug.at[t], ug.at[t], us.at[k], ur.at[k], **at(rep, t_of(k))
        )

    def low_copy(k):
        return pltpu.make_async_remote_copy(
            ysend, yrecv.at[k - 1], ns.at[k], nr.at[k], **at(rep, t_of(k))
        )

    def ahead(b):
        return 1 + 2 * lax.div(b, 2)

    def back(b):
        return 3 - 2 * lax.div(b, 2)

    def relay_copy(b):
        return pltpu.make_async_remote_copy(
            sr.at[b], rr.at[b], ys.at[0, b], yr.at[0, b], **at(rep, t_of(ahead(b)))
        )

    def direct_copy(b):
        return pltpu.make_async_remote_copy(
            sd.at[b], rd.at[b], ys.at[1, b], yr.at[1, b], **at(rep, t_of(back(b)))
        )

    def sum_copy(b):
        return pltpu.make_async_remote_copy(
            sc.at[b], rc.at[b], ys.at[2, b], yr.at[2, b], **at(rep, t_of(ahead(b)))
        )

    pl.semaphore_wait(barrier, planes - 1 + COLUMNS - 1 + 1 + tps - 1)
    first_hop[0].start()
    first_hop[1].start()

    for c in small[3:5]:
        c.wait()
    pairs = up_ref[...]
    count = pairs.shape[0] // 2
    pick = iota((count, 2 * count), 1) - 2 * iota((count, 2 * count), 0)
    rank = uall.shape[1]
    uall[:, :, 0:HEAD] = mm(one_hot(pick == 0), pairs).astype(BF16).reshape(-1, rank, HEAD)
    uall[:, :, HEAD:] = mm(one_hot(pick == 1), pairs).astype(BF16).reshape(-1, rank, HEAD)
    selected = pslot_ref[0]
    ug[t] = uall[selected]
    for k in far_first(tps):
        up_copy(k).start()
    both_up_copy.start()
    down_copy.start()

    lens[...] = jnp.broadcast_to(column(length_ref[...].astype(F32)), (decodes, HEAD))

    for c in small[5:8]:
        c.wait()
    first = pfirst_ref[0]
    high = high_ref[pl.ds(lax.div(first, PIECE), 1), :]
    low = low_ref[pl.ds(lax.rem(first, PIECE), 1), :]

    def turn(a, b):
        ca, sa, cb, sb = a[:, 0:HEAD], a[:, HEAD:], b[:, 0:HEAD], b[:, HEAD:]
        return ca * cb - sa * sb, sa * cb + ca * sb

    c0, s0 = turn(high, low)
    steps = high_ref[0:16, :]
    cb, sb = steps[:, 0:HEAD], steps[:, HEAD:]
    base[:, 0:HEAD] = c0 * cb - s0 * sb
    base[:, HEAD:] = s0 * cb + c0 * sb

    out_at = iota((slots, slots), 0)
    in_at = iota((slots, slots), 1)
    to_x = one_hot(in_at == ((out_at >> 2) & 7) * 16 + (out_at >> 5) * 4 + (out_at & 3))
    to_z = one_hot(in_at == ((out_at >> 2) & 3) * 32 + (out_at >> 4) * 4 + (out_at & 3))

    d_load.wait()
    for c in w_load(2):
        c.wait()

    def part_of(b, j):
        here = pl.ds(pl.multiple_of(b * rows, rows), rows)
        return mm(x[here, :], w[j]) + mm(lrp[here, :], ug[t_of(j)])

    def relay_step(b):
        here = pl.ds(pl.multiple_of(b * rows, rows), rows)

        @pl.when(b == 0)
        def _():
            load(x_hbm.at[rest], x.at[rest], 0).wait()

        @pl.when(b > 0)
        def _():
            x_load(b).wait()

        low_rank = mt(x[here, :], d[selected])
        row = iota(low_rank.shape, 0) + b * rows
        lrp[here, :] = jnp.where(row >= decodes, low_rank, 0.0).astype(BF16)
        own[here, :] = mm(x[here, :], w[2])

    def relay_sum(b):
        here = pl.ds(pl.multiple_of(b * rows, rows), rows)
        sr[b] = (own[here, :] + mm(lrp[here, :], ug[t_of(2)])).astype(BF16)

    def direct_step(b):
        sd[b] = part_of(b, back(b)).astype(BF16)

    def sum_step(b):
        part = part_of(b, ahead(b))
        relay_copy(b).wait_recv()
        sc[b] = (part + rr[b].astype(F32)).astype(BF16)

    def own_step(b):
        own[pl.ds(pl.multiple_of(b * rows, rows), rows), :] = part_of(b, 0)

    def order(i):
        return lax.div(i, 2) + 2 * lax.rem(i, 2)

    each(0, BLOCKS, lambda i: relay_step(order(i)))
    for k in far_first(tps):
        up_copy(k).wait_recv()
    each(0, 2, lambda i: relay_sum(order(i)))
    for b in (0, 2):
        relay_copy(b).start()
    each(2, BLOCKS, lambda i: relay_sum(order(i)))
    for j in (3, 1):
        for c in w_load(j):
            c.wait()
    each(0, 2, lambda i: direct_step(order(i)))

    def forward(c):
        first_hop[c].all().wait_recv()
        moved = mm((to_x, to_z)[c], first_hop[c].got[...].reshape(slots, -1)).astype(BF16)
        second_hop[c].sent[...] = moved.reshape(second_hop[c].sent.shape)
        second_hop[c].start()

    forward(1)
    for b in (1, 3):
        relay_copy(b).start()
    each(2, BLOCKS, lambda i: direct_step(order(i)))
    for c in w_load(0):
        c.wait()
    each(0, BLOCKS, own_step)
    each(0, 2, lambda i: sum_step(order(i)))
    forward(0)
    for b in (0, 2, 1, 3):
        direct_copy(b).start()
    each(2, BLOCKS, lambda i: sum_step(order(i)))

    for c in (q_load, kpool_load, vpool_load, small[8]):
        c.wait()
    maxp, page = table_ref.shape[0], kpool.shape[1]
    span = maxp * page

    def gather(i):
        for j in range(maxp):
            number = table_ref[j, i]
            here = pl.ds(pl.multiple_of((i * maxp + j) * page, page), page)
            kbuf[here, :] = kpool[number]
            vbuf[here, :] = vpool[number]

    each(0, decodes, gather)
    heads = q.shape[1] // HEAD
    scale = HEAD**-0.5

    def queries_of(i):
        here = pl.ds(pl.multiple_of(i * GROUP, GROUP), GROUP)
        return jnp.concatenate(
            [q[here, g * HEAD : (g + 1) * HEAD] for g in range(heads)], axis=0
        )

    def cached(i):
        here = pl.ds(pl.multiple_of(i * GROUP * span, GROUP * span), GROUP * span)
        scores = mt(queries_of(i), kbuf[here, :]) * scale
        length = lens[pl.ds(pl.multiple_of(i * GROUP, GROUP), GROUP), 0:1]
        length = jnp.concatenate([length] * heads, axis=0)
        begin = (iota(length.shape, 0) & (GROUP - 1)) * span
        end = begin + length.astype(jnp.int32)
        place = iota(scores.shape, 1)
        scores = jnp.where((place >= begin) & (place < end), scores, -1e30)
        top = jnp.max(scores, axis=1, keepdims=True)
        weights = jnp.exp(scores - top)
        o_s[i] = mm(weights.astype(BF16), vbuf[here, :])
        m_s[i] = jnp.broadcast_to(top, (GROUP * heads, HEAD))
        l_s[i] = jnp.broadcast_to(jnp.sum(weights, axis=1, keepdims=True), (GROUP * heads, HEAD))

    each(0, decodes // GROUP, cached)
    here_core = ((iota((slots, d.shape[0] * rank), 0) >> 1) & 1) == core

    def reduced(rows_in, c):
        part = pl.ds(c * width, width)
        own_part = mt(rows_in, d[:, :, part].reshape(-1, width))
        other_part = mt(rows_in, d_other[:, :, part].reshape(-1, width))
        return jnp.where(here_core, own_part, other_part)

    down_copy.wait_recv()
    both_up_copy.wait_recv()
    second_hop[0].all().wait_recv()
    got = mm(to_z, r2a[...].reshape(slots, -1)).astype(BF16)
    partial = reduced(got[:, 0:width], 0)
    code = got[:, width:].astype(F32)
    second_hop[1].all().wait_recv()
    partial = partial + reduced(r2b[...].reshape(slots, width), 1)
    lane_slot = (iota((slots, HEAD), 1) >> 6) + 1
    lane_slot = lane_slot.astype(F32)
    low_half = code == lane_slot
    high_half = code == lane_slot + 2.0
    mine = jnp.where(low_half, partial[:, 0:HEAD], 0.0) + jnp.where(
        high_half, partial[:, HEAD:], 0.0
    )
    ysend[...] = mine.astype(BF16)
    for k in far_first(tps):
        low_copy(k).start()
    for b in (0, 2, 1, 3):
        sum_copy(b).start()

    sign = jnp.where(iota((1, HEAD), 1) < HALF, -1.0, 1.0)

    def rotated(keys, cosine, sine):
        return keys * cosine + pltpu.roll(keys, HALF, 1) * (sine * sign)

    def finish(b):
        here = pl.ds(pl.multiple_of(b * rows, rows), rows)
        direct_copy(b).wait_recv()
        sum_copy(b).wait_recv()
        total = own[here, :] + rd[b].astype(F32) + rc[b].astype(F32)
        own[here, :] = total
        low_c, low_s = low_ref[0:PIECE, 0:HEAD], low_ref[0:PIECE, HEAD:]
        for i in range(rows // PIECE):
            if b == 0 and i == 0:
                continue
            a = b * (rows // PIECE) + i - 1
            ca, sa = base[a : a + 1, 0:HEAD], base[a : a + 1, HEAD:]
            piece = total[i * PIECE : (i + 1) * PIECE]
            keys = rotated(piece[:, 0:HEAD], ca * low_c - sa * low_s, sa * low_c + ca * low_s)
            stage[pl.ds(2 * i * PIECE, PIECE, stride=2), :] = keys
            stage[pl.ds(2 * i * PIECE + 1, PIECE, stride=2), :] = piece[:, HEAD:]
        skip = 2 * PIECE if b == 0 else 0
        begin = 2 * (b * rows - decodes) + skip
        begin = begin + 2 * decodes
        out[begin : begin + 2 * rows - skip, :] = stage[skip:, :].astype(BF16)

    for k in far_first(tps):
        low_copy(k).wait_recv()
    whole = mine
    for k in range(3):
        whole = whole + yrecv[k].astype(F32)
    wide = jnp.concatenate(
        [jnp.where(low_half, whole, 0.0), jnp.where(high_half, whole, 0.0)], axis=1
    )
    coarse = wide.astype(BF16)
    fine = (wide - coarse.astype(F32)).astype(BF16)
    both_parts = jnp.concatenate([coarse, fine], axis=0)
    own_delta = mm(both_parts, uall[...].reshape(-1, 2 * HEAD))
    other_delta = mm(both_parts, uall_other[...].reshape(-1, 2 * HEAD))
    delta = jnp.where(
        here_core[:, 0 : 2 * HEAD],
        own_delta[0:slots] + own_delta[slots:],
        other_delta[0:slots] + other_delta[slots:],
    )
    s3[...] = delta.astype(BF16).reshape(planes, 16, 2 * HEAD)
    back_hop[0].start()

    back_hop[0].all().wait_recv()
    s4[...] = mm(to_x, r3[...].reshape(slots, -1)).astype(BF16).reshape(s4.shape)
    back_hop[1].start()

    for b in (0, 2, 1, 3):
        finish(b)

    chosen = lens[:, 0:1] == iota((decodes, low_ref.shape[0]), 1).astype(F32)
    angles = lax.dot_general(
        jnp.where(chosen, 1.0, 0.0),
        low_ref[...],
        (((1,), (0,)), ((), ())),
        precision=lax.Precision.HIGHEST,
        preferred_element_type=F32,
    )
    for hop in first_hop + second_hop + back_hop[0:1]:
        hop.all().wait_send()
    down_copy.wait_send()
    both_up_copy.wait_send()
    for k in far_first(tps):
        up_copy(k).wait_send()
        low_copy(k).wait_send()

    def sent(b):
        relay_copy(b).wait_send()
        direct_copy(b).wait_send()
        sum_copy(b).wait_send()

    each(0, BLOCKS, sent)

    back_hop[1].all().wait_recv()
    both = own[0:decodes, :] + mm(placing_back, r4[...].reshape(slots, -1))
    keys = rotated(both[:, 0:HEAD], angles[:, 0:HEAD], angles[:, HEAD:]).astype(BF16).astype(F32)
    values = both[:, HEAD:].astype(BF16).astype(F32)
    dec[pl.ds(0, decodes, stride=2), :] = keys
    dec[pl.ds(1, decodes, stride=2), :] = values
    out[0 : 2 * decodes, :] = dec[...].astype(BF16)
    for i in range(decodes // GROUP):
        key = jnp.concatenate([keys[i * GROUP : (i + 1) * GROUP]] * heads, axis=0)
        value = jnp.concatenate([values[i * GROUP : (i + 1) * GROUP]] * heads, axis=0)
        score = jnp.sum(queries_of(i).astype(F32) * key, axis=1, keepdims=True) * scale
        old = m_s[i]
        top = jnp.maximum(old, score)
        shrink = jnp.exp(old - top)
        share = jnp.exp(score - top)
        result = (o_s[i] * shrink + share * value) / (l_s[i] * shrink + share)
        for g in range(heads):
            begin = 2 * x.shape[0] + g * decodes + i * GROUP
            out[begin : begin + GROUP, :] = result[g * GROUP : (g + 1) * GROUP].astype(BF16)
    back_hop[1].all().wait_send()


def hand_over(held, dec_out, pre_out, att_out, sem):
    decodes = att_out.shape[0]
    middle = 2 * decodes + pre_out.shape[0]
    copies = [
        pltpu.make_async_copy(held.at[pl.ds(0, 2 * decodes)], dec_out, sem.at[0]),
        pltpu.make_async_copy(held.at[pl.ds(2 * decodes, pre_out.shape[0])], pre_out, sem.at[1]),
    ]
    for g in range(att_out.shape[1] // HEAD):
        source = held.at[pl.ds(middle + g * decodes, decodes)]
        target = att_out.at[:, pl.ds(g * HEAD, HEAD)]
        copies.append(pltpu.make_async_copy(source, target, sem.at[2 + g]))
    for c in copies:
        c.start()
    for c in copies:
        c.wait()


def shards(
    normed_input_rows,
    key_projection_weight,
    value_projection_weight,
    adapter_down_factors,
    adapter_up_factors,
    request_owner_replica,
    request_adapter_slot,
    prefill_adapter_slot,
    prefill_first_row,
    context_length,
    request_page_table,
    queries,
    rotated_cache_keys,
    paged_cache_values,
):
    total, width = normed_input_rows.shape
    decodes = request_adapter_slot.shape[0]
    adapters, _, rank = adapter_down_factors.shape
    pages, page, local = rotated_cache_keys.shape
    slots = 2 * lax.axis_size("rep")
    planes = lax.axis_size("rep") // PLANE
    tps = lax.axis_size("tp")
    rows = total // BLOCKS
    part = width // CHUNKS
    prefills = total - decodes
    groups = decodes // GROUP
    heads = queries.shape[1] // HEAD
    span = decodes * request_page_table.shape[1] * page
    vmem = pl.BlockSpec(memory_space=pltpu.VMEM)
    hbm = pl.BlockSpec(memory_space=pltpu.HBM)
    dma = pltpu.SemaphoreType.DMA

    def bf(*shape):
        return pltpu.VMEM(shape, BF16)

    def fl(*shape):
        return pltpu.VMEM(shape, F32)

    held = pl.pallas_call(
        kernel,
        out_shape=jax.ShapeDtypeStruct((2 * total + decodes * heads, HEAD), BF16),
        in_specs=[hbm] * 16,
        out_specs=vmem,
        scratch_shapes=[
            bf(2 * adapters * rank, HEAD),
            pltpu.VMEM((1, decodes), jnp.int32),
            pltpu.VMEM((1, decodes), jnp.int32),
            pltpu.SMEM((1,), jnp.int32),
            pltpu.SMEM((1,), jnp.int32),
            pltpu.VMEM((1, decodes), jnp.int32),
            pltpu.SMEM(request_page_table.shape[::-1], jnp.int32),
            fl(128, 2 * HEAD),
            fl(64, 2 * HEAD),
            bf(total, width),
            bf(tps, width, 2 * HEAD),
            bf(adapters, rank, width),
            bf(*queries.shape),
            bf(pages, page, local),
            bf(pages, page, local),
            bf(span, HEAD),
            bf(span, HEAD),
            bf(planes, 16, part + HEAD),
            bf(COLUMNS, 32, part),
            bf(planes, 16, part + HEAD),
            bf(COLUMNS, 32, part),
            bf(COLUMNS, 32, part + HEAD),
            bf(planes, 16, part),
            bf(COLUMNS, 32, part + HEAD),
            bf(planes, 16, part),
            bf(planes, 16, 2 * HEAD),
            bf(planes, 16, 2 * HEAD),
            bf(COLUMNS, 32, 2 * HEAD),
            bf(COLUMNS, 32, 2 * HEAD),
            bf(adapters, rank, 2 * HEAD),
            bf(adapters, rank, 2 * HEAD),
            bf(adapters, rank, width),
            bf(tps, rank, 2 * HEAD),
            bf(slots, HEAD),
            bf(tps - 1, slots, HEAD),
        ]
        + [bf(BLOCKS, rows, 2 * HEAD)] * 6
        + [
            bf(total, rank),
            fl(total, 2 * HEAD),
            fl(2 * rows, HEAD),
            fl(2 * decodes, HEAD),
            fl(16, 2 * HEAD),
            fl(decodes, HEAD),
            fl(groups, GROUP * heads, HEAD),
            fl(groups, GROUP * heads, HEAD),
            fl(groups, GROUP * heads, HEAD),
            dma((BLOCKS + 2 * 4 + 4 + 10,)),
            dma((8,)),
            dma((8,)),
            dma((tps,)),
            dma((tps,)),
            dma((3, BLOCKS)),
            dma((3, BLOCKS)),
            dma((tps,)),
            dma((tps,)),
        ],
        compiler_params=pltpu.CompilerParams(
            collective_id=0, has_side_effects=True, vmem_limit_bytes=LIMIT
        ),
    )(*(a if a.size == 1 else pltpu.with_memory_space_constraint(a, pltpu.HBM) for a in (
        normed_input_rows,
        key_projection_weight,
        value_projection_weight,
        jnp.swapaxes(adapter_down_factors, 1, 2),
        adapter_up_factors.reshape(-1, HEAD),
        request_owner_replica.reshape(1, -1),
        request_adapter_slot.reshape(1, -1),
        prefill_adapter_slot,
        prefill_first_row,
        context_length.reshape(1, -1),
        request_page_table.T,
        queries,
        rotated_cache_keys,
        paged_cache_values,
        jnp.asarray(trig(1, 128)),
        jnp.asarray(trig(PIECE, 64)),
        )))
    decode_kv, prefill_kv, attended = pl.pallas_call(
        hand_over,
        out_shape=(
            jax.ShapeDtypeStruct((2 * decodes, HEAD), BF16),
            jax.ShapeDtypeStruct((2 * prefills, HEAD), BF16),
            jax.ShapeDtypeStruct(queries.shape, BF16),
        ),
        in_specs=[vmem],
        out_specs=(hbm,) * 3,
        scratch_shapes=[dma((2 + heads,))],
        compiler_params=pltpu.CompilerParams(vmem_limit_bytes=LIMIT),
    )(held)
    return (
        decode_kv.reshape(decodes, 2, HEAD),
        prefill_kv.reshape(prefills, 2, HEAD),
        attended,
    )


def solution(mesh):
    in_specs = (
        P("rep", "tp"),
        P("tp", None),
        P("tp", None),
        P("rep", "tp", None),
        P("rep", None, None, "tp"),
        P("rep", None),
        P("rep"),
        P("rep"),
        P("rep"),
        P("rep"),
        P("rep", None),
        P("rep", "tp"),
        P("rep", None, "tp"),
        P("rep", None, "tp"),
    )
    out_specs = (P("rep", None, "tp"), P("rep", None, "tp"), P("rep", "tp"))
    return jax.shard_map(shards, mesh=mesh, in_specs=in_specs, out_specs=out_specs, check_vma=False)
```
